256 devices in a mesh: lat: 8 (over x_hi, y), lon: 32 (over x_lo, z, core).
Axes of the slice: x: 4 (x_hi: 2, x_lo: 2; x = x_hi * 2 + x_lo), y: 4, z: 8, core: 2. Of those that a mesh axis runs over, the one named last changes fastest.
Arguments:
- features: bfloat16 [8, 64, 128, 384], P('lat', 'lon'), may hold values from -6 to 6
- w_query: bfloat16 [384, 384], replicated, may hold values from -0.3125 to 0.3125
- w_key: bfloat16 [384, 384], replicated, may hold values from -0.3125 to 0.3125
- w_value: bfloat16 [384, 384], replicated, may hold values from -0.3125 to 0.3125
- w_out: bfloat16 [384, 384], replicated, may hold values from -0.3125 to 0.3125
- key_bias: bfloat16 [8, 64, 8, 128], P('lat', 'lon'), may hold values from -4 to 320
- neighbours: int32 [8, 64, 4], P('lat', 'lon'), may hold values from 0 to 511, as said below
- key_counts: int32 [8, 64, 4], P('lat', 'lon'), may hold values from 16 to 128, as said below
- grad_out: bfloat16 [8, 64, 128, 384], P('lat', 'lon'), may hold values from -6 to 6
Outputs:
- grad_features: bfloat16 [8, 64, 128, 384], P('lat', 'lon')
- grad_bias: float32 [8, 64, 8, 128], P('lat', 'lon')
- grad_wq: float32 [384, 384], replicated
- grad_wk: float32 [384, 384], replicated
- grad_wv: float32 [384, 384], replicated
- grad_wo: float32 [384, 384], replicated
The draws below stay inside these ranges and needn't reach their ends.
Inputs may be any that keep to these rules, and one draw needn't show every extreme that they name: `neighbours`: entry 0 of each query block names that block itself; every entry names a block whose row differs by at most 1 (kept in range at the first and last rows) and whose column differs by at most 1 modulo 64; a block may be named more than once. `key_counts`: entry 0 is 128.
All inputs are finite; a program needn't handle non-finite values.
Results may differ from the reference program's by a relative error of at most 0.012.
Values may be sent and summed in bfloat16 or wider, within the bound.
A program may use at most 64 MiB of HBM per device.

```python
import jax
import jax.numpy as jnp
from jax import lax

HEADS = 8
CH = 384
BS = 128
KB = 4
GLA = 8
GLO = 64


def draw_neighbours(key, part):
    key = jax.random.fold_in(key, 11)
    lat_key, lon_key = jax.random.split(key)
    shape = (GLA, GLO, KB)
    step_lat = jax.random.randint(lat_key, shape, -1, 2)
    step_lon = jax.random.randint(lon_key, shape, -1, 2)
    entry = jnp.arange(KB, dtype=jnp.int32)[None, None, :]
    step_lat = jnp.where(entry == 0, 0, step_lat)
    step_lon = jnp.where(entry == 0, 0, step_lon)
    rows = jnp.arange(GLA, dtype=jnp.int32)[:, None, None]
    columns = jnp.arange(GLO, dtype=jnp.int32)[None, :, None]
    target_rows = jnp.clip(rows + step_lat, 0, GLA - 1)
    target_columns = (columns + step_lon) % GLO
    return (target_rows * GLO + target_columns).astype(jnp.int32)


def draw_key_counts(key, part):
    key = jax.random.fold_in(key, 17)
    counts = jax.random.randint(key, (GLA, GLO, KB), BS // 8, BS + 1)
    entry = jnp.arange(KB, dtype=jnp.int32)[None, None, :]
    return jnp.where(entry == 0, BS, counts).astype(jnp.int32)


def draw_key_bias(key, part):
    key = jax.random.fold_in(key, 29)
    shape = (GLA, GLO, HEADS, BS)
    result = jnp.clip(jax.random.normal(key, shape, jnp.float32), -4.0, 4.0)
    return result.astype(jnp.bfloat16)


def block_levels(stream_key, dims, cuts, least, largest):
    loudness = 1.0
    for dim, shards_of in cuts:
        heights = jax.random.uniform(jax.random.fold_in(jax.random.fold_in(stream_key, 6), dim), (shards_of,), jnp.float32, least / len(cuts), largest / len(cuts))
        loudness = loudness * jnp.repeat(jnp.exp(heights), dims[dim] // shards_of).reshape((-1,) + (1,) * (len(dims) - 1 - dim))
    return loudness


def noise(key, dims, spread, most, cuts=(), kind=jnp.bfloat16):
    values = spread * jax.random.normal(key, dims, jnp.float32)
    if cuts:
        values = values * block_levels(key, dims, cuts, -0.22, 0.18)
    return jnp.clip(values, -most, most).astype(kind)


def setup_inputs(seed: int = 0) -> dict:
    seeds = jax.random.split(jax.random.key(seed), 10)
    features = noise(seeds[0], (GLA, GLO, BS, CH), 1.0, 6.0, ((0, 8), (1, 32)))
    w_query = noise(seeds[1], (CH, CH), CH ** -0.5, 0.3125)
    w_key = noise(seeds[2], (CH, CH), CH ** -0.5, 0.3125)
    w_value = noise(seeds[3], (CH, CH), CH ** -0.5, 0.3125)
    w_out = noise(seeds[4], (CH, CH), CH ** -0.5, 0.3125)
    key_bias = draw_key_bias(jax.random.fold_in(seeds[9], 71), 0)
    neighbours = draw_neighbours(jax.random.fold_in(seeds[9], 71), 0)
    key_counts = draw_key_counts(jax.random.fold_in(seeds[9], 71), 0)
    grad_out = noise(seeds[8], (GLA, GLO, BS, CH), 1.0, 6.0, ((0, 8), (1, 32)))
    return dict(features=features, w_query=w_query, w_key=w_key, w_value=w_value, w_out=w_out, key_bias=key_bias, neighbours=neighbours, key_counts=key_counts, grad_out=grad_out)


def attend_blocks(query_blocks, key_blocks, value_blocks, bias_blocks, counts, grad_blocks):
    groups = query_blocks.shape[0]
    slots = query_blocks.shape[1]
    chans = query_blocks.shape[2]
    entries = key_blocks.shape[1]
    width = chans // HEADS
    scale = float(width) ** -0.5
    head_query = query_blocks.astype(jnp.float32).reshape(groups, slots, HEADS, width)
    head_key = key_blocks.astype(jnp.float32).reshape(groups, entries * slots, HEADS, width)
    head_value = value_blocks.astype(jnp.float32).reshape(groups, entries * slots, HEADS, width)
    bias_rows = bias_blocks.astype(jnp.float32).transpose(0, 2, 1, 3).reshape(groups, HEADS, entries * slots)
    valid = (jnp.arange(slots, dtype=jnp.int32)[None, None, :] < counts[:, :, None]).reshape(groups, entries * slots)
    scores = jnp.einsum('gihd,gkhd->ghik', head_query, head_key) * scale + bias_rows[:, :, None, :]
    scores = jnp.where(valid[:, None, None, :], scores, -jnp.inf)
    probs = jax.nn.softmax(scores, axis=-1)
    probs_low = lax.optimization_barrier(probs.astype(jnp.bfloat16)).astype(jnp.float32)
    attended = jnp.einsum('ghik,gkhd->gihd', probs_low, head_value).astype(jnp.bfloat16).reshape(groups, slots, chans)
    head_grad = grad_blocks.astype(jnp.float32).reshape(groups, slots, HEADS, width)
    grad_probs = jnp.einsum('gihd,gkhd->ghik', head_grad, head_value)
    centre = jnp.sum(probs * grad_probs, axis=-1, keepdims=True)
    grad_scores = probs * (grad_probs - centre)
    scores_low = lax.optimization_barrier(grad_scores.astype(jnp.bfloat16)).astype(jnp.float32)
    grad_query = (jnp.einsum('ghik,gkhd->gihd', scores_low, head_key) * scale).reshape(groups, slots, chans)
    grad_key = (jnp.einsum('ghik,gihd->gkhd', scores_low, head_query) * scale).reshape(groups * entries, slots, chans)
    grad_value = jnp.einsum('ghik,gihd->gkhd', probs_low, head_grad).reshape(groups * entries, slots, chans)
    grad_bias = jnp.sum(grad_scores, axis=2).reshape(groups, HEADS, entries, slots).transpose(0, 2, 1, 3)
    grad_bias = grad_bias.reshape(groups * entries, HEADS, slots)
    return attended, grad_query, grad_key, grad_value, grad_bias


def reference(features, w_query, w_key, w_value, w_out, key_bias, neighbours, key_counts, grad_out):
    blocks = GLA * GLO
    flat_features = features.reshape(blocks * BS, CH)
    flat_grad = grad_out.reshape(blocks * BS, CH)
    queries = jnp.dot(flat_features, w_query, preferred_element_type=jnp.float32).astype(jnp.bfloat16).reshape(GLA, GLO, BS, CH)
    keys = jnp.dot(flat_features, w_key, preferred_element_type=jnp.float32).astype(jnp.bfloat16).reshape(blocks, BS, CH)
    values = jnp.dot(flat_features, w_value, preferred_element_type=jnp.float32).astype(jnp.bfloat16).reshape(blocks, BS, CH)
    bias_all = key_bias.reshape(blocks, HEADS, BS)
    grad_attended = jnp.dot(flat_grad, w_out.T, preferred_element_type=jnp.float32).astype(jnp.bfloat16).reshape(GLA, GLO, BS, CH)

    def one_row(carry, inputs):
        grad_keys, grad_values, grad_biases = carry
        query_row, neighbour_row, count_row, grad_row = inputs
        picks = neighbour_row.reshape(-1).astype(jnp.int32)
        key_rows = keys[picks].reshape(GLO, KB, BS, CH)
        value_rows = values[picks].reshape(GLO, KB, BS, CH)
        bias_rows = bias_all[picks].reshape(GLO, KB, HEADS, BS)
        attended, grad_query, grad_key, grad_value, grad_bias = attend_blocks(query_row, key_rows, value_rows, bias_rows, count_row, grad_row)
        carry = (grad_keys.at[picks].add(grad_key), grad_values.at[picks].add(grad_value), grad_biases.at[picks].add(grad_bias))
        return carry, (attended, grad_query)

    start = (jnp.zeros((blocks, BS, CH), jnp.float32), jnp.zeros((blocks, BS, CH), jnp.float32), jnp.zeros((blocks, HEADS, BS), jnp.float32))
    (grad_keys, grad_values, grad_biases), (attended, grad_queries) = lax.scan(one_row, start, (queries, neighbours, key_counts, grad_attended))
    weight_scale = float(blocks * BS) ** -0.5
    flat_attended = attended.reshape(blocks * BS, CH)
    grad_wo = jnp.dot(flat_attended.T, flat_grad, preferred_element_type=jnp.float32) * weight_scale
    wide_features = flat_features.astype(jnp.float32)
    query_flat = grad_queries.reshape(blocks * BS, CH)
    key_flat = grad_keys.reshape(blocks * BS, CH)
    value_flat = grad_values.reshape(blocks * BS, CH)
    highest = lax.Precision.HIGHEST
    grad_wq = jnp.dot(wide_features.T, query_flat, precision=highest) * weight_scale
    grad_wk = jnp.dot(wide_features.T, key_flat, precision=highest) * weight_scale
    grad_wv = jnp.dot(wide_features.T, value_flat, precision=highest) * weight_scale
    grad_features = jnp.dot(query_flat, w_query.astype(jnp.float32).T, precision=highest)
    grad_features = grad_features + jnp.dot(key_flat, w_key.astype(jnp.float32).T, precision=highest)
    grad_features = grad_features + jnp.dot(value_flat, w_value.astype(jnp.float32).T, precision=highest)
    grad_features = grad_features.astype(jnp.bfloat16).reshape(GLA, GLO, BS, CH)
    grad_bias = grad_biases.reshape(GLA, GLO, HEADS, BS)
    return grad_features, grad_bias, grad_wq, grad_wk, grad_wv, grad_wo
```

```python
import math

import jax
import jax.numpy as jnp
from jax import lax
from jax.experimental import pallas as pl
from jax.experimental.pallas import tpu as pltpu
from jax.sharding import PartitionSpec as P

MESH = pl.DeviceIdType.MESH
NXY = 16
NZ = 8
NPEER = NXY + NZ
ROWS = 32


def remote(src, dst, send_sem, recv_sem, device):
    return pltpu.make_async_remote_copy(
        src_ref=src, dst_ref=dst, send_sem=send_sem, recv_sem=recv_sem,
        device_id=device, device_id_type=MESH,
    )


def reduce_kernel(
    part, out, from_core, half, from_first, mine, from_second, total,
    core_send, core_recv, first_send, first_recv, second_send, second_recv,
    third_send, third_recv, fourth_send, fourth_recv,
):
    lat = lax.axis_index("lat")
    lon = lax.axis_index("lon")
    core = lon % 2
    z = (lon // 2) % NZ
    x_lo = lon // (2 * NZ)
    x_hi = lat // 4
    y = lat % 4
    xy = (x_hi * 2 + x_lo) * 4 + y
    partner = (lat, lon + 1 - 2 * core)
    base = core * NPEER
    other = (1 - core) * NPEER

    def plane_peer(index):
        x = index // 4
        return ((x // 2) * 4 + index % 4, (x % 2) * (2 * NZ) + z * 2 + core)

    def depth_peer(index):
        return (lat, x_lo * (2 * NZ) + index * 2 + core)

    barrier = pltpu.get_barrier_semaphore()
    pl.semaphore_signal(barrier, inc=1, device_id=partner, device_id_type=MESH)

    @pl.loop(1, NXY)
    def _(step):
        pl.semaphore_signal(barrier, inc=1, device_id=plane_peer((xy + step) % NXY), device_id_type=MESH)

    @pl.loop(1, NZ)
    def _(step):
        pl.semaphore_signal(barrier, inc=1, device_id=depth_peer((z + step) % NZ), device_id_type=MESH)

    pl.semaphore_wait(barrier, NPEER - 1)

    def chunks(step):
        return ((xy + 2 * step + 1) % NXY, (xy + 2 * step + 2) % NXY, NXY + (z + step + 1) % NZ)

    def core_copy(chunk):
        return remote(part.at[other + chunk], from_core.at[chunk], core_send.at[chunk], core_recv.at[chunk], partner)

    def first_copy(chunk, device, slot):
        return remote(half.at[chunk], from_first.at[slot], first_send.at[chunk], first_recv.at[slot], device)

    @pl.loop(0, NZ)
    def _(step):
        for chunk in chunks(step):
            core_copy(chunk).start()

    @pl.loop(0, NZ)
    def _(step):
        a, b, c = chunks(step)
        for chunk in (a, b, c):
            core_copy(chunk).wait_recv()
            half[chunk] = (part[base + chunk].astype(jnp.float32) + from_core[chunk].astype(jnp.float32)).astype(jnp.bfloat16)
        first_copy(a, plane_peer(a), xy).start()

        @pl.when(step < NZ - 1)
        def _():
            first_copy(b, plane_peer(b), xy).start()
            first_copy(c, depth_peer(c - NXY), NXY + z).start()

    from_first[xy] = half[xy]
    from_first[NXY + z] = half[NXY + z]

    def wait_first(step, index):
        slot = index
        first_copy(slot, partner, slot).wait_recv()

    @pl.loop(1, NZ)
    def _(step):
        wait_first(step, NXY + (z - step + NZ) % NZ)

    mine[1] = jnp.sum(from_first[NXY:NPEER].astype(jnp.float32), axis=0).astype(jnp.bfloat16)

    def second_b(index):
        return remote(mine.at[1], from_second.at[xy], second_send.at[index], second_recv.at[xy], plane_peer(index))

    def second_a(index):
        return remote(mine.at[0], from_second.at[NXY + z], second_send.at[NXY + index], second_recv.at[NXY + z], depth_peer(index))

    @pl.loop(1, NXY)
    def _(step):
        second_b((xy + step) % NXY).start()

    @pl.loop(1, NXY)
    def _(step):
        wait_first(step, (xy - step + NXY) % NXY)

    mine[0] = jnp.sum(from_first[0:NXY].astype(jnp.float32), axis=0).astype(jnp.bfloat16)

    @pl.loop(1, NZ)
    def _(step):
        second_a((z + step) % NZ).start()

    from_second[xy] = mine[1]
    from_second[NXY + z] = mine[0]

    def wait_second(slot):
        remote(mine.at[0], from_second.at[slot], second_send.at[slot], second_recv.at[slot], partner).wait_recv()

    def third_copy(which, slot, index, device):
        return remote(total.at[which], out.at[slot], third_send.at[index], third_recv.at[slot], device)

    def fourth_copy(slot):
        return remote(out.at[slot], out.at[slot], fourth_send.at[slot], fourth_recv.at[slot], partner)

    @pl.loop(1, NXY)
    def _(step):
        wait_second((xy - step + NXY) % NXY)

    total[1] = jnp.sum(from_second[0:NXY].astype(jnp.float32), axis=0).astype(jnp.bfloat16)

    @pl.loop(1, NZ)
    def _(step):
        index = (z + step) % NZ
        third_copy(1, base + NXY + z, NXY + index, depth_peer(index)).start()

    out[base + NXY + z] = total[1]
    fourth_copy(base + NXY + z).start()

    @pl.loop(1, NZ)
    def _(step):
        wait_second(NXY + (z - step + NZ) % NZ)

    total[0] = jnp.sum(from_second[NXY:NPEER].astype(jnp.float32), axis=0).astype(jnp.bfloat16)

    @pl.loop(1, NXY)
    def _(step):
        index = (xy + step) % NXY
        third_copy(0, base + xy, index, plane_peer(index)).start()

    out[base + xy] = total[0]
    fourth_copy(base + xy).start()

    def forward(slot):
        third_copy(0, slot, 0, partner).wait_recv()
        fourth_copy(slot).start()

    @pl.loop(1, NZ)
    def _(step):
        forward(base + NXY + (z - step + NZ) % NZ)

    @pl.loop(1, NXY)
    def _(step):
        forward(base + (xy - step + NXY) % NXY)

    @pl.loop(0, NPEER)
    def _(chunk):
        core_copy(chunk).wait_send()
        fourth_copy(base + chunk).wait_send()
        fourth_copy(other + chunk).wait_recv()

    @pl.loop(1, NXY)
    def _(step):
        index = (xy + step) % NXY
        first_copy(index, partner, index).wait_send()
        second_b(index).wait_send()
        third_copy(0, base + xy, index, partner).wait_send()

    @pl.loop(1, NZ)
    def _(step):
        index = (z + step) % NZ
        first_copy(NXY + index, partner, index).wait_send()
        second_a(index).wait_send()
        third_copy(1, base + xy, NXY + index, partner).wait_send()


def reduce_call(part):
    chans = part.shape[2]
    vmem = pl.BlockSpec(memory_space=pltpu.VMEM)
    low = lambda count: pltpu.VMEM((count, ROWS, chans), jnp.bfloat16)
    dma = pltpu.SemaphoreType.DMA
    return pl.pallas_call(
        reduce_kernel,
        out_shape=jax.ShapeDtypeStruct(part.shape, jnp.bfloat16),
        in_specs=[vmem],
        out_specs=vmem,
        scratch_shapes=[low(NPEER), low(NPEER), low(NPEER), low(2), low(NPEER), low(2)]
        + [dma((NPEER,))] * 7 + [dma((2 * NPEER,)), dma((2 * NPEER,)), dma((2 * NPEER,))],
        compiler_params=pltpu.CompilerParams(collective_id=0, has_side_effects=True, vmem_limit_bytes=32 << 20),
        name="sum_weight_gradients",
    )(part)


def with_halo(block, sides, width, periodic):
    for axis, dim in sides:
        count = lax.axis_size(axis)
        forward = [(i, i + 1) for i in range(count - 1)]
        if periodic:
            forward.append((count - 1, 0))
        backward = [(target, source) for source, target in forward]
        low = lax.ppermute(
            lax.slice_in_dim(block, block.shape[dim] - width, None, axis=dim), axis, forward
        )
        high = lax.ppermute(lax.slice_in_dim(block, 0, width, axis=dim), axis, backward)
        block = jnp.concatenate([low, block, high], axis=dim)
    return block


def attend_blocks(query_blocks, key_blocks, value_blocks, bias_blocks, counts, grad_blocks):
    groups = query_blocks.shape[0]
    slots = query_blocks.shape[1]
    chans = query_blocks.shape[2]
    entries = key_blocks.shape[1]
    heads = bias_blocks.shape[2]
    width = chans // heads
    scale = float(width) ** (-0.5)
    head_query = query_blocks.reshape(groups, slots, heads, width)
    head_key = key_blocks.reshape(groups, entries * slots, heads, width)
    head_value = value_blocks.reshape(groups, entries * slots, heads, width)
    bias_rows = (
        bias_blocks.astype(jnp.float32)
        .transpose(0, 2, 1, 3)
        .reshape(groups, heads, entries * slots)
    )
    valid = (jnp.arange(slots, dtype=jnp.int32)[None, None, :] < counts[:, :, None]).reshape(
        groups, entries * slots
    )
    scores = (
        jnp.einsum("gihd,gkhd->ghik", head_query, head_key, preferred_element_type=jnp.float32)
        * scale
    )
    scores = jnp.where(valid[:, None, None, :], scores + bias_rows[:, :, None, :], -jnp.inf)
    probs = jax.nn.softmax(scores, axis=-1)
    probs_low = probs.astype(jnp.bfloat16)
    attended = jnp.einsum(
        "ghik,gkhd->gihd", probs_low, head_value, preferred_element_type=jnp.float32
    )
    attended = attended.astype(jnp.bfloat16).reshape(groups, slots, chans)
    head_grad = grad_blocks.reshape(groups, slots, heads, width)
    grad_probs = jnp.einsum(
        "gihd,gkhd->ghik", head_grad, head_value, preferred_element_type=jnp.float32
    )
    centre = jnp.sum(probs * grad_probs, axis=-1, keepdims=True)
    grad_scores = probs * (grad_probs - centre)
    scores_low = grad_scores.astype(jnp.bfloat16)
    grad_query = (
        jnp.einsum("ghik,gkhd->gihd", scores_low, head_key, preferred_element_type=jnp.float32)
        * scale
    )
    grad_key = (
        jnp.einsum("ghik,gihd->gkhd", scores_low, head_query, preferred_element_type=jnp.float32)
        * scale
    )
    grad_value = jnp.einsum(
        "ghik,gihd->gkhd", probs_low, head_grad, preferred_element_type=jnp.float32
    )
    grad_bias = (
        jnp.sum(grad_scores, axis=2).reshape(groups, heads, entries, slots).transpose(0, 2, 1, 3)
    )
    return (
        attended,
        grad_query.reshape(groups, slots, chans),
        grad_key.reshape(groups * entries, slots, chans),
        grad_value.reshape(groups * entries, slots, chans),
        grad_bias.reshape(groups * entries, heads, slots),
    )


def split_parts(gradient):
    high_part = gradient.astype(jnp.bfloat16)
    low_part = (gradient - high_part.astype(jnp.float32)).astype(jnp.bfloat16)
    return (high_part, low_part)


def weight_product(inputs_low, gradient):
    high_part, low_part = split_parts(gradient)
    dims = (((0,), (0,)), ((), ()))
    result = lax.dot_general(inputs_low, high_part, dims, preferred_element_type=jnp.float32)
    return result + lax.dot_general(inputs_low, low_part, dims, preferred_element_type=jnp.float32)


def input_product(gradient, weight_low):
    high_part, low_part = split_parts(gradient)
    dims = (((1,), (1,)), ((), ()))
    result = lax.dot_general(high_part, weight_low, dims, preferred_element_type=jnp.float32)
    return result + lax.dot_general(low_part, weight_low, dims, preferred_element_type=jnp.float32)


def fold_rows(piece, exchange):
    rims = jnp.concatenate([piece[0:1], piece[-1:]], axis=0)
    coming = exchange(rims)
    middle = piece[1:-1]
    middle = middle.at[0].add(coming[0])
    middle = middle.at[-1].add(coming[3])
    return middle


def fold_columns(piece, exchange):
    rims = jnp.concatenate([piece[:, 0:1], piece[:, -1:]], axis=1)
    coming = exchange(rims)
    middle = piece[:, 1:-1]
    middle = middle.at[:, 0].add(coming[:, 0])
    middle = middle.at[:, -1].add(coming[:, 3])
    return middle


def per_device(
    features, w_query, w_key, w_value, w_out, key_bias, neighbours, key_counts, grad_out
):
    brows, bcols, slots, chans = features.shape
    heads = key_bias.shape[2]
    entries = neighbours.shape[2]
    nlat = lax.axis_size("lat")
    nlon = lax.axis_size("lon")
    glon = bcols * nlon
    lat_index = lax.axis_index("lat")
    lon_index = lax.axis_index("lon")
    blocks = brows * bcols
    extended = (brows + 2) * (bcols + 2)
    plane = slots * chans
    bias_size = heads * slots
    flat_features = features.reshape(blocks * slots, chans)
    flat_grad = grad_out.reshape(blocks * slots, chans)
    queries = jnp.dot(flat_features, w_query, preferred_element_type=jnp.float32).astype(
        jnp.bfloat16
    )
    queries = queries.reshape(blocks, slots, chans)
    bias_plane = key_bias.reshape(brows, bcols, bias_size)
    keys = jnp.dot(flat_features, w_key, preferred_element_type=jnp.float32).astype(jnp.bfloat16)
    values = jnp.dot(flat_features, w_value, preferred_element_type=jnp.float32).astype(
        jnp.bfloat16
    )
    packed = jnp.concatenate(
        [keys.reshape(brows, bcols, plane), values.reshape(brows, bcols, plane), bias_plane], axis=2
    )
    wide = with_halo(packed, (("lon", 1),), 1, True)
    ext_all = with_halo(wide, (("lat", 0),), 1, False)
    ext_keys = ext_all[:, :, :plane]
    ext_values = ext_all[:, :, plane : 2 * plane]
    ext_bias = ext_all[:, :, 2 * plane :]
    ext_keys = ext_keys.reshape(extended, slots, chans)
    ext_values = ext_values.reshape(extended, slots, chans)
    ext_bias = ext_bias.reshape(extended, heads, slots)
    global_ids = neighbours.reshape(blocks, entries)
    local_rows = global_ids // glon - lat_index * brows + 1
    local_columns = (global_ids % glon - lon_index * bcols + 1) % glon
    local_ids = local_rows * (bcols + 2) + local_columns
    grad_attended = jnp.dot(flat_grad, w_out.T, preferred_element_type=jnp.float32).astype(
        jnp.bfloat16
    )
    grad_attended = grad_attended.reshape(blocks, slots, chans)
    group = math.gcd(blocks, 4)
    rounds = blocks // group

    def one_group(carry, inputs):
        grad_keys, grad_values, grad_biases = carry
        query_group, id_group, count_group, grad_group = inputs
        picks = id_group.reshape(-1)
        key_group = ext_keys[picks].reshape(group, entries, slots, chans)
        value_group = ext_values[picks].reshape(group, entries, slots, chans)
        bias_group = ext_bias[picks].reshape(group, entries, heads, slots)
        attended, grad_query, grad_key, grad_value, grad_bias = attend_blocks(
            query_group, key_group, value_group, bias_group, count_group, grad_group
        )
        carry = (
            grad_keys.at[picks].add(grad_key),
            grad_values.at[picks].add(grad_value),
            grad_biases.at[picks].add(grad_bias),
        )
        return (carry, (attended, grad_query))

    start = (
        jnp.zeros((extended, slots, chans), jnp.float32),
        jnp.zeros((extended, slots, chans), jnp.float32),
        jnp.zeros((extended, heads, slots), jnp.float32),
    )
    scanned = (
        queries.reshape(rounds, group, slots, chans),
        local_ids.reshape(rounds, group, entries),
        key_counts,
        grad_attended.reshape(rounds, group, slots, chans),
    )
    (grad_keys, grad_values, grad_biases), (attended, grad_queries) = lax.scan(
        one_group, start, scanned
    )
    flat_attended = attended.reshape(blocks * slots, chans)
    grad_wo = jnp.dot(flat_attended.T, flat_grad, preferred_element_type=jnp.float32)
    query_flat = grad_queries.reshape(blocks * slots, chans)
    grad_wq = weight_product(flat_features, query_flat)
    grad_features = input_product(query_flat, w_query)
    bias_grid = grad_biases.reshape(brows + 2, bcols + 2, bias_size)
    key_grid = grad_keys.reshape(brows + 2, bcols + 2, plane)
    value_grid = grad_values.reshape(brows + 2, bcols + 2, plane)
    packed_grad = jnp.concatenate([key_grid, value_grid, bias_grid], axis=2)
    row_folded = fold_rows(
        packed_grad,
        lambda rims: with_halo(rims.astype(jnp.bfloat16), (("lat", 0),), 1, False).astype(
            rims.dtype
        ),
    )
    owned = fold_columns(
        row_folded,
        lambda rims: with_halo(rims.astype(jnp.bfloat16), (("lon", 1),), 1, True).astype(
            rims.dtype
        ),
    )
    key_flat = owned[:, :, :plane].reshape(blocks * slots, chans)
    value_flat = owned[:, :, plane : 2 * plane].reshape(blocks * slots, chans)
    bias_own = owned[:, :, 2 * plane :].reshape(brows, bcols, heads, slots)
    grad_wk = weight_product(flat_features, key_flat)
    grad_wv = weight_product(flat_features, value_flat)
    grad_features = grad_features + input_product(key_flat, w_key)
    grad_features = grad_features + input_product(value_flat, w_value)
    stacked = jnp.stack([grad_wq, grad_wk, grad_wv, grad_wo], axis=0)
    low = stacked.astype(jnp.bfloat16).reshape(2 * NPEER, ROWS, chans)
    summed = reduce_call(low).astype(jnp.float32).reshape(stacked.shape)
    weight_scale = float(brows * nlat * glon * slots) ** (-0.5)
    grad_features = grad_features.astype(jnp.bfloat16).reshape(brows, bcols, slots, chans)
    return (
        grad_features,
        bias_own,
        summed[0] * weight_scale,
        summed[1] * weight_scale,
        summed[2] * weight_scale,
        summed[3] * weight_scale,
    )


def solution(mesh):
    placed = (
        P("lat", "lon", None, None),
        P(),
        P(),
        P(),
        P(),
        P("lat", "lon", None, None),
        P("lat", "lon", None),
        P("lat", "lon", None),
        P("lat", "lon", None, None),
    )
    return jax.shard_map(
        per_device,
        mesh=mesh,
        in_specs=placed,
        out_specs=(P("lat", "lon", None, None), P("lat", "lon", None, None), P(), P(), P(), P()),
        check_vma=False,
    )
```

```python
import math

import jax
import jax.numpy as jnp
import numpy as np
from jax import lax
from jax.experimental import pallas as pl
from jax.experimental.pallas import tpu as pltpu
from jax.sharding import PartitionSpec as P

BF = jnp.bfloat16
F32 = jnp.float32
HEADS = 8
PAIR = 4
WINDOW = 256
NT = (((1,), (1,)), ((), ()))
TN = (((0,), (0,)), ((), ()))
FAR = -1e30


def bf16_parts(value, count):
    parts = []
    for _ in range(count):
        part = float(np.asarray(value, dtype=jnp.bfloat16).astype(np.float64))
        parts.append(part)
        value = value - part
    return parts


def mm(a, b, dims=None):
    if dims is None:
        return jnp.dot(a, b, preferred_element_type=F32)
    return lax.dot_general(a, b, dims, preferred_element_type=F32)


def attend_kernel(
    neighbours, counts, ext, ext_bias, grad_out, w_query, w_kv, w_out,
    halo, own, bias_sum, weights,
    gathered, scores, grad_probs, probs_low, scores_low, scores_rest, grad_kv, attended_t, grad_query_t, acc,
):
    lat = lax.axis_index("lat")
    lon = lax.axis_index("lon")
    columns = 2 * lax.axis_size("lon")

    def local_slot(block):
        row = lax.div(block, columns) - lat + 1
        column = lax.rem(lax.rem(block, columns) - 2 * lon + 1 + columns, columns)
        return column * 3 + row

    slots, chans = ext.shape[1:]
    width = chans // HEADS
    entries = counts.shape[0] // 2
    keys_all = entries * slots
    root = math.sqrt(width)
    parts = bf16_parts(root, 3)
    log2e = math.log2(math.e) / root
    lane = lax.broadcasted_iota(jnp.int32, (slots, WINDOW), 1)
    row = lax.broadcasted_iota(jnp.int32, (slots, WINDOW), 0)
    place_row = lax.broadcasted_iota(jnp.int32, (HEADS, WINDOW), 0)
    place_lane = lax.broadcasted_iota(jnp.int32, (HEADS, WINDOW), 1)
    pick_row = lax.broadcasted_iota(jnp.int32, (2 * HEADS, PAIR * slots), 0)
    pick_lane = lax.broadcasted_iota(jnp.int32, (2 * HEADS, PAIR * slots), 1)
    acc[...] = jnp.zeros_like(acc)
    bias_sum[...] = jnp.zeros_like(bias_sum)
    for b in range(2):
        picks = [local_slot(neighbours[b * entries + e]) for e in range(entries)]
        feat = ext[3 * (1 + b) + 1]
        grad_rows = grad_out[b]
        query = mm(feat, w_query[...]).astype(BF)
        grad_att = mm(grad_rows, w_out[...], NT).astype(BF)
        for e in range(entries):
            gathered[b, e * slots:(e + 1) * slots, :] = ext[picks[e]]
        kv = mm(gathered[b], w_kv[...]).astype(BF)
        bias_row = jnp.concatenate([ext_bias[picks[e]] for e in range(entries)], axis=1)
        bias_rows = jnp.zeros((2 * HEADS, keys_all), F32)
        for w in range(2):
            lo = w * (chans - WINDOW)
            first = PAIR * w
            spare = PAIR * width if w == 0 else 0
            region = (lane < PAIR * width) if w == 0 else (lane >= WINDOW - PAIR * width)
            place = jnp.zeros((HEADS, WINDOW), F32)
            for hh in range(PAIR):
                start = spare + 3 * hh
                place = jnp.where(
                    (place_row == first + hh) & (place_lane >= start) & (place_lane < start + 3), 1.0, place
                )
            bias_cols = mm(bias_row, place, TN)
            key_aug = []
            for e in range(entries):
                cols = bias_cols[e * slots:(e + 1) * slots]
                cols = jnp.where((lane == spare + 3 * PAIR) & (row >= counts[b * entries + e]), FAR, cols)
                piece = kv[e * slots:(e + 1) * slots, lo:lo + WINDOW]
                key_aug.append(jnp.where(region, piece.astype(F32), cols).astype(BF))
            key_aug = jnp.concatenate(key_aug, axis=0)
            value_win = kv[:, chans + lo:chans + lo + WINDOW]
            query_win = query[:, lo:lo + WINDOW].astype(F32)
            grad_win = grad_att[:, lo:lo + WINDOW].astype(F32)
            query_aug, grad_aug = [], []
            for hh in range(PAIR):
                inside = (lane >= (first + hh) * width - lo) & (lane < (first + hh + 1) * width - lo)
                const = jnp.where(lane == spare + 3 * PAIR, 1.0, 0.0)
                for t in range(3):
                    const = jnp.where(lane == spare + 3 * hh + t, parts[t], const)
                query_aug.append(jnp.where(inside, query_win, const).astype(BF))
                grad_aug.append(jnp.where(inside, grad_win, 0.0).astype(BF))
            query_aug = jnp.concatenate(query_aug, axis=0)
            grad_aug = jnp.concatenate(grad_aug, axis=0)
            scores[...] = mm(key_aug, query_aug, NT)
            grad_probs[...] = mm(value_win, grad_aug, NT)
            for hh in range(PAIR):
                cut = pl.ds(hh * slots, slots)
                logits = scores[:, cut]
                powers = jnp.exp2((logits - jnp.max(logits, axis=0, keepdims=True)) * log2e)
                probs = powers * (1.0 / jnp.sum(powers, axis=0, keepdims=True))
                probs_low[:, cut] = probs.astype(BF)
                grads = grad_probs[:, cut]
                centre = jnp.sum(probs * grads, axis=0, keepdims=True)
                full = probs * (grads - centre)
                high = full.astype(BF)
                scores_low[:, cut] = high
                scores_rest[:, cut] = (full - high.astype(F32)).astype(BF)
            value_grad = mm(probs_low[...], grad_aug)
            key_grad = mm(scores_low[...], query_aug)
            chosen = jnp.where(pick_lane // slots + first == pick_row, 1.0, 0.0).astype(BF)
            bias_rows = bias_rows + mm(chosen, scores_low[...], NT) + mm(chosen, scores_rest[...], NT)
            scale = 1.0 / root
            base = b * keys_all
            rows = pl.ds(base, keys_all)
            half = WINDOW // 2
            edge = PAIR * width - half
            low_lane = lane[0:1, 0:half]
            if w == 0:
                grad_kv[rows, 0:half] = (key_grad[:, 0:half] * scale).astype(BF)
                grad_kv[rows, chans:chans + half] = value_grad[:, 0:half].astype(BF)
                saved_key, saved_value = key_grad[:, half:], value_grad[:, half:]
            else:
                middle = jnp.where(low_lane < edge, saved_key, key_grad[:, 0:half]) * scale
                grad_kv[rows, half:2 * half] = middle.astype(BF)
                grad_kv[rows, 2 * half:3 * half] = (key_grad[:, half:] * scale).astype(BF)
                middle = saved_value + value_grad[:, 0:half]
                grad_kv[rows, chans + half:chans + 2 * half] = middle.astype(BF)
                grad_kv[rows, chans + 2 * half:chans + 3 * half] = value_grad[:, half:].astype(BF)
            for pair in range(2):
                head = first + 2 * pair
                cut = pl.ds(2 * pair * slots, 2 * slots)
                value_rows = kv[:, chans + head * width:chans + (head + 2) * width]
                key_rows = kv[:, head * width:(head + 2) * width]
                both = mm(value_rows, probs_low[:, cut], TN)
                attended_t[head * width:(head + 1) * width, b * slots:(b + 1) * slots] = both[:width, :slots].astype(BF)
                attended_t[(head + 1) * width:(head + 2) * width, b * slots:(b + 1) * slots] = both[width:, slots:].astype(BF)
                both = mm(key_rows, scores_low[:, cut], TN) * scale
                grad_query_t[head * width:(head + 1) * width, b * slots:(b + 1) * slots] = both[:width, :slots].astype(BF)
                grad_query_t[(head + 1) * width:(head + 2) * width, b * slots:(b + 1) * slots] = both[width:, slots:].astype(BF)
        for e in range(entries):
            bias_sum[picks[e]] += bias_rows[:HEADS, e * slots:(e + 1) * slots]
        grad_feat = mm(grad_kv[pl.ds(b * keys_all, keys_all), :], w_kv[...], NT)
        for e in range(entries):
            acc[picks[e]] += grad_feat[e * slots:(e + 1) * slots]
    grad_query = jnp.transpose(grad_query_t[...].astype(F32)).astype(BF)
    feat_both = jnp.concatenate([ext[4], ext[7]], axis=0)
    query_part = mm(grad_query, w_query[...], NT)
    own[0] = acc[4] + query_part[:slots]
    own[1] = acc[7] + query_part[slots:]
    halo[...] = acc[...].astype(BF)
    grad_both = grad_out[...].reshape(2 * slots, chans)
    weights[0:chans, :] = mm(feat_both, grad_query, TN).astype(BF)
    feat_all = gathered[...].reshape(2 * keys_all, chans)
    weight_kv = mm(feat_all, grad_kv[...], TN)
    weights[chans:2 * chans, :] = weight_kv[:, :chans].astype(BF)
    weights[2 * chans:3 * chans, :] = weight_kv[:, chans:].astype(BF)
    weights[3 * chans:, :] = mm(attended_t[...], grad_both).astype(BF)


def attend_call(ids, counts, ext, ext_bias, grad_out, w_query, w_kv, w_out):
    blocks, slots, chans = ext.shape
    keys_all = ids.shape[0] // 2 * slots
    vmem = pl.BlockSpec(memory_space=pltpu.VMEM)
    smem = pl.BlockSpec(memory_space=pltpu.SMEM)
    return pl.pallas_call(
        attend_kernel,
        out_shape=[
            jax.ShapeDtypeStruct((blocks, slots, chans), BF),
            jax.ShapeDtypeStruct((2, slots, chans), F32),
            jax.ShapeDtypeStruct((blocks, HEADS, slots), F32),
            jax.ShapeDtypeStruct((4 * chans, chans), BF),
        ],
        in_specs=[smem, smem] + [vmem] * 6,
        out_specs=[vmem] * 4,
        scratch_shapes=[
            pltpu.VMEM((2, keys_all, chans), BF),
            pltpu.VMEM((keys_all, PAIR * slots), F32),
            pltpu.VMEM((keys_all, PAIR * slots), F32),
            pltpu.VMEM((keys_all, PAIR * slots), BF),
            pltpu.VMEM((keys_all, PAIR * slots), BF),
            pltpu.VMEM((keys_all, PAIR * slots), BF),
            pltpu.VMEM((2 * keys_all, 2 * chans), BF),
            pltpu.VMEM((chans, 2 * slots), BF),
            pltpu.VMEM((chans, 2 * slots), BF),
            pltpu.VMEM((blocks, slots, chans), F32),
        ],
        compiler_params=pltpu.CompilerParams(vmem_limit_bytes=48 << 20),
        name="attend_backward",
    )(ids, counts, ext, ext_bias, grad_out, w_query, w_kv, w_out)


MESH = pl.DeviceIdType.MESH
NXY = 16
NZ = 8
NPEER = NXY + NZ
ROWS = 32


def remote(src, dst, send_sem, recv_sem, device):
    return pltpu.make_async_remote_copy(
        src_ref=src, dst_ref=dst, send_sem=send_sem, recv_sem=recv_sem,
        device_id=device, device_id_type=MESH,
    )


def reduce_kernel(
    part, halo, own, bias_sum, out, grad_feat, grad_bias, from_core, half, from_first, mine, from_second, total,
    core_send, core_recv, first_send, first_recv, second_send, second_recv,
    third_send, third_recv, fourth_send, fourth_recv,
    side, side_bias, rows_out, rows_bias, edge, edge_bias,
    side_send, side_recv, edge_send, edge_recv,
):
    lat = lax.axis_index("lat")
    lon = lax.axis_index("lon")
    core = lon % 2
    z = (lon // 2) % NZ
    x_lo = lon // (2 * NZ)
    x_hi = lat // 4
    y = lat % 4
    xy = (x_hi * 2 + x_lo) * 4 + y
    partner = (lat, lon + 1 - 2 * core)
    nlat = lax.axis_size("lat")
    nlon = lax.axis_size("lon")
    east = (lat, (lon + 1) % nlon)
    west = (lat, (lon + nlon - 1) % nlon)
    north = (lat - 1, lon)
    south = (lat + 1, lon)
    base = core * NPEER
    other = (1 - core) * NPEER

    def plane_peer(index):
        x = index // 4
        return ((x // 2) * 4 + index % 4, (x % 2) * (2 * NZ) + z * 2 + core)

    def depth_peer(index):
        return (lat, x_lo * (2 * NZ) + index * 2 + core)

    barrier = pltpu.get_barrier_semaphore()
    def greet(device):
        pl.semaphore_signal(barrier, inc=1, device_id=device, device_id_type=MESH)

    greet(east)
    greet(west)
    pl.when(lat > 0)(lambda: greet(north))
    pl.when(lat < nlat - 1)(lambda: greet(south))
    @pl.loop(1, NXY)
    def _(step):
        pl.semaphore_signal(barrier, inc=1, device_id=plane_peer((xy + step) % NXY), device_id_type=MESH)

    @pl.loop(1, NZ)
    def _(step):
        pl.semaphore_signal(barrier, inc=1, device_id=depth_peer((z + step) % NZ), device_id_type=MESH)

    inner = jnp.minimum(lat, 1) + jnp.minimum(nlat - 1 - lat, 1)
    pl.semaphore_wait(barrier, NPEER + inner)

    def side_copies(index):
        device = (west, east)[index]
        source = pl.ds(9 * index, 3)
        return (
            remote(halo.at[source], side.at[1 - index], side_send.at[2 * index], side_recv.at[2 - 2 * index], device),
            remote(bias_sum.at[source], side_bias.at[1 - index], side_send.at[2 * index + 1], side_recv.at[3 - 2 * index], device),
        )

    def edge_copies(index):
        device = (north, south)[index]
        return (
            remote(rows_out.at[index], edge.at[1 - index], edge_send.at[2 * index], edge_recv.at[2 - 2 * index], device),
            remote(rows_bias.at[index], edge_bias.at[1 - index], edge_send.at[2 * index + 1], edge_recv.at[3 - 2 * index], device),
        )

    def each(copies, what):
        for copy in copies:
            getattr(copy, what)()

    def chunks(step):
        return ((xy + 2 * step + 1) % NXY, (xy + 2 * step + 2) % NXY, NXY + (z + step + 1) % NZ)

    def core_copy(chunk):
        return remote(part.at[other + chunk], from_core.at[chunk], core_send.at[chunk], core_recv.at[chunk], partner)

    def first_copy(chunk, device, slot):
        return remote(half.at[chunk], from_first.at[slot], first_send.at[chunk], first_recv.at[slot], device)

    @pl.loop(0, NZ)
    def _(step):
        for chunk in chunks(step):
            core_copy(chunk).start()

    each(side_copies(0), "start")
    each(side_copies(1), "start")

    @pl.loop(0, NZ)
    def _(step):
        a, b, c = chunks(step)
        for chunk in (a, b, c):
            core_copy(chunk).wait_recv()
            half[chunk] = (part[base + chunk].astype(jnp.float32) + from_core[chunk].astype(jnp.float32)).astype(jnp.bfloat16)
        first_copy(a, plane_peer(a), xy).start()

        @pl.when(step < NZ - 1)
        def _():
            first_copy(b, plane_peer(b), xy).start()
            first_copy(c, depth_peer(c - NXY), NXY + z).start()

    each(side_copies(0), "wait_recv")
    each(side_copies(1), "wait_recv")
    for index in range(2):
        for j in range(2):
            slot = 3 * j + 3 + 2 * index
            rows_out[index, j] = (halo[slot].astype(F32) + side[j, 2 * index].astype(F32)).astype(BF)
            rows_bias[index, j] = bias_sum[slot] + side_bias[j, 2 * index]
    pl.when(lat > 0)(lambda: each(edge_copies(0), "start"))
    pl.when(lat < nlat - 1)(lambda: each(edge_copies(1), "start"))

    from_first[xy] = half[xy]
    from_first[NXY + z] = half[NXY + z]

    def wait_first(step, index):
        slot = index
        first_copy(slot, partner, slot).wait_recv()

    @pl.loop(1, NZ)
    def _(step):
        wait_first(step, NXY + (z - step + NZ) % NZ)

    mine[1] = jnp.sum(from_first[NXY:NPEER].astype(jnp.float32), axis=0).astype(jnp.bfloat16)

    def second_b(index):
        return remote(mine.at[1], from_second.at[xy], second_send.at[index], second_recv.at[xy], plane_peer(index))

    def second_a(index):
        return remote(mine.at[0], from_second.at[NXY + z], second_send.at[NXY + index], second_recv.at[NXY + z], depth_peer(index))

    @pl.loop(1, NXY)
    def _(step):
        second_b((xy + step) % NXY).start()

    @pl.loop(1, NXY)
    def _(step):
        wait_first(step, (xy - step + NXY) % NXY)

    mine[0] = jnp.sum(from_first[0:NXY].astype(jnp.float32), axis=0).astype(jnp.bfloat16)

    @pl.loop(1, NZ)
    def _(step):
        second_a((z + step) % NZ).start()

    from_second[xy] = mine[1]
    from_second[NXY + z] = mine[0]

    def wait_second(slot):
        remote(mine.at[0], from_second.at[slot], second_send.at[slot], second_recv.at[slot], partner).wait_recv()

    def third_copy(which, slot, index, device):
        return remote(total.at[which], out.at[slot], third_send.at[index], third_recv.at[slot], device)

    def fourth_copy(slot):
        return remote(out.at[slot], out.at[slot], fourth_send.at[slot], fourth_recv.at[slot], partner)

    @pl.loop(1, NXY)
    def _(step):
        wait_second((xy - step + NXY) % NXY)

    total[1] = jnp.sum(from_second[0:NXY].astype(jnp.float32), axis=0).astype(jnp.bfloat16)

    @pl.loop(1, NZ)
    def _(step):
        index = (z + step) % NZ
        third_copy(1, base + NXY + z, NXY + index, depth_peer(index)).start()

    out[base + NXY + z] = total[1]
    fourth_copy(base + NXY + z).start()

    @pl.loop(1, NZ)
    def _(step):
        wait_second(NXY + (z - step + NZ) % NZ)

    total[0] = jnp.sum(from_second[NXY:NPEER].astype(jnp.float32), axis=0).astype(jnp.bfloat16)

    @pl.loop(1, NXY)
    def _(step):
        index = (xy + step) % NXY
        third_copy(0, base + xy, index, plane_peer(index)).start()

    out[base + xy] = total[0]
    fourth_copy(base + xy).start()

    def forward(slot):
        third_copy(0, slot, 0, partner).wait_recv()
        fourth_copy(slot).start()

    @pl.loop(1, NZ)
    def _(step):
        forward(base + NXY + (z - step + NZ) % NZ)

    @pl.loop(1, NXY)
    def _(step):
        forward(base + (xy - step + NXY) % NXY)

    @pl.loop(0, NPEER)
    def _(chunk):
        core_copy(chunk).wait_send()
        fourth_copy(base + chunk).wait_send()
        fourth_copy(other + chunk).wait_recv()

    @pl.loop(1, NXY)
    def _(step):
        index = (xy + step) % NXY
        first_copy(index, partner, index).wait_send()
        second_b(index).wait_send()
        third_copy(0, base + xy, index, partner).wait_send()

    @pl.loop(1, NZ)
    def _(step):
        index = (z + step) % NZ
        first_copy(NXY + index, partner, index).wait_send()
        second_a(index).wait_send()
        third_copy(1, base + xy, NXY + index, partner).wait_send()

    each(side_copies(0), "wait_send")
    each(side_copies(1), "wait_send")

    @pl.when(lat == 0)
    def _():
        edge[0] = jnp.zeros_like(edge[0])
        edge_bias[0] = jnp.zeros_like(edge_bias[0])

    @pl.when(lat == nlat - 1)
    def _():
        edge[1] = jnp.zeros_like(edge[1])
        edge_bias[1] = jnp.zeros_like(edge_bias[1])

    @pl.when(lat > 0)
    def _():
        each(edge_copies(0), "wait_send")
        each(edge_copies(1), "wait_recv")

    @pl.when(lat < nlat - 1)
    def _():
        each(edge_copies(1), "wait_send")
        each(edge_copies(0), "wait_recv")

    for j in range(2):
        total_grad = own[j] + side[j, 1].astype(F32) + (edge[0, j].astype(F32) + edge[1, j].astype(F32))
        grad_feat[j] = total_grad.astype(BF)
        grad_bias[j] = bias_sum[3 * j + 4] + side_bias[j, 1] + (edge_bias[0, j] + edge_bias[1, j])


def reduce_call(part, halo, own, bias_sum):
    chans = part.shape[2]
    slots = own.shape[1]
    heads = bias_sum.shape[1]
    vmem = pl.BlockSpec(memory_space=pltpu.VMEM)
    low = lambda count: pltpu.VMEM((count, ROWS, chans), BF)
    dma = pltpu.SemaphoreType.DMA
    return pl.pallas_call(
        reduce_kernel,
        out_shape=[
            jax.ShapeDtypeStruct(part.shape, BF),
            jax.ShapeDtypeStruct((2, slots, chans), BF),
            jax.ShapeDtypeStruct((2, heads, slots), F32),
        ],
        in_specs=[vmem] * 4,
        out_specs=[vmem] * 3,
        scratch_shapes=[low(NPEER), low(NPEER), low(NPEER), low(2), low(NPEER), low(2)]
        + [dma((NPEER,))] * 7 + [dma((2 * NPEER,)), dma((2 * NPEER,)), dma((2 * NPEER,))]
        + [
            pltpu.VMEM((2, 3, slots, chans), BF),
            pltpu.VMEM((2, 3, heads, slots), F32),
            pltpu.VMEM((2, 2, slots, chans), BF),
            pltpu.VMEM((2, 2, heads, slots), F32),
            pltpu.VMEM((2, 2, slots, chans), BF),
            pltpu.VMEM((2, 2, heads, slots), F32),
        ]
        + [dma((4,))] * 4,
        compiler_params=pltpu.CompilerParams(collective_id=0, has_side_effects=True, vmem_limit_bytes=32 << 20),
        name="sum_gradients",
    )(part, halo, own, bias_sum)


def halo_kernel(feat, bias, ext, ext_bias, wide_send, wide_recv, bias_send, bias_recv):
    lat = lax.axis_index("lat")
    lon = lax.axis_index("lon")
    nlat = lax.axis_size("lat")
    nlon = lax.axis_size("lon")
    core = lon % 2
    east = (lat, (lon + 1) % nlon)
    west = (lat, (lon + nlon - 1) % nlon)
    north = (lat - 1, lon)
    south = (lat + 1, lon)
    barrier = pltpu.get_barrier_semaphore()

    def greet(device):
        pl.semaphore_signal(barrier, inc=1, device_id=device, device_id_type=MESH)

    greet(east)
    greet(west)
    pl.when(lat > 0)(lambda: greet(north))
    pl.when(lat < nlat - 1)(lambda: greet(south))
    for j in range(2):
        ext[3 * j + 4] = feat[j]
        ext_bias[3 * j + 4] = bias[j].astype(F32)
    inner = jnp.minimum(lat, 1) + jnp.minimum(nlat - 1 - lat, 1)
    pl.semaphore_wait(barrier, 2 + inner)

    def copies(source, target, order, device):
        return (
            remote(ext.at[source], ext.at[target], wide_send.at[order], wide_recv.at[target], device),
            remote(ext_bias.at[source], ext_bias.at[target], bias_send.at[order], bias_recv.at[target], device),
        )

    def start(*args):
        for copy in copies(*args):
            copy.start()

    def wait_recv(slot):
        for copy in copies(slot, slot, 0, east):
            copy.wait_recv()

    def wait_send(order):
        for copy in copies(4, 4, order, east):
            copy.wait_send()

    first = 4 + 3 * core
    second = 7 - 3 * core

    def to_north():
        start(first, first + 1, 0, north)
        start(second, second + 1, 1, north)

    def to_south():
        start(first, first - 1, 2, south)
        start(second, second - 1, 3, south)

    pl.when(lat > 0)(to_north)
    pl.when(lat < nlat - 1)(to_south)
    start(7, 1, 4, east)
    start(4, 10, 5, west)

    def pass_on(row, order):
        def send_west():
            wait_recv(3 + row)
            start(3 + row, 9 + row, order, west)

        def send_east():
            wait_recv(6 + row)
            start(6 + row, row, order + 1, east)

        @pl.when(core == 0)
        def _():
            send_west()
            send_east()

        @pl.when(core == 1)
        def _():
            send_east()
            send_west()

    pl.when(lat < nlat - 1)(lambda: pass_on(2, 6))
    pl.when(lat > 0)(lambda: pass_on(0, 8))
    wait_recv(1)
    wait_recv(10)
    wait_send(4)
    wait_send(5)

    @pl.when(lat > 0)
    def _():
        wait_recv(0)
        wait_recv(9)
        for order in (0, 1, 8, 9):
            wait_send(order)

    @pl.when(lat < nlat - 1)
    def _():
        wait_recv(2)
        wait_recv(11)
        for order in (2, 3, 6, 7):
            wait_send(order)


def halo_call(feat, bias):
    _, slots, chans = feat.shape
    heads = bias.shape[1]
    vmem = pl.BlockSpec(memory_space=pltpu.VMEM)
    dma = pltpu.SemaphoreType.DMA
    return pl.pallas_call(
        halo_kernel,
        out_shape=[
            jax.ShapeDtypeStruct((12, slots, chans), BF),
            jax.ShapeDtypeStruct((12, heads, slots), F32),
        ],
        in_specs=[vmem] * 2,
        out_specs=[vmem] * 2,
        scratch_shapes=[dma((10,)), dma((12,)), dma((10,)), dma((12,))],
        compiler_params=pltpu.CompilerParams(collective_id=1, has_side_effects=True, vmem_limit_bytes=16 << 20),
        name="gather_halo",
    )(feat, bias)


def per_device(
    features, w_query, w_key, w_value, w_out, key_bias, neighbours, key_counts, grad_out
):
    brows, bcols, slots, chans = features.shape
    heads = key_bias.shape[2]
    ext, ext_bias = halo_call(features[0], key_bias[0])
    halo, own, bias_sum, weights = attend_call(
        neighbours.reshape(-1), key_counts.reshape(-1), ext, ext_bias, grad_out[0],
        w_query, jnp.concatenate([w_key, w_value], axis=1), w_out,
    )
    low, grad_features, grad_bias = reduce_call(
        weights.reshape(2 * NPEER, ROWS, chans), halo, own, bias_sum
    )
    cells = lax.axis_size("lat") * lax.axis_size("lon") * brows * bcols * slots
    summed = low.astype(F32).reshape(4, chans, chans) * float(cells) ** (-0.5)
    return (
        grad_features.reshape(brows, bcols, slots, chans),
        grad_bias.reshape(brows, bcols, heads, slots),
        summed[0],
        summed[1],
        summed[2],
        summed[3],
    )


def solution(mesh):
    placed = (
        P("lat", "lon", None, None),
        P(),
        P(),
        P(),
        P(),
        P("lat", "lon", None, None),
        P("lat", "lon", None),
        P("lat", "lon", None),
        P("lat", "lon", None, None),
    )
    return jax.shard_map(
        per_device,
        mesh=mesh,
        in_specs=placed,
        out_specs=(P("lat", "lon", None, None), P("lat", "lon", None, None), P(), P(), P(), P()),
        check_vma=False,
    )
```

```python
import math

import jax
import jax.numpy as jnp
import numpy as np
from jax import lax
from jax.experimental import pallas as pl
from jax.experimental.pallas import tpu as pltpu
from jax.sharding import PartitionSpec as P

BF = jnp.bfloat16
F32 = jnp.float32
HEADS = 8
PAIR = 4
WINDOW = 256
NT = (((1,), (1,)), ((), ()))
TN = (((0,), (0,)), ((), ()))
FAR = -1e30


def bf16_parts(value, count):
    parts = []
    for _ in range(count):
        part = float(np.asarray(value, dtype=jnp.bfloat16).astype(np.float64))
        parts.append(part)
        value = value - part
    return parts


def mm(a, b, dims=None):
    if dims is None:
        return jnp.dot(a, b, preferred_element_type=F32)
    return lax.dot_general(a, b, dims, preferred_element_type=F32)


def attend(
    neighbours, counts, ext, ext_bias, grad_out, w_query, w_key, w_value, w_out, part,
    w_kv, gathered, scores, grad_probs, probs_low, scores_low, scores_rest, grad_kv,
    attended_t, grad_query_t, bias_parts,
):
    lat = lax.axis_index("lat")
    lon = lax.axis_index("lon")
    columns = 2 * lax.axis_size("lon")

    def local_slot(block):
        row = lax.div(block, columns) - lat + 1
        column = lax.rem(lax.rem(block, columns) - 2 * lon + 1 + columns, columns)
        return jnp.clip(column, 0, 3) * 3 + jnp.clip(row, 0, 2)

    slots, chans = ext.shape[1:]
    width = chans // HEADS
    entries = counts.shape[2]
    keys_all = entries * slots
    root = math.sqrt(width)
    parts = bf16_parts(root, 3)
    log2e = math.log2(math.e) / root
    lane = lax.broadcasted_iota(jnp.int32, (slots, WINDOW), 1)
    row = lax.broadcasted_iota(jnp.int32, (slots, WINDOW), 0)
    place_row = lax.broadcasted_iota(jnp.int32, (HEADS, WINDOW), 0)
    place_lane = lax.broadcasted_iota(jnp.int32, (HEADS, WINDOW), 1)
    pick_row = lax.broadcasted_iota(jnp.int32, (2 * HEADS, PAIR * slots), 0)
    pick_lane = lax.broadcasted_iota(jnp.int32, (2 * HEADS, PAIR * slots), 1)
    w_kv[:, :chans] = w_key[...]
    w_kv[:, chans:] = w_value[...]
    all_picks = []
    for b in range(2):
        picks = [local_slot(neighbours[0, b, e]) for e in range(entries)]
        all_picks.append(picks)
        feat = ext[3 * (1 + b) + 1]
        grad_rows = grad_out[b]
        query = mm(feat, w_query[...]).astype(BF)
        grad_att = mm(grad_rows, w_out[...], NT).astype(BF)
        for e in range(entries):
            gathered[b, e * slots:(e + 1) * slots, :] = ext[picks[e]]
        kv = mm(gathered[b], w_kv[...]).astype(BF)
        bias_row = jnp.concatenate([ext_bias[picks[e]] for e in range(entries)], axis=1)
        bias_rows = jnp.zeros((2 * HEADS, keys_all), F32)
        for w in range(2):
            lo = w * (chans - WINDOW)
            first = PAIR * w
            spare = PAIR * width if w == 0 else 0
            region = (lane < PAIR * width) if w == 0 else (lane >= WINDOW - PAIR * width)
            place = jnp.zeros((HEADS, WINDOW), F32)
            for hh in range(PAIR):
                start = spare + 3 * hh
                place = jnp.where(
                    (place_row == first + hh) & (place_lane >= start) & (place_lane < start + 3), 1.0, place
                )
            bias_cols = mm(bias_row, place, TN)
            key_aug = []
            for e in range(entries):
                cols = bias_cols[e * slots:(e + 1) * slots]
                cols = jnp.where((lane == spare + 3 * PAIR) & (row >= counts[0, b, e]), FAR, cols)
                piece = kv[e * slots:(e + 1) * slots, lo:lo + WINDOW]
                key_aug.append(jnp.where(region, piece.astype(F32), cols).astype(BF))
            key_aug = jnp.concatenate(key_aug, axis=0)
            value_win = kv[:, chans + lo:chans + lo + WINDOW]
            query_win = query[:, lo:lo + WINDOW].astype(F32)
            grad_win = grad_att[:, lo:lo + WINDOW].astype(F32)
            query_aug, grad_aug = [], []
            for hh in range(PAIR):
                inside = (lane >= (first + hh) * width - lo) & (lane < (first + hh + 1) * width - lo)
                const = jnp.where(lane == spare + 3 * PAIR, 1.0, 0.0)
                for t in range(3):
                    const = jnp.where(lane == spare + 3 * hh + t, parts[t], const)
                query_aug.append(jnp.where(inside, query_win, const).astype(BF))
                grad_aug.append(jnp.where(inside, grad_win, 0.0).astype(BF))
            query_aug = jnp.concatenate(query_aug, axis=0)
            grad_aug = jnp.concatenate(grad_aug, axis=0)
            scores[...] = mm(key_aug, query_aug, NT)
            grad_probs[...] = mm(value_win, grad_aug, NT)
            for hh in range(PAIR):
                cut = pl.ds(hh * slots, slots)
                logits = scores[:, cut]
                powers = jnp.exp2((logits - jnp.max(logits, axis=0, keepdims=True)) * log2e)
                probs = powers * (1.0 / jnp.sum(powers, axis=0, keepdims=True))
                probs_low[:, cut] = probs.astype(BF)
                grads = grad_probs[:, cut]
                centre = jnp.sum(probs * grads, axis=0, keepdims=True)
                full = probs * (grads - centre)
                high = full.astype(BF)
                scores_low[:, cut] = high
                scores_rest[:, cut] = (full - high.astype(F32)).astype(BF)
            value_grad = mm(probs_low[...], grad_aug)
            key_grad = mm(scores_low[...], query_aug)
            chosen = jnp.where(pick_lane // slots + first == pick_row, 1.0, 0.0).astype(BF)
            bias_rows = bias_rows + mm(chosen, scores_low[...], NT) + mm(chosen, scores_rest[...], NT)
            scale = 1.0 / root
            base = b * keys_all
            rows = pl.ds(base, keys_all)
            half = WINDOW // 2
            edge = PAIR * width - half
            low_lane = lane[0:1, 0:half]
            if w == 0:
                grad_kv[rows, 0:half] = (key_grad[:, 0:half] * scale).astype(BF)
                grad_kv[rows, chans:chans + half] = value_grad[:, 0:half].astype(BF)
                saved_key, saved_value = key_grad[:, half:], value_grad[:, half:]
            else:
                middle = jnp.where(low_lane < edge, saved_key, key_grad[:, 0:half]) * scale
                grad_kv[rows, half:2 * half] = middle.astype(BF)
                grad_kv[rows, 2 * half:3 * half] = (key_grad[:, half:] * scale).astype(BF)
                middle = saved_value + value_grad[:, 0:half]
                grad_kv[rows, chans + half:chans + 2 * half] = middle.astype(BF)
                grad_kv[rows, chans + 2 * half:chans + 3 * half] = value_grad[:, half:].astype(BF)
            for pair in range(2):
                head = first + 2 * pair
                cut = pl.ds(2 * pair * slots, 2 * slots)
                value_rows = kv[:, chans + head * width:chans + (head + 2) * width]
                key_rows = kv[:, head * width:(head + 2) * width]
                both = mm(value_rows, probs_low[:, cut], TN)
                attended_t[head * width:(head + 1) * width, b * slots:(b + 1) * slots] = both[:width, :slots].astype(BF)
                attended_t[(head + 1) * width:(head + 2) * width, b * slots:(b + 1) * slots] = both[width:, slots:].astype(BF)
                both = mm(key_rows, scores_low[:, cut], TN) * scale
                grad_query_t[head * width:(head + 1) * width, b * slots:(b + 1) * slots] = both[:width, :slots].astype(BF)
                grad_query_t[(head + 1) * width:(head + 2) * width, b * slots:(b + 1) * slots] = both[width:, slots:].astype(BF)
        for e in range(entries):
            bias_parts[b, e] = bias_rows[:HEADS, e * slots:(e + 1) * slots]
    grad_query = jnp.transpose(grad_query_t[...].astype(F32)).astype(BF)
    feat_both = jnp.concatenate([ext[4], ext[7]], axis=0)
    grad_both = grad_out[...].reshape(2 * slots, chans)
    piece = chans // ROWS

    def put(index, value):
        part[index * piece:(index + 1) * piece] = value.astype(BF).reshape(piece, ROWS, chans)

    put(0, mm(feat_both, grad_query, TN))
    put(3, mm(attended_t[...], grad_both))
    weight_kv = mm(gathered[...].reshape(2 * keys_all, chans), grad_kv[...], TN)
    put(1, weight_kv[:, :chans])
    put(2, weight_kv[:, chans:])
    return all_picks, grad_query


def scatter(all_picks, grad_query, w_query, w_kv, grad_kv, bias_parts, feat_parts, halo, own, bias_sum):
    slots, chans = halo.shape[1:]
    entries = len(all_picks[0])
    keys_all = entries * slots
    for b in range(2):
        feat_parts[b] = mm(grad_kv[pl.ds(b * keys_all, keys_all), :], w_kv[...], NT)
    query_part = mm(grad_query, w_query[...], NT)
    for slot in range(halo.shape[0]):
        column = slot // 3
        total, bias_total = None, None
        for b in range(2):
            if column - b not in (0, 1, 2):
                continue
            for e in range(1, entries):
                hit = all_picks[b][e] == slot
                piece = jnp.where(hit, feat_parts[b, e * slots:(e + 1) * slots], 0.0)
                total = piece if total is None else total + piece
                piece = jnp.where(hit, bias_parts[b, e], 0.0)
                bias_total = piece if bias_total is None else bias_total + piece
        if slot in (4, 7):
            b = column - 1
            own[b] = total + (feat_parts[b, 0:slots] + query_part[b * slots:(b + 1) * slots])
            bias_total = bias_total + bias_parts[b, 0]
        else:
            halo[slot] = total.astype(BF)
        bias_sum[slot] = bias_total


MESH = pl.DeviceIdType.MESH
NXY = 16
NZ = 8
NPEER = NXY + NZ
ROWS = 32


def remote(src, dst, send_sem, recv_sem, device):
    return pltpu.make_async_remote_copy(
        src_ref=src, dst_ref=dst, send_sem=send_sem, recv_sem=recv_sem,
        device_id=device, device_id_type=MESH,
    )


def layer_kernel(
    neighbours, counts, ext, ext_bias, grad_out, w_query, w_key, w_value, w_out,
    out, grad_feat, grad_bias,
    part, halo, own, bias_sum, feat_parts, bias_parts, w_kv, gathered, scores, grad_probs, probs_low,
    scores_low, scores_rest, grad_kv, attended_t, grad_query_t, from_core, half, from_first, mine, from_second, total,
    core_send, core_recv, first_send, first_recv, second_send, second_recv,
    third_send, third_recv, fourth_send, fourth_recv,
    side, side_bias, rows_out, rows_bias, edge, edge_bias,
    side_send, side_recv, edge_send, edge_recv,
):
    lat = lax.axis_index("lat")
    lon = lax.axis_index("lon")
    core = lon % 2
    z = (lon // 2) % NZ
    x_lo = lon // (2 * NZ)
    x_hi = lat // 4
    y = lat % 4
    xy = (x_hi * 2 + x_lo) * 4 + y
    partner = (lat, lon + 1 - 2 * core)
    nlat = lax.axis_size("lat")
    nlon = lax.axis_size("lon")
    east = (lat, (lon + 1) % nlon)
    west = (lat, (lon + nlon - 1) % nlon)
    north = (lat - 1, lon)
    south = (lat + 1, lon)
    base = core * NPEER
    other = (1 - core) * NPEER

    def plane_peer(index):
        x = index // 4
        return ((x // 2) * 4 + index % 4, (x % 2) * (2 * NZ) + z * 2 + core)

    def depth_peer(index):
        return (lat, x_lo * (2 * NZ) + index * 2 + core)

    barrier = pltpu.get_barrier_semaphore()
    def greet(device):
        pl.semaphore_signal(barrier, inc=1, device_id=device, device_id_type=MESH)

    greet(east)
    greet(west)
    pl.when(lat > 0)(lambda: greet(north))
    pl.when(lat < nlat - 1)(lambda: greet(south))
    @pl.loop(1, NXY)
    def _(step):
        pl.semaphore_signal(barrier, inc=1, device_id=plane_peer((xy + step) % NXY), device_id_type=MESH)

    @pl.loop(1, NZ)
    def _(step):
        pl.semaphore_signal(barrier, inc=1, device_id=depth_peer((z + step) % NZ), device_id_type=MESH)

    all_picks, grad_query = attend(
        neighbours, counts, ext, ext_bias, grad_out, w_query, w_key, w_value, w_out, part,
        w_kv, gathered, scores, grad_probs, probs_low, scores_low, scores_rest, grad_kv,
        attended_t, grad_query_t, bias_parts,
    )
    inner = jnp.minimum(lat, 1) + jnp.minimum(nlat - 1 - lat, 1)
    pl.semaphore_wait(barrier, NPEER + inner)

    def side_copies(index):
        device = (west, east)[index]
        source = pl.ds(9 * index, 3)
        return (
            remote(halo.at[source], side.at[1 - index], side_send.at[2 * index], side_recv.at[2 - 2 * index], device),
            remote(bias_sum.at[source], side_bias.at[1 - index], side_send.at[2 * index + 1], side_recv.at[3 - 2 * index], device),
        )

    def edge_copies(index):
        device = (north, south)[index]
        return (
            remote(rows_out.at[index], edge.at[1 - index], edge_send.at[2 * index], edge_recv.at[2 - 2 * index], device),
            remote(rows_bias.at[index], edge_bias.at[1 - index], edge_send.at[2 * index + 1], edge_recv.at[3 - 2 * index], device),
        )

    def each(copies, what):
        for copy in copies:
            getattr(copy, what)()

    def chunks(step):
        return ((xy + 2 * step + 1) % NXY, (xy + 2 * step + 2) % NXY, NXY + (z + step + 1) % NZ)

    def core_copy(chunk):
        return remote(part.at[other + chunk], from_core.at[chunk], core_send.at[chunk], core_recv.at[chunk], partner)

    def first_copy(chunk, device, slot):
        return remote(half.at[chunk], from_first.at[slot], first_send.at[chunk], first_recv.at[slot], device)

    @pl.loop(0, NZ)
    def _(step):
        for chunk in chunks(step):
            core_copy(chunk).start()

    scatter(all_picks, grad_query, w_query, w_kv, grad_kv, bias_parts, feat_parts, halo, own, bias_sum)
    each(side_copies(0), "start")
    each(side_copies(1), "start")

    @pl.loop(0, NZ)
    def _(step):
        a, b, c = chunks(step)
        for chunk in (a, b, c):
            core_copy(chunk).wait_recv()
            half[chunk] = (part[base + chunk].astype(jnp.float32) + from_core[chunk].astype(jnp.float32)).astype(jnp.bfloat16)
        first_copy(a, plane_peer(a), xy).start()

        @pl.when(step < NZ - 1)
        def _():
            first_copy(b, plane_peer(b), xy).start()
            first_copy(c, depth_peer(c - NXY), NXY + z).start()

    each(side_copies(0), "wait_recv")
    each(side_copies(1), "wait_recv")
    for index in range(2):
        for j in range(2):
            slot = 3 * j + 3 + 2 * index
            rows_out[index, j] = (halo[slot].astype(F32) + side[j, 2 * index].astype(F32)).astype(BF)
            rows_bias[index, j] = bias_sum[slot] + side_bias[j, 2 * index]
    pl.when(lat > 0)(lambda: each(edge_copies(0), "start"))
    pl.when(lat < nlat - 1)(lambda: each(edge_copies(1), "start"))

    from_first[xy] = half[xy]
    from_first[NXY + z] = half[NXY + z]

    def wait_first(step, index):
        slot = index
        first_copy(slot, partner, slot).wait_recv()

    @pl.loop(1, NZ)
    def _(step):
        wait_first(step, NXY + (z - step + NZ) % NZ)

    mine[1] = jnp.sum(from_first[NXY:NPEER].astype(jnp.float32), axis=0).astype(jnp.bfloat16)

    def second_b(index):
        return remote(mine.at[1], from_second.at[xy], second_send.at[index], second_recv.at[xy], plane_peer(index))

    def second_a(index):
        return remote(mine.at[0], from_second.at[NXY + z], second_send.at[NXY + index], second_recv.at[NXY + z], depth_peer(index))

    @pl.loop(1, NXY)
    def _(step):
        second_b((xy + step) % NXY).start()

    @pl.loop(1, NXY)
    def _(step):
        wait_first(step, (xy - step + NXY) % NXY)

    mine[0] = jnp.sum(from_first[0:NXY].astype(jnp.float32), axis=0).astype(jnp.bfloat16)

    @pl.loop(1, NZ)
    def _(step):
        second_a((z + step) % NZ).start()

    from_second[xy] = mine[1]
    from_second[NXY + z] = mine[0]

    def wait_second(slot):
        remote(mine.at[0], from_second.at[slot], second_send.at[slot], second_recv.at[slot], partner).wait_recv()

    def third_copy(which, slot, index, device):
        return remote(total.at[which], out.at[slot], third_send.at[index], third_recv.at[slot], device)

    def fourth_copy(slot):
        return remote(out.at[slot], out.at[slot], fourth_send.at[slot], fourth_recv.at[slot], partner)

    @pl.loop(1, NXY)
    def _(step):
        wait_second((xy - step + NXY) % NXY)

    total[1] = jnp.sum(from_second[0:NXY].astype(jnp.float32), axis=0).astype(jnp.bfloat16)

    @pl.loop(1, NZ)
    def _(step):
        index = (z + step) % NZ
        third_copy(1, base + NXY + z, NXY + index, depth_peer(index)).start()

    out[base + NXY + z] = total[1]
    fourth_copy(base + NXY + z).start()

    @pl.loop(1, NZ)
    def _(step):
        wait_second(NXY + (z - step + NZ) % NZ)

    total[0] = jnp.sum(from_second[NXY:NPEER].astype(jnp.float32), axis=0).astype(jnp.bfloat16)

    @pl.loop(1, NXY)
    def _(step):
        index = (xy + step) % NXY
        third_copy(0, base + xy, index, plane_peer(index)).start()

    out[base + xy] = total[0]
    fourth_copy(base + xy).start()

    def forward(slot):
        third_copy(0, slot, 0, partner).wait_recv()
        fourth_copy(slot).start()

    @pl.loop(1, NZ)
    def _(step):
        forward(base + NXY + (z - step + NZ) % NZ)

    @pl.loop(1, NXY)
    def _(step):
        forward(base + (xy - step + NXY) % NXY)

    @pl.loop(0, NPEER)
    def _(chunk):
        core_copy(chunk).wait_send()
        fourth_copy(base + chunk).wait_send()
        fourth_copy(other + chunk).wait_recv()

    @pl.loop(1, NXY)
    def _(step):
        index = (xy + step) % NXY
        first_copy(index, partner, index).wait_send()
        second_b(index).wait_send()
        third_copy(0, base + xy, index, partner).wait_send()

    @pl.loop(1, NZ)
    def _(step):
        index = (z + step) % NZ
        first_copy(NXY + index, partner, index).wait_send()
        second_a(index).wait_send()
        third_copy(1, base + xy, NXY + index, partner).wait_send()

    each(side_copies(0), "wait_send")
    each(side_copies(1), "wait_send")

    @pl.when(lat == 0)
    def _():
        edge[0] = jnp.zeros_like(edge[0])
        edge_bias[0] = jnp.zeros_like(edge_bias[0])

    @pl.when(lat == nlat - 1)
    def _():
        edge[1] = jnp.zeros_like(edge[1])
        edge_bias[1] = jnp.zeros_like(edge_bias[1])

    @pl.when(lat > 0)
    def _():
        each(edge_copies(0), "wait_send")
        each(edge_copies(1), "wait_recv")

    @pl.when(lat < nlat - 1)
    def _():
        each(edge_copies(1), "wait_send")
        each(edge_copies(0), "wait_recv")

    for j in range(2):
        total_grad = own[j] + side[j, 1].astype(F32) + (edge[0, j].astype(F32) + edge[1, j].astype(F32))
        grad_feat[j] = total_grad.astype(BF)
        grad_bias[j] = bias_sum[3 * j + 4] + side_bias[j, 1] + (edge_bias[0, j] + edge_bias[1, j])


def layer_call(neighbours, counts, ext, ext_bias, grad_out, w_query, w_key, w_value, w_out):
    blocks, slots, chans = ext.shape
    heads = ext_bias.shape[1]
    entries = counts.shape[2]
    keys_all = entries * slots
    vmem = pl.BlockSpec(memory_space=pltpu.VMEM)
    smem = pl.BlockSpec(memory_space=pltpu.SMEM)
    low = lambda *shape: pltpu.VMEM(shape, BF)
    wide = lambda *shape: pltpu.VMEM(shape, F32)
    dma = pltpu.SemaphoreType.DMA
    return pl.pallas_call(
        layer_kernel,
        out_shape=[
            jax.ShapeDtypeStruct((2 * NPEER, ROWS, chans), BF),
            jax.ShapeDtypeStruct((2, slots, chans), BF),
            jax.ShapeDtypeStruct((2, heads, slots), F32),
        ],
        in_specs=[smem] * 2 + [vmem] * 7,
        out_specs=[vmem] * 3,
        scratch_shapes=[
            low(2 * NPEER, ROWS, chans),
            low(blocks, slots, chans),
            wide(2, slots, chans),
            wide(blocks, heads, slots),
            wide(2, keys_all, chans),
            wide(2, entries, heads, slots),
            low(chans, 2 * chans),
            low(2, keys_all, chans),
            wide(keys_all, PAIR * slots),
            wide(keys_all, PAIR * slots),
            low(keys_all, PAIR * slots),
            low(keys_all, PAIR * slots),
            low(keys_all, PAIR * slots),
            low(2 * keys_all, 2 * chans),
            low(chans, 2 * slots),
            low(chans, 2 * slots),
            low(NPEER, ROWS, chans),
            low(NPEER, ROWS, chans),
            low(NPEER, ROWS, chans),
            low(2, ROWS, chans),
            low(NPEER, ROWS, chans),
            low(2, ROWS, chans),
        ]
        + [dma((NPEER,))] * 7 + [dma((2 * NPEER,))] * 3
        + [
            low(2, 3, slots, chans),
            wide(2, 3, heads, slots),
            low(2, 2, slots, chans),
            wide(2, 2, heads, slots),
            low(2, 2, slots, chans),
            wide(2, 2, heads, slots),
        ]
        + [dma((4,))] * 4,
        compiler_params=pltpu.CompilerParams(collective_id=0, has_side_effects=True, vmem_limit_bytes=48 << 20),
        name="layer_backward",
    )(neighbours, counts, ext, ext_bias, grad_out, w_query, w_key, w_value, w_out)


def halo_kernel(feat, bias, ext, ext_bias, wide_send, wide_recv, bias_send, bias_recv):
    lat = lax.axis_index("lat")
    lon = lax.axis_index("lon")
    nlat = lax.axis_size("lat")
    nlon = lax.axis_size("lon")
    core = lon % 2
    east = (lat, (lon + 1) % nlon)
    west = (lat, (lon + nlon - 1) % nlon)
    north = (lat - 1, lon)
    south = (lat + 1, lon)
    barrier = pltpu.get_barrier_semaphore()

    def greet(device):
        pl.semaphore_signal(barrier, inc=1, device_id=device, device_id_type=MESH)

    greet(east)
    greet(west)
    pl.when(lat > 0)(lambda: greet(north))
    pl.when(lat < nlat - 1)(lambda: greet(south))
    for j in range(2):
        ext[3 * j + 4] = feat[j]
        ext_bias[3 * j + 4] = bias[j].astype(F32)
    inner = jnp.minimum(lat, 1) + jnp.minimum(nlat - 1 - lat, 1)
    pl.semaphore_wait(barrier, 2 + inner)

    def copies(source, target, order, device):
        return (
            remote(ext.at[source], ext.at[target], wide_send.at[order], wide_recv.at[target], device),
            remote(ext_bias.at[source], ext_bias.at[target], bias_send.at[order], bias_recv.at[target], device),
        )

    def start(*args):
        for copy in copies(*args):
            copy.start()

    def wait_recv(slot):
        for copy in copies(slot, slot, 0, east):
            copy.wait_recv()

    def wait_send(order):
        for copy in copies(4, 4, order, east):
            copy.wait_send()

    first = 4 + 3 * core
    second = 7 - 3 * core

    def to_north():
        start(first, first + 1, 0, north)
        start(second, second + 1, 1, north)

    def to_south():
        start(first, first - 1, 2, south)
        start(second, second - 1, 3, south)

    seam = nlat // 2
    pl.when(lat == seam - 1)(to_south)
    pl.when(lat > 0)(to_north)
    pl.when((lat < nlat - 1) & (lat != seam - 1))(to_south)
    start(7, 1, 4, east)
    start(4, 10, 5, west)

    def pass_on(row, order):
        def send_west():
            wait_recv(3 + row)
            start(3 + row, 9 + row, order, west)

        def send_east():
            wait_recv(6 + row)
            start(6 + row, row, order + 1, east)

        @pl.when(core == 0)
        def _():
            send_west()
            send_east()

        @pl.when(core == 1)
        def _():
            send_east()
            send_west()

    pl.when(lat == seam - 1)(lambda: pass_on(0, 8))
    pl.when(lat < nlat - 1)(lambda: pass_on(2, 6))
    pl.when((lat > 0) & (lat != seam - 1))(lambda: pass_on(0, 8))
    wait_recv(1)
    wait_recv(10)
    wait_send(4)
    wait_send(5)

    @pl.when(lat > 0)
    def _():
        wait_recv(0)
        wait_recv(9)
        for order in (0, 1, 8, 9):
            wait_send(order)

    @pl.when(lat < nlat - 1)
    def _():
        wait_recv(2)
        wait_recv(11)
        for order in (2, 3, 6, 7):
            wait_send(order)


def halo_call(feat, bias):
    _, slots, chans = feat.shape
    heads = bias.shape[1]
    vmem = pl.BlockSpec(memory_space=pltpu.VMEM)
    dma = pltpu.SemaphoreType.DMA
    return pl.pallas_call(
        halo_kernel,
        out_shape=[
            jax.ShapeDtypeStruct((12, slots, chans), BF),
            jax.ShapeDtypeStruct((12, heads, slots), F32),
        ],
        in_specs=[vmem] * 2,
        out_specs=[vmem] * 2,
        scratch_shapes=[dma((10,)), dma((12,)), dma((10,)), dma((12,))],
        compiler_params=pltpu.CompilerParams(collective_id=1, has_side_effects=True, vmem_limit_bytes=16 << 20),
        name="gather_halo",
    )(feat, bias)


def per_device(
    features, w_query, w_key, w_value, w_out, key_bias, neighbours, key_counts, grad_out
):
    brows, bcols, slots, chans = features.shape
    heads = key_bias.shape[2]
    ext, ext_bias = halo_call(features[0], key_bias[0])
    low, grad_features, grad_bias = layer_call(
        neighbours, key_counts, ext, ext_bias, grad_out[0], w_query, w_key, w_value, w_out
    )
    cells = lax.axis_size("lat") * lax.axis_size("lon") * brows * bcols * slots
    summed = low.astype(F32).reshape(4, chans, chans) * float(cells) ** (-0.5)
    return (
        grad_features.reshape(brows, bcols, slots, chans),
        grad_bias.reshape(brows, bcols, heads, slots),
        summed[0],
        summed[1],
        summed[2],
        summed[3],
    )


def solution(mesh):
    placed = (
        P("lat", "lon", None, None),
        P(),
        P(),
        P(),
        P(),
        P("lat", "lon", None, None),
        P("lat", "lon", None),
        P("lat", "lon", None),
        P("lat", "lon", None, None),
    )
    return jax.shard_map(
        per_device,
        mesh=mesh,
        in_specs=placed,
        out_specs=(P("lat", "lon", None, None), P("lat", "lon", None, None), P(), P(), P(), P()),
        check_vma=False,
    )
```

```python
import math

import jax
import jax.numpy as jnp
import numpy as np
from jax import lax
from jax.experimental import pallas as pl
from jax.experimental.pallas import tpu as pltpu
from jax.sharding import PartitionSpec as P

BF = jnp.bfloat16
F32 = jnp.float32
HEADS = 8
PAIR = 4
WINDOW = 256
NT = (((1,), (1,)), ((), ()))
TN = (((0,), (0,)), ((), ()))
FAR = -1e30


def bf16_parts(value, count):
    parts = []
    for _ in range(count):
        part = float(np.asarray(value, dtype=jnp.bfloat16).astype(np.float64))
        parts.append(part)
        value = value - part
    return parts


def mm(a, b, dims=None):
    if dims is None:
        return jnp.dot(a, b, preferred_element_type=F32)
    return lax.dot_general(a, b, dims, preferred_element_type=F32)


def project(ext, grad_rows, w_query, w_out, w_kv, query, grad_att, key_value):
    slots = ext.shape[1]
    entries = key_value.shape[0] // (2 * slots)
    for b in range(2):
        feat = ext[3 * b + 4]
        query[b] = mm(feat, w_query[...]).astype(BF)
        grad_att[b] = mm(grad_rows[b], w_out[...], NT).astype(BF)
        key_value[b * entries * slots:(b * entries + 1) * slots] = mm(feat, w_kv[...]).astype(BF)


def attend(
    neighbours, counts, ext, ext_bias, grad_out, query_all, grad_att_all, key_value, part,
    w_kv, gathered, scores, grad_probs, probs_low, scores_low, scores_rest, grad_kv,
    attended_t, grad_query_t, bias_parts,
):
    lat = lax.axis_index("lat")
    lon = lax.axis_index("lon")
    columns = 2 * lax.axis_size("lon")

    def local_slot(block):
        row = lax.div(block, columns) - lat + 1
        column = lax.rem(lax.rem(block, columns) - 2 * lon + 1 + columns, columns)
        return jnp.clip(column, 0, 3) * 3 + jnp.clip(row, 0, 2)

    slots, chans = ext.shape[1:]
    width = chans // HEADS
    entries = counts.shape[2]
    keys_all = entries * slots
    root = math.sqrt(width)
    parts = bf16_parts(root, 3)
    log2e = math.log2(math.e) / root
    lane = lax.broadcasted_iota(jnp.int32, (slots, WINDOW), 1)
    row = lax.broadcasted_iota(jnp.int32, (slots, WINDOW), 0)
    place_row = lax.broadcasted_iota(jnp.int32, (HEADS, WINDOW), 0)
    place_lane = lax.broadcasted_iota(jnp.int32, (HEADS, WINDOW), 1)
    pick_row = lax.broadcasted_iota(jnp.int32, (2 * HEADS, PAIR * slots), 0)
    pick_lane = lax.broadcasted_iota(jnp.int32, (2 * HEADS, PAIR * slots), 1)
    all_picks = []
    for b in range(2):
        picks = [local_slot(neighbours[0, b, e]) for e in range(entries)]
        all_picks.append(picks)
        query = query_all[b]
        grad_att = grad_att_all[b]
        gathered[b, 0:slots, :] = ext[3 * b + 4]
        for e in range(1, entries):
            gathered[b, e * slots:(e + 1) * slots, :] = ext[picks[e]]
        rest = pl.ds(b * keys_all + slots, keys_all - slots)
        key_value[rest, :] = mm(gathered[b, slots:], w_kv[...]).astype(BF)
        kv = key_value[pl.ds(b * keys_all, keys_all), :]
        bias_row = jnp.concatenate([ext_bias[picks[e]] for e in range(entries)], axis=1)
        bias_rows = jnp.zeros((2 * HEADS, keys_all), F32)
        for w in range(2):
            lo = w * (chans - WINDOW)
            first = PAIR * w
            spare = PAIR * width if w == 0 else 0
            region = (lane < PAIR * width) if w == 0 else (lane >= WINDOW - PAIR * width)
            place = jnp.zeros((HEADS, WINDOW), F32)
            for hh in range(PAIR):
                start = spare + 3 * hh
                place = jnp.where(
                    (place_row == first + hh) & (place_lane >= start) & (place_lane < start + 3), 1.0, place
                )
            bias_cols = mm(bias_row, place, TN)
            key_aug = []
            for e in range(entries):
                cols = bias_cols[e * slots:(e + 1) * slots]
                cols = jnp.where((lane == spare + 3 * PAIR) & (row >= counts[0, b, e]), FAR, cols)
                piece = kv[e * slots:(e + 1) * slots, lo:lo + WINDOW]
                key_aug.append(jnp.where(region, piece.astype(F32), cols).astype(BF))
            key_aug = jnp.concatenate(key_aug, axis=0)
            value_win = kv[:, chans + lo:chans + lo + WINDOW]
            query_win = query[:, lo:lo + WINDOW].astype(F32)
            grad_win = grad_att[:, lo:lo + WINDOW].astype(F32)
            query_aug, grad_aug = [], []
            for hh in range(PAIR):
                inside = (lane >= (first + hh) * width - lo) & (lane < (first + hh + 1) * width - lo)
                const = jnp.where(lane == spare + 3 * PAIR, 1.0, 0.0)
                for t in range(3):
                    const = jnp.where(lane == spare + 3 * hh + t, parts[t], const)
                query_aug.append(jnp.where(inside, query_win, const).astype(BF))
                grad_aug.append(jnp.where(inside, grad_win, 0.0).astype(BF))
            query_aug = jnp.concatenate(query_aug, axis=0)
            grad_aug = jnp.concatenate(grad_aug, axis=0)
            scores[...] = mm(key_aug, query_aug, NT)
            grad_probs[...] = mm(value_win, grad_aug, NT)
            for hh in range(PAIR):
                cut = pl.ds(hh * slots, slots)
                logits = scores[:, cut]
                powers = jnp.exp2((logits - jnp.max(logits, axis=0, keepdims=True)) * log2e)
                probs = powers * (1.0 / jnp.sum(powers, axis=0, keepdims=True))
                probs_low[:, cut] = probs.astype(BF)
                grads = grad_probs[:, cut]
                centre = jnp.sum(probs * grads, axis=0, keepdims=True)
                full = probs * (grads - centre)
                high = full.astype(BF)
                scores_low[:, cut] = high
                scores_rest[:, cut] = (full - high.astype(F32)).astype(BF)
            value_grad = mm(probs_low[...], grad_aug)
            key_grad = mm(scores_low[...], query_aug)
            chosen = jnp.where(pick_lane // slots + first == pick_row, 1.0, 0.0).astype(BF)
            bias_rows = bias_rows + mm(chosen, scores_low[...], NT) + mm(chosen, scores_rest[...], NT)
            scale = 1.0 / root
            base = b * keys_all
            rows = pl.ds(base, keys_all)
            half = WINDOW // 2
            edge = PAIR * width - half
            low_lane = lane[0:1, 0:half]
            if w == 0:
                grad_kv[rows, 0:half] = (key_grad[:, 0:half] * scale).astype(BF)
                grad_kv[rows, chans:chans + half] = value_grad[:, 0:half].astype(BF)
                saved_key, saved_value = key_grad[:, half:], value_grad[:, half:]
            else:
                middle = jnp.where(low_lane < edge, saved_key, key_grad[:, 0:half]) * scale
                grad_kv[rows, half:2 * half] = middle.astype(BF)
                grad_kv[rows, 2 * half:3 * half] = (key_grad[:, half:] * scale).astype(BF)
                middle = saved_value + value_grad[:, 0:half]
                grad_kv[rows, chans + half:chans + 2 * half] = middle.astype(BF)
                grad_kv[rows, chans + 2 * half:chans + 3 * half] = value_grad[:, half:].astype(BF)
            for pair in range(2):
                head = first + 2 * pair
                cut = pl.ds(2 * pair * slots, 2 * slots)
                value_rows = kv[:, chans + head * width:chans + (head + 2) * width]
                key_rows = kv[:, head * width:(head + 2) * width]
                both = mm(value_rows, probs_low[:, cut], TN)
                attended_t[head * width:(head + 1) * width, b * slots:(b + 1) * slots] = both[:width, :slots].astype(BF)
                attended_t[(head + 1) * width:(head + 2) * width, b * slots:(b + 1) * slots] = both[width:, slots:].astype(BF)
                both = mm(key_rows, scores_low[:, cut], TN) * scale
                grad_query_t[head * width:(head + 1) * width, b * slots:(b + 1) * slots] = both[:width, :slots].astype(BF)
                grad_query_t[(head + 1) * width:(head + 2) * width, b * slots:(b + 1) * slots] = both[width:, slots:].astype(BF)
        for e in range(entries):
            bias_parts[b, e] = bias_rows[:HEADS, e * slots:(e + 1) * slots]
    grad_query = jnp.transpose(grad_query_t[...].astype(F32)).astype(BF)
    feat_both = jnp.concatenate([ext[4], ext[7]], axis=0)
    grad_both = grad_out[...].reshape(2 * slots, chans)
    piece = chans // ROWS

    def put(index, value):
        part[index * piece:(index + 1) * piece] = value.astype(BF).reshape(piece, ROWS, chans)

    put(0, mm(feat_both, grad_query, TN))
    put(3, mm(attended_t[...], grad_both))
    weight_kv = mm(gathered[...].reshape(2 * keys_all, chans), grad_kv[...], TN)
    put(1, weight_kv[:, :chans])
    put(2, weight_kv[:, chans:])
    return all_picks, grad_query


def scatter(all_picks, grad_query, w_query, w_kv, grad_kv, bias_parts, feat_parts, halo, own, bias_sum):
    slots, chans = halo.shape[1:]
    entries = len(all_picks[0])
    keys_all = entries * slots
    for b in range(2):
        feat_parts[b] = mm(grad_kv[pl.ds(b * keys_all, keys_all), :], w_kv[...], NT)
    query_part = mm(grad_query, w_query[...], NT)
    for slot in range(halo.shape[0]):
        column = slot // 3
        total, bias_total = None, None
        for b in range(2):
            if column - b not in (0, 1, 2):
                continue
            for e in range(1, entries):
                hit = all_picks[b][e] == slot
                piece = jnp.where(hit, feat_parts[b, e * slots:(e + 1) * slots], 0.0)
                total = piece if total is None else total + piece
                piece = jnp.where(hit, bias_parts[b, e], 0.0)
                bias_total = piece if bias_total is None else bias_total + piece
        if slot in (4, 7):
            b = column - 1
            own[b] = total + (feat_parts[b, 0:slots] + query_part[b * slots:(b + 1) * slots])
            bias_total = bias_total + bias_parts[b, 0]
        else:
            halo[slot] = total.astype(BF)
        bias_sum[slot] = bias_total


MESH = pl.DeviceIdType.MESH
NXY = 16
NZ = 8
NPEER = NXY + NZ
ROWS = 32


def remote(src, dst, send_sem, recv_sem, device):
    return pltpu.make_async_remote_copy(
        src_ref=src, dst_ref=dst, send_sem=send_sem, recv_sem=recv_sem,
        device_id=device, device_id_type=MESH,
    )


def layer_kernel(
    neighbours, counts, feat, key_bias, grad_out, w_query_hbm, w_key_hbm, w_value_hbm, w_out_hbm,
    out, grad_feat, grad_bias,
    ext, near_bias, ext_bias, grad_rows, w_query, w_out, query, grad_att, key_value,
    part, halo, own, bias_sum, feat_parts, bias_parts, w_kv, gathered, scores, grad_probs, probs_low,
    scores_low, scores_rest, grad_kv, attended_t, grad_query_t, from_core, half, from_first, mine, from_second, total,
    core_send, core_recv, first_send, first_recv, second_send, second_recv,
    third_send, third_recv, fourth_send, fourth_recv,
    side, side_bias, rows_out, rows_bias, edge, edge_bias,
    side_send, side_recv, edge_send, edge_recv,
    local_sem, wide_send, wide_recv, near_send, near_recv,
):
    lat = lax.axis_index("lat")
    lon = lax.axis_index("lon")
    core = lon % 2
    z = (lon // 2) % NZ
    x_lo = lon // (2 * NZ)
    x_hi = lat // 4
    y = lat % 4
    xy = (x_hi * 2 + x_lo) * 4 + y
    partner = (lat, lon + 1 - 2 * core)
    nlat = lax.axis_size("lat")
    nlon = lax.axis_size("lon")
    east = (lat, (lon + 1) % nlon)
    west = (lat, (lon + nlon - 1) % nlon)
    north = (lat - 1, lon)
    south = (lat + 1, lon)
    base = core * NPEER
    other = (1 - core) * NPEER

    off_lon = (lon + nlon - 1 + 2 * core) % nlon
    off = (lat, off_lon)
    seam = nlat // 2

    def plane_peer(index):
        x = index // 4
        return ((x // 2) * 4 + index % 4, (x % 2) * (2 * NZ) + z * 2 + core)

    def depth_peer(index):
        return (lat, x_lo * (2 * NZ) + index * 2 + core)

    barrier = pltpu.get_barrier_semaphore()

    def greet(device):
        pl.semaphore_signal(barrier, inc=1, device_id=device, device_id_type=MESH)

    greet(partner)
    greet(off)

    @pl.when(lat > 0)
    def _():
        greet((lat - 1, off_lon))
        greet((lat - 1, partner[1]))

    @pl.when(lat < nlat - 1)
    def _():
        greet((lat + 1, off_lon))
        greet((lat + 1, partner[1]))

    @pl.loop(1, NXY)
    def _(step):
        greet(plane_peer((xy + step) % NXY))

    @pl.loop(1, NZ)
    def _(step):
        greet(depth_peer((z + step) % NZ))

    chans = feat.shape[3]
    loads = [
        (feat.at[0, 0], ext.at[4]),
        (feat.at[0, 1], ext.at[7]),
        (w_query_hbm, w_query),
        (grad_out.at[0], grad_rows),
        (w_out_hbm, w_out),
        (w_key_hbm, w_kv.at[:, pl.ds(0, chans)]),
        (w_value_hbm, w_kv.at[:, pl.ds(chans, chans)]),
    ]
    loads = [pltpu.make_async_copy(src, dst, local_sem.at[i]) for i, (src, dst) in enumerate(loads)]
    for load in loads:
        load.start()
    near_bias[4] = key_bias[...]
    loads[0].wait()
    loads[1].wait()
    inner = jnp.minimum(lat, 1) + jnp.minimum(nlat - 1 - lat, 1)
    pl.semaphore_wait(barrier, NPEER + 2 * inner)

    s_off = 4 + 3 * core
    s_in = 7 - 3 * core
    t_off = 9 - 9 * core
    t_in = 9 * core
    b_off = 2 - 2 * core
    b_in = 2 * core

    def wide_copy(source, target, order, device):
        return remote(ext.at[source], ext.at[target], wide_send.at[order], wide_recv.at[target], device)

    def near_copy(target, order, device):
        return remote(near_bias.at[4], near_bias.at[target], near_send.at[order], near_recv.at[target], device)

    def to_row(up):
        device = north if up else south
        corner = (lat - 1, off_lon) if up else (lat + 1, off_lon)
        step, row, order = (1, 2, 0) if up else (-1, 0, 3)
        wide_copy(s_in, s_in + step, order, device).start()
        wide_copy(s_off, t_off + row, order + 1, corner).start()
        wide_copy(s_off, s_off + step, order + 2, device).start()
        near_copy(3 * row + 1, order, device).start()
        near_copy(3 * row + b_off, order + 1, corner).start()
        near_copy(3 * row + b_in, order + 2, (corner[0], partner[1])).start()

    def wait_row(up):
        step, row, order = (1, 2, 0) if up else (-1, 0, 3)
        for k in range(3):
            wide_copy(4, 4, order + k, partner).wait_send()
            near_copy(4, order + k, partner).wait_send()

    wide_copy(s_in, t_in + 1, 6, partner).start()
    wide_copy(s_off, t_off + 1, 7, off).start()
    near_copy(3 + b_in, 6, partner).start()
    near_copy(3 + b_off, 7, off).start()
    pl.when(lat == seam - 1)(lambda: to_row(False))
    pl.when(lat > 0)(lambda: to_row(True))
    pl.when((lat < nlat - 1) & (lat != seam - 1))(lambda: to_row(False))

    for load in loads[2:]:
        load.wait()
    project(ext, grad_rows, w_query, w_out, w_kv, query, grad_att, key_value)

    def pass_on(row, order):
        slot = s_in - 1 + row
        wide_copy(slot, slot, order, partner).wait_recv()
        wide_copy(slot, t_in + row, order, partner).start()

    pl.when(lat == seam - 1)(lambda: pass_on(0, 8))
    pl.when(lat < nlat - 1)(lambda: pass_on(2, 9))
    pl.when((lat > 0) & (lat != seam - 1))(lambda: pass_on(0, 8))

    def arrived(row):
        for slot in (s_off - 1 + row, t_in + row, t_off + row):
            wide_copy(slot, slot, 0, partner).wait_recv()
        for column in range(3):
            near_copy(3 * row + column, 0, partner).wait_recv()

    for slot in (t_in + 1, t_off + 1):
        wide_copy(slot, slot, 0, partner).wait_recv()
    for column in (0, 2):
        near_copy(3 + column, 0, partner).wait_recv()
    pl.when(lat > 0)(lambda: arrived(0))
    pl.when(lat < nlat - 1)(lambda: arrived(2))
    heads = ext_bias.shape[1]
    for row in range(3):
        west_bias = near_bias[3 * row].astype(F32)
        own_bias = near_bias[3 * row + 1].astype(F32)
        east_bias = near_bias[3 * row + 2].astype(F32)
        ext_bias[row] = west_bias[heads:]
        ext_bias[3 + row] = own_bias[:heads]
        ext_bias[6 + row] = own_bias[heads:]
        ext_bias[9 + row] = east_bias[:heads]

    all_picks, grad_query = attend(
        neighbours, counts, ext, ext_bias, grad_rows, query, grad_att, key_value, part,
        w_kv, gathered, scores, grad_probs, probs_low, scores_low, scores_rest, grad_kv,
        attended_t, grad_query_t, bias_parts,
    )

    def side_copies(index):
        device = (west, east)[index]
        source = pl.ds(9 * index, 3)
        return (
            remote(halo.at[source], side.at[1 - index], side_send.at[2 * index], side_recv.at[2 - 2 * index], device),
            remote(bias_sum.at[source], side_bias.at[1 - index], side_send.at[2 * index + 1], side_recv.at[3 - 2 * index], device),
        )

    def edge_copies(index):
        device = (north, south)[index]
        return (
            remote(rows_out.at[index], edge.at[1 - index], edge_send.at[2 * index], edge_recv.at[2 - 2 * index], device),
            remote(rows_bias.at[index], edge_bias.at[1 - index], edge_send.at[2 * index + 1], edge_recv.at[3 - 2 * index], device),
        )

    def each(copies, what):
        for copy in copies:
            getattr(copy, what)()

    def chunks(step):
        return ((xy + 2 * step + 1) % NXY, (xy + 2 * step + 2) % NXY, NXY + (z + step + 1) % NZ)

    def core_copy(chunk):
        return remote(part.at[other + chunk], from_core.at[chunk], core_send.at[chunk], core_recv.at[chunk], partner)

    def first_copy(chunk, device, slot):
        return remote(half.at[chunk], from_first.at[slot], first_send.at[chunk], first_recv.at[slot], device)

    @pl.loop(0, NZ)
    def _(step):
        for chunk in chunks(step):
            core_copy(chunk).start()

    @pl.loop(0, NZ)
    def _(step):
        a, b, c = chunks(step)
        for chunk in (a, b, c):
            core_copy(chunk).wait_recv()
            half[chunk] = (part[base + chunk].astype(jnp.float32) + from_core[chunk].astype(jnp.float32)).astype(jnp.bfloat16)
        first_copy(a, plane_peer(a), xy).start()

        @pl.when(step < NZ - 1)
        def _():
            first_copy(b, plane_peer(b), xy).start()
            first_copy(c, depth_peer(c - NXY), NXY + z).start()

    scatter(all_picks, grad_query, w_query, w_kv, grad_kv, bias_parts, feat_parts, halo, own, bias_sum)
    each(side_copies(0), "start")
    each(side_copies(1), "start")

    each(side_copies(0), "wait_recv")
    each(side_copies(1), "wait_recv")
    for index in range(2):
        for j in range(2):
            slot = 3 * j + 3 + 2 * index
            rows_out[index, j] = (halo[slot].astype(F32) + side[j, 2 * index].astype(F32)).astype(BF)
            rows_bias[index, j] = bias_sum[slot] + side_bias[j, 2 * index]
    pl.when(lat > 0)(lambda: each(edge_copies(0), "start"))
    pl.when(lat < nlat - 1)(lambda: each(edge_copies(1), "start"))

    from_first[xy] = half[xy]
    from_first[NXY + z] = half[NXY + z]

    def wait_first(step, index):
        slot = index
        first_copy(slot, partner, slot).wait_recv()

    @pl.loop(1, NZ)
    def _(step):
        wait_first(step, NXY + (z - step + NZ) % NZ)

    mine[1] = jnp.sum(from_first[NXY:NPEER].astype(jnp.float32), axis=0).astype(jnp.bfloat16)

    def second_b(index):
        return remote(mine.at[1], from_second.at[xy], second_send.at[index], second_recv.at[xy], plane_peer(index))

    def second_a(index):
        return remote(mine.at[0], from_second.at[NXY + z], second_send.at[NXY + index], second_recv.at[NXY + z], depth_peer(index))

    @pl.loop(1, NXY)
    def _(step):
        second_b((xy + step) % NXY).start()

    @pl.loop(1, NXY)
    def _(step):
        wait_first(step, (xy - step + NXY) % NXY)

    mine[0] = jnp.sum(from_first[0:NXY].astype(jnp.float32), axis=0).astype(jnp.bfloat16)

    @pl.loop(1, NZ)
    def _(step):
        second_a((z + step) % NZ).start()

    from_second[xy] = mine[1]
    from_second[NXY + z] = mine[0]

    def wait_second(slot):
        remote(mine.at[0], from_second.at[slot], second_send.at[slot], second_recv.at[slot], partner).wait_recv()

    def third_copy(which, slot, index, device):
        return remote(total.at[which], out.at[slot], third_send.at[index], third_recv.at[slot], device)

    def fourth_copy(slot):
        return remote(out.at[slot], out.at[slot], fourth_send.at[slot], fourth_recv.at[slot], partner)

    @pl.loop(1, NXY)
    def _(step):
        wait_second((xy - step + NXY) % NXY)

    total[1] = jnp.sum(from_second[0:NXY].astype(jnp.float32), axis=0).astype(jnp.bfloat16)

    @pl.loop(1, NZ)
    def _(step):
        index = (z + step) % NZ
        third_copy(1, base + NXY + z, NXY + index, depth_peer(index)).start()

    out[base + NXY + z] = total[1]
    fourth_copy(base + NXY + z).start()

    @pl.loop(1, NZ)
    def _(step):
        wait_second(NXY + (z - step + NZ) % NZ)

    total[0] = jnp.sum(from_second[NXY:NPEER].astype(jnp.float32), axis=0).astype(jnp.bfloat16)

    @pl.loop(1, NXY)
    def _(step):
        index = (xy + step) % NXY
        third_copy(0, base + xy, index, plane_peer(index)).start()

    out[base + xy] = total[0]
    fourth_copy(base + xy).start()

    def forward(slot):
        third_copy(0, slot, 0, partner).wait_recv()
        fourth_copy(slot).start()

    @pl.loop(1, NZ)
    def _(step):
        forward(base + NXY + (z - step + NZ) % NZ)

    @pl.loop(1, NXY)
    def _(step):
        forward(base + (xy - step + NXY) % NXY)

    @pl.loop(0, NPEER)
    def _(chunk):
        core_copy(chunk).wait_send()
        fourth_copy(base + chunk).wait_send()
        fourth_copy(other + chunk).wait_recv()

    @pl.loop(1, NXY)
    def _(step):
        index = (xy + step) % NXY
        first_copy(index, partner, index).wait_send()
        second_b(index).wait_send()
        third_copy(0, base + xy, index, partner).wait_send()

    @pl.loop(1, NZ)
    def _(step):
        index = (z + step) % NZ
        first_copy(NXY + index, partner, index).wait_send()
        second_a(index).wait_send()
        third_copy(1, base + xy, NXY + index, partner).wait_send()

    each(side_copies(0), "wait_send")
    each(side_copies(1), "wait_send")

    @pl.when(lat == 0)
    def _():
        edge[0] = jnp.zeros_like(edge[0])
        edge_bias[0] = jnp.zeros_like(edge_bias[0])

    @pl.when(lat == nlat - 1)
    def _():
        edge[1] = jnp.zeros_like(edge[1])
        edge_bias[1] = jnp.zeros_like(edge_bias[1])

    @pl.when(lat > 0)
    def _():
        each(edge_copies(0), "wait_send")
        each(edge_copies(1), "wait_recv")

    @pl.when(lat < nlat - 1)
    def _():
        each(edge_copies(1), "wait_send")
        each(edge_copies(0), "wait_recv")

    for j in range(2):
        total_grad = own[j] + side[j, 1].astype(F32) + (edge[0, j].astype(F32) + edge[1, j].astype(F32))
        grad_feat[j] = total_grad.astype(BF)
        grad_bias[j] = bias_sum[3 * j + 4] + side_bias[j, 1] + (edge_bias[0, j] + edge_bias[1, j])

    wide_copy(4, 4, 6, partner).wait_send()
    wide_copy(4, 4, 7, partner).wait_send()
    near_copy(4, 6, partner).wait_send()
    near_copy(4, 7, partner).wait_send()

    @pl.when(lat > 0)
    def _():
        wait_row(True)
        wide_copy(4, 4, 8, partner).wait_send()

    @pl.when(lat < nlat - 1)
    def _():
        wait_row(False)
        wide_copy(4, 4, 9, partner).wait_send()


def layer_call(neighbours, counts, feat, key_bias, grad_out, w_query, w_key, w_value, w_out):
    _, _, slots, chans = feat.shape
    heads = key_bias.shape[0] // 2
    blocks = 12
    entries = counts.shape[2]
    keys_all = entries * slots
    vmem = pl.BlockSpec(memory_space=pltpu.VMEM)
    smem = pl.BlockSpec(memory_space=pltpu.SMEM)
    hbm = pl.BlockSpec(memory_space=pl.ANY)
    low = lambda *shape: pltpu.VMEM(shape, BF)
    wide = lambda *shape: pltpu.VMEM(shape, F32)
    dma = pltpu.SemaphoreType.DMA
    return pl.pallas_call(
        layer_kernel,
        out_shape=[
            jax.ShapeDtypeStruct((2 * NPEER, ROWS, chans), BF),
            jax.ShapeDtypeStruct((2, slots, chans), BF),
            jax.ShapeDtypeStruct((2, heads, slots), F32),
        ],
        in_specs=[smem] * 2 + [hbm, vmem] + [hbm] * 5,
        out_specs=[vmem] * 3,
        scratch_shapes=[
            low(blocks, slots, chans),
            low(9, 2 * heads, slots),
            wide(blocks, heads, slots),
            low(2, slots, chans),
            low(chans, chans),
            low(chans, chans),
            low(2, slots, chans),
            low(2, slots, chans),
            low(2 * keys_all, 2 * chans),
            low(2 * NPEER, ROWS, chans),
            low(blocks, slots, chans),
            wide(2, slots, chans),
            wide(blocks, heads, slots),
            wide(2, keys_all, chans),
            wide(2, entries, heads, slots),
            low(chans, 2 * chans),
            low(2, keys_all, chans),
            wide(keys_all, PAIR * slots),
            wide(keys_all, PAIR * slots),
            low(keys_all, PAIR * slots),
            low(keys_all, PAIR * slots),
            low(keys_all, PAIR * slots),
            low(2 * keys_all, 2 * chans),
            low(chans, 2 * slots),
            low(chans, 2 * slots),
            low(NPEER, ROWS, chans),
            low(NPEER, ROWS, chans),
            low(NPEER, ROWS, chans),
            low(2, ROWS, chans),
            low(NPEER, ROWS, chans),
            low(2, ROWS, chans),
        ]
        + [dma((NPEER,))] * 7 + [dma((2 * NPEER,))] * 3
        + [
            low(2, 3, slots, chans),
            wide(2, 3, heads, slots),
            low(2, 2, slots, chans),
            wide(2, 2, heads, slots),
            low(2, 2, slots, chans),
            wide(2, 2, heads, slots),
        ]
        + [dma((4,))] * 4
        + [dma((7,)), dma((10,)), dma((12,)), dma((8,)), dma((9,))],
        compiler_params=pltpu.CompilerParams(collective_id=0, has_side_effects=True, vmem_limit_bytes=48 << 20),
        name="layer_backward",
    )(neighbours, counts, feat, key_bias, grad_out, w_query, w_key, w_value, w_out)


def per_device(
    features, w_query, w_key, w_value, w_out, key_bias, neighbours, key_counts, grad_out
):
    brows, bcols, slots, chans = features.shape
    heads = key_bias.shape[2]
    low, grad_features, grad_bias = layer_call(
        neighbours, key_counts, features, key_bias.reshape(bcols * heads, slots), grad_out,
        w_query, w_key, w_value, w_out,
    )
    cells = lax.axis_size("lat") * lax.axis_size("lon") * brows * bcols * slots
    summed = low.astype(F32).reshape(4, chans, chans) * float(cells) ** (-0.5)
    return (
        grad_features.reshape(brows, bcols, slots, chans),
        grad_bias.reshape(brows, bcols, heads, slots),
        summed[0],
        summed[1],
        summed[2],
        summed[3],
    )


def solution(mesh):
    placed = (
        P("lat", "lon", None, None),
        P(),
        P(),
        P(),
        P(),
        P("lat", "lon", None, None),
        P("lat", "lon", None),
        P("lat", "lon", None),
        P("lat", "lon", None, None),
    )
    return jax.shard_map(
        per_device,
        mesh=mesh,
        in_specs=placed,
        out_specs=(P("lat", "lon", None, None), P("lat", "lon", None, None), P(), P(), P(), P()),
        check_vma=False,
    )
```

```python
import functools
import math

import jax
import jax.numpy as jnp
import numpy as np
from jax import lax
from jax.experimental import pallas as pl
from jax.experimental.pallas import tpu as pltpu
from jax.sharding import PartitionSpec as P

BF = jnp.bfloat16
F32 = jnp.float32
HEADS = 8
PAIR = 4
WINDOW = 256
NT = (((1,), (1,)), ((), ()))
TN = (((0,), (0,)), ((), ()))
FAR = -1e30


def bf16_parts(value, count):
    parts = []
    for _ in range(count):
        part = float(np.asarray(value, dtype=jnp.bfloat16).astype(np.float64))
        parts.append(part)
        value = value - part
    return parts


def mm(a, b, dims=None):
    if dims is None:
        return jnp.dot(a, b, preferred_element_type=F32)
    return lax.dot_general(a, b, dims, preferred_element_type=F32)


def project(ext, grad_rows, w_query, w_out, w_kv, query, grad_att, key_value):
    slots = ext.shape[1]
    entries = key_value.shape[0] // (2 * slots)
    for b in range(2):
        feat = ext[3 * b + 4]
        query[b] = mm(feat, w_query[...]).astype(BF)
        grad_att[b] = mm(grad_rows[b], w_out[...], NT).astype(BF)
        key_value[b * entries * slots:(b * entries + 1) * slots] = mm(feat, w_kv[...]).astype(BF)


def attend(
    neighbours, counts, ext, ext_bias, grad_out, query_all, grad_att_all, key_value, part,
    w_kv, gathered, scores, grad_probs, probs_low, scores_low, scores_rest, grad_kv,
    attended_t, grad_query_t, bias_parts,
):
    lat = lax.axis_index("lat")
    lon = lax.axis_index("lon")
    columns = 2 * lax.axis_size("lon")

    def local_slot(block):
        row = lax.div(block, columns) - lat + 1
        column = lax.rem(lax.rem(block, columns) - 2 * lon + 1 + columns, columns)
        return jnp.clip(column, 0, 3) * 3 + jnp.clip(row, 0, 2)

    slots, chans = ext.shape[1:]
    width = chans // HEADS
    entries = counts.shape[2]
    keys_all = entries * slots
    root = math.sqrt(width)
    parts = bf16_parts(root, 3)
    log2e = math.log2(math.e) / root
    lane = lax.broadcasted_iota(jnp.int32, (slots, WINDOW), 1)
    row = lax.broadcasted_iota(jnp.int32, (slots, WINDOW), 0)
    place_row = lax.broadcasted_iota(jnp.int32, (HEADS, WINDOW), 0)
    place_lane = lax.broadcasted_iota(jnp.int32, (HEADS, WINDOW), 1)
    pick_row = lax.broadcasted_iota(jnp.int32, (2 * HEADS, PAIR * slots), 0)
    pick_lane = lax.broadcasted_iota(jnp.int32, (2 * HEADS, PAIR * slots), 1)
    all_picks = []
    for b in range(2):
        picks = [local_slot(neighbours[0, b, e]) for e in range(entries)]
        all_picks.append(picks)
        query = query_all[b]
        grad_att = grad_att_all[b]
        gathered[b, 0:slots, :] = ext[3 * b + 4]
        for e in range(1, entries):
            gathered[b, e * slots:(e + 1) * slots, :] = ext[picks[e]]
        rest = pl.ds(b * keys_all + slots, keys_all - slots)
        key_value[rest, :] = mm(gathered[b, slots:], w_kv[...]).astype(BF)
        kv = key_value[pl.ds(b * keys_all, keys_all), :]
        bias_row = jnp.concatenate([ext_bias[picks[e]] for e in range(entries)], axis=1)
        bias_rows = jnp.zeros((2 * HEADS, keys_all), F32)
        for w in range(2):
            lo = w * (chans - WINDOW)
            first = PAIR * w
            spare = PAIR * width if w == 0 else 0
            region = (lane < PAIR * width) if w == 0 else (lane >= WINDOW - PAIR * width)
            place = jnp.zeros((HEADS, WINDOW), F32)
            for hh in range(PAIR):
                start = spare + 3 * hh
                place = jnp.where(
                    (place_row == first + hh) & (place_lane >= start) & (place_lane < start + 3), 1.0, place
                )
            bias_cols = mm(bias_row, place, TN)
            key_aug = []
            for e in range(entries):
                cols = bias_cols[e * slots:(e + 1) * slots]
                cols = jnp.where((lane == spare + 3 * PAIR) & (row >= counts[0, b, e]), FAR, cols)
                piece = kv[e * slots:(e + 1) * slots, lo:lo + WINDOW]
                key_aug.append(jnp.where(region, piece.astype(F32), cols).astype(BF))
            key_aug = jnp.concatenate(key_aug, axis=0)
            value_win = kv[:, chans + lo:chans + lo + WINDOW]
            query_win = query[:, lo:lo + WINDOW].astype(F32)
            grad_win = grad_att[:, lo:lo + WINDOW].astype(F32)
            query_aug, grad_aug = [], []
            for hh in range(PAIR):
                inside = (lane >= (first + hh) * width - lo) & (lane < (first + hh + 1) * width - lo)
                const = jnp.where(lane == spare + 3 * PAIR, 1.0, 0.0)
                for t in range(3):
                    const = jnp.where(lane == spare + 3 * hh + t, parts[t], const)
                query_aug.append(jnp.where(inside, query_win, const).astype(BF))
                grad_aug.append(jnp.where(inside, grad_win, 0.0).astype(BF))
            query_aug = jnp.concatenate(query_aug, axis=0)
            grad_aug = jnp.concatenate(grad_aug, axis=0)
            scores[...] = mm(key_aug, query_aug, NT)
            grad_probs[...] = mm(value_win, grad_aug, NT)
            for hh in range(PAIR):
                cut = pl.ds(hh * slots, slots)
                logits = scores[:, cut]
                powers = jnp.exp2((logits - jnp.max(logits, axis=0, keepdims=True)) * log2e)
                probs = powers * (1.0 / jnp.sum(powers, axis=0, keepdims=True))
                probs_low[:, cut] = probs.astype(BF)
                grads = grad_probs[:, cut]
                centre = jnp.sum(probs * grads, axis=0, keepdims=True)
                full = probs * (grads - centre)
                high = full.astype(BF)
                scores_low[:, cut] = high
                scores_rest[:, cut] = (full - high.astype(F32)).astype(BF)
            value_grad = mm(probs_low[...], grad_aug)
            key_grad = mm(scores_low[...], query_aug)
            chosen = jnp.where(pick_lane // slots + first == pick_row, 1.0, 0.0).astype(BF)
            bias_rows = bias_rows + mm(chosen, scores_low[...], NT) + mm(chosen, scores_rest[...], NT)
            scale = 1.0 / root
            base = b * keys_all
            rows = pl.ds(base, keys_all)
            half = WINDOW // 2
            edge = PAIR * width - half
            low_lane = lane[0:1, 0:half]
            if w == 0:
                grad_kv[rows, 0:half] = (key_grad[:, 0:half] * scale).astype(BF)
                grad_kv[rows, chans:chans + half] = value_grad[:, 0:half].astype(BF)
                saved_key, saved_value = key_grad[:, half:], value_grad[:, half:]
            else:
                middle = jnp.where(low_lane < edge, saved_key, key_grad[:, 0:half]) * scale
                grad_kv[rows, half:2 * half] = middle.astype(BF)
                grad_kv[rows, 2 * half:3 * half] = (key_grad[:, half:] * scale).astype(BF)
                middle = saved_value + value_grad[:, 0:half]
                grad_kv[rows, chans + half:chans + 2 * half] = middle.astype(BF)
                grad_kv[rows, chans + 2 * half:chans + 3 * half] = value_grad[:, half:].astype(BF)
            for pair in range(2):
                head = first + 2 * pair
                cut = pl.ds(2 * pair * slots, 2 * slots)
                value_rows = kv[:, chans + head * width:chans + (head + 2) * width]
                key_rows = kv[:, head * width:(head + 2) * width]
                both = mm(value_rows, probs_low[:, cut], TN)
                attended_t[head * width:(head + 1) * width, b * slots:(b + 1) * slots] = both[:width, :slots].astype(BF)
                attended_t[(head + 1) * width:(head + 2) * width, b * slots:(b + 1) * slots] = both[width:, slots:].astype(BF)
                both = mm(key_rows, scores_low[:, cut], TN) * scale
                grad_query_t[head * width:(head + 1) * width, b * slots:(b + 1) * slots] = both[:width, :slots].astype(BF)
                grad_query_t[(head + 1) * width:(head + 2) * width, b * slots:(b + 1) * slots] = both[width:, slots:].astype(BF)
        for e in range(entries):
            bias_parts[b, e] = bias_rows[:HEADS, e * slots:(e + 1) * slots]
    grad_query = jnp.transpose(grad_query_t[...].astype(F32)).astype(BF)
    feat_both = jnp.concatenate([ext[4], ext[7]], axis=0)
    grad_both = grad_out[...].reshape(2 * slots, chans)
    piece = chans // ROWS

    def put(index, value):
        part[index * piece:(index + 1) * piece] = value.astype(BF).reshape(piece, ROWS, chans)

    put(0, mm(feat_both, grad_query, TN))
    put(3, mm(attended_t[...], grad_both))
    weight_kv = mm(gathered[...].reshape(2 * keys_all, chans), grad_kv[...], TN)
    put(1, weight_kv[:, :chans])
    put(2, weight_kv[:, chans:])
    return all_picks, grad_query


def scatter(all_picks, grad_query, w_query, w_kv, grad_kv, bias_parts, feat_parts, halo, own, bias_sum):
    slots, chans = halo.shape[1:]
    entries = len(all_picks[0])
    keys_all = entries * slots
    for b in range(2):
        feat_parts[b] = mm(grad_kv[pl.ds(b * keys_all, keys_all), :], w_kv[...], NT)
    query_part = mm(grad_query, w_query[...], NT)
    for slot in range(halo.shape[0]):
        column = slot // 3
        total, bias_total = None, None
        for b in range(2):
            if column - b not in (0, 1, 2):
                continue
            for e in range(1, entries):
                hit = all_picks[b][e] == slot
                piece = jnp.where(hit, feat_parts[b, e * slots:(e + 1) * slots], 0.0)
                total = piece if total is None else total + piece
                piece = jnp.where(hit, bias_parts[b, e], 0.0)
                bias_total = piece if bias_total is None else bias_total + piece
        if slot in (4, 7):
            b = column - 1
            own[b] = total + (feat_parts[b, 0:slots] + query_part[b * slots:(b + 1) * slots])
            bias_total = bias_total + bias_parts[b, 0]
        else:
            halo[slot] = total.astype(BF)
        bias_sum[slot] = bias_total


MESH = pl.DeviceIdType.MESH
NXY = 16
NZ = 8
NPEER = NXY + NZ
ROWS = 32


def remote(src, dst, send_sem, recv_sem, device):
    return pltpu.make_async_remote_copy(
        src_ref=src, dst_ref=dst, send_sem=send_sem, recv_sem=recv_sem,
        device_id=device, device_id_type=MESH,
    )


def layer_kernel(
    neighbours_hbm, counts_hbm, feat, key_bias, grad_out, w_query_hbm, w_key_hbm, w_value_hbm, w_out_hbm,
    out, grad_feat, grad_bias,
    neighbours, counts, ext, near_bias, ext_bias, grad_rows, w_query, w_out, query, grad_att, key_value,
    part, halo, own, bias_sum, feat_parts, bias_parts, w_kv, gathered, scores, grad_probs, probs_low,
    scores_low, scores_rest, grad_kv, attended_t, grad_query_t,
    from_core, half, from_first, mine, from_second, total, summed,
    side, side_bias, rows_out, rows_bias, edge, edge_bias,
    local_sem, out_sem, wide_send, wide_recv, near_send, near_recv,
    core_send, core_recv, first_send, first_recv, second_send, second_recv,
    third_send, third_recv, fourth_send, fourth_recv, side_send, side_recv, edge_send, edge_recv,
):
    lat = lax.axis_index("lat")
    lon = lax.axis_index("lon")
    core = lon % 2
    z = (lon // 2) % NZ
    x_lo = lon // (2 * NZ)
    x_hi = lat // 4
    y = lat % 4
    xy = (x_hi * 2 + x_lo) * 4 + y
    partner = (lat, lon + 1 - 2 * core)
    nlat = lax.axis_size("lat")
    nlon = lax.axis_size("lon")
    east = (lat, (lon + 1) % nlon)
    west = (lat, (lon + nlon - 1) % nlon)
    north = (lat - 1, lon)
    south = (lat + 1, lon)
    base = core * NPEER
    other = (1 - core) * NPEER

    off_lon = (lon + nlon - 1 + 2 * core) % nlon
    off = (lat, off_lon)
    seam = nlat // 2

    def plane_peer(index):
        x = index // 4
        return ((x // 2) * 4 + index % 4, (x % 2) * (2 * NZ) + z * 2 + core)

    def depth_peer(index):
        return (lat, x_lo * (2 * NZ) + index * 2 + core)

    barrier = pltpu.get_barrier_semaphore()

    def greet(device):
        pl.semaphore_signal(barrier, inc=1, device_id=device, device_id_type=MESH)

    def settle(like, sem):
        pltpu.make_async_copy(like, like, sem).wait()

    chans = feat.shape[3]
    loads = [
        (feat.at[0, 0], ext.at[4], 0),
        (feat.at[0, 1], ext.at[7], 0),
        (w_query_hbm, w_query, 1),
        (grad_out.at[0], grad_rows, 2),
        (w_out_hbm, w_out, 3),
        (w_key_hbm, w_kv.at[:, pl.ds(0, chans)], 4),
        (w_value_hbm, w_kv.at[:, pl.ds(chans, chans)], 4),
        (neighbours_hbm, neighbours, 5),
        (counts_hbm, counts, 6),
    ]
    for src, dst, index in loads:
        pltpu.make_async_copy(src, dst, local_sem.at[index]).start()
    greet(partner)
    greet(off)

    @pl.when(lat > 0)
    def _():
        greet((lat - 1, off_lon))
        greet((lat - 1, partner[1]))

    @pl.when(lat < nlat - 1)
    def _():
        greet((lat + 1, off_lon))
        greet((lat + 1, partner[1]))

    @pl.loop(1, NXY)
    def _(step):
        greet(plane_peer((xy + step) % NXY))

    @pl.loop(1, NZ)
    def _(step):
        greet(depth_peer((z + step) % NZ))

    near_bias[4] = key_bias[...]
    settle(ext.at[pl.ds(0, 2)], local_sem.at[0])
    inner = jnp.minimum(lat, 1) + jnp.minimum(nlat - 1 - lat, 1)
    pl.semaphore_wait(barrier, NPEER + 2 * inner)

    s_off = 4 + 3 * core
    s_in = 7 - 3 * core
    t_off = 9 - 9 * core
    t_in = 9 * core
    b_off = 2 - 2 * core
    b_in = 2 * core

    def wide_copy(source, target, sent, landed, device):
        return remote(ext.at[source], ext.at[target], wide_send.at[sent], wide_recv.at[landed], device)

    def near_copy(target, sent, landed, device):
        return remote(near_bias.at[4], near_bias.at[target], near_send.at[sent], near_recv.at[landed], device)

    def to_row(up):
        device = north if up else south
        corner = (lat - 1, off_lon) if up else (lat + 1, off_lon)
        inside = (corner[0], partner[1])
        step, row, sent, landed = (1, 2, 1, 2) if up else (-1, 0, 2, 1)
        wide_copy(s_in, s_in + step, sent, landed, device).start()
        wide_copy(s_off, t_off + row, sent, landed + 2, corner).start()
        wide_copy(s_off, s_off + step, sent, landed + 2, device).start()
        near_copy(3 * row + 1, sent, landed, device).start()
        near_copy(3 * row + b_off, sent, landed, corner).start()
        near_copy(3 * row + b_in, sent, landed, inside).start()

    wide_copy(s_in, t_in + 1, 0, 0, partner).start()
    wide_copy(s_off, t_off + 1, 0, 0, off).start()
    near_copy(3 + b_in, 0, 0, partner).start()
    near_copy(3 + b_off, 0, 0, off).start()
    pl.when(lat == seam - 1)(lambda: to_row(False))
    pl.when(lat > 0)(lambda: to_row(True))
    pl.when((lat < nlat - 1) & (lat != seam - 1))(lambda: to_row(False))

    settle(w_query, local_sem.at[1])
    settle(grad_rows, local_sem.at[2])
    settle(w_out, local_sem.at[3])
    settle(w_kv, local_sem.at[4])
    settle(neighbours, local_sem.at[5])
    settle(counts, local_sem.at[6])
    project(ext, grad_rows, w_query, w_out, w_kv, query, grad_att, key_value)

    def pass_on(row):
        landed = 1 + row // 2
        slot = s_in - 1 + row
        settle(ext.at[slot], wide_recv.at[landed])
        wide_copy(slot, t_in + row, landed + 2, landed + 2, partner).start()

    def arrived(row):
        landed = 1 + row // 2
        settle(ext.at[pl.ds(0, 3)], wide_recv.at[landed + 2])
        settle(near_bias.at[pl.ds(0, 3)], near_recv.at[landed])

    pl.when(lat == seam - 1)(lambda: pass_on(0))
    pl.when(lat < nlat - 1)(lambda: pass_on(2))
    pl.when((lat > 0) & (lat != seam - 1))(lambda: pass_on(0))
    settle(ext.at[pl.ds(0, 2)], wide_recv.at[0])
    settle(near_bias.at[pl.ds(0, 2)], near_recv.at[0])
    pl.when(lat > 0)(lambda: arrived(0))
    pl.when(lat < nlat - 1)(lambda: arrived(2))
    heads = ext_bias.shape[1]
    for row in range(3):
        west_bias = near_bias[3 * row].astype(F32)
        own_bias = near_bias[3 * row + 1].astype(F32)
        east_bias = near_bias[3 * row + 2].astype(F32)
        ext_bias[row] = west_bias[heads:]
        ext_bias[3 + row] = own_bias[:heads]
        ext_bias[6 + row] = own_bias[heads:]
        ext_bias[9 + row] = east_bias[:heads]

    all_picks, grad_query = attend(
        neighbours, counts, ext, ext_bias, grad_rows, query, grad_att, key_value, part,
        w_kv, gathered, scores, grad_probs, probs_low, scores_low, scores_rest, grad_kv,
        attended_t, grad_query_t, bias_parts,
    )

    plane = pl.ds(0, NXY)
    depth = pl.ds(NXY, NZ)

    def core_copy(which):
        start, count = ((0, NXY), (NXY, NZ))[which]
        return remote(
            part.at[pl.ds(other + start, count)], from_core.at[pl.ds(start, count)],
            core_send.at[which], core_recv.at[which], partner,
        )

    core_copy(1).start()
    core_copy(0).start()

    def add_core(start, count):
        mine_rows = part[pl.ds(base + start, count)].astype(F32)
        half[pl.ds(start, count)] = (mine_rows + from_core[pl.ds(start, count)].astype(F32)).astype(BF)

    core_copy(1).wait_recv()
    add_core(NXY, NZ)

    @pl.loop(1, NZ)
    def _(step):
        peer = (z + step) % NZ
        remote(half.at[NXY + peer], from_first.at[NXY + z], first_send.at[1], first_recv.at[1], depth_peer(peer)).start()

    core_copy(0).wait_recv()
    add_core(0, NXY)

    @pl.loop(1, NXY)
    def _(step):
        peer = (xy + step) % NXY
        remote(half.at[peer], from_first.at[xy], first_send.at[0], first_recv.at[0], plane_peer(peer)).start()

    from_first[xy] = half[xy]
    from_first[NXY + z] = half[NXY + z]
    scatter(all_picks, grad_query, w_query, w_kv, grad_kv, bias_parts, feat_parts, halo, own, bias_sum)
    for index in range(2):
        device = (west, east)[index]
        columns = pl.ds(9 * index, 3)
        remote(halo.at[columns], side.at[1 - index], side_send.at[0], side_recv.at[0], device).start()
        remote(bias_sum.at[columns], side_bias.at[1 - index], side_send.at[1], side_recv.at[1], device).start()

    settle(half.at[pl.ds(0, NZ - 1)], first_recv.at[1])
    mine[1] = jnp.sum(from_first[depth].astype(F32), axis=0).astype(BF)

    @pl.loop(1, NXY)
    def _(step):
        peer = (xy + step) % NXY
        remote(mine.at[1], from_second.at[xy], second_send.at[1], second_recv.at[1], plane_peer(peer)).start()

    settle(half.at[pl.ds(0, NXY - 1)], first_recv.at[0])
    mine[0] = jnp.sum(from_first[plane].astype(F32), axis=0).astype(BF)

    @pl.loop(1, NZ)
    def _(step):
        peer = (z + step) % NZ
        remote(mine.at[0], from_second.at[NXY + z], second_send.at[0], second_recv.at[0], depth_peer(peer)).start()

    from_second[xy] = mine[1]
    from_second[NXY + z] = mine[0]

    settle(side, side_recv.at[0])
    settle(side_bias, side_recv.at[1])
    for index in range(2):
        for j in range(2):
            slot = 3 * j + 3 + 2 * index
            rows_out[index, j] = (halo[slot].astype(F32) + side[j, 2 * index].astype(F32)).astype(BF)
            rows_bias[index, j] = bias_sum[slot] + side_bias[j, 2 * index]

    def to_edge(index):
        device = (north, south)[index]
        landed = 2 - 2 * index
        remote(rows_out.at[index], edge.at[1 - index], edge_send.at[2 * index], edge_recv.at[landed], device).start()
        remote(rows_bias.at[index], edge_bias.at[1 - index], edge_send.at[2 * index + 1], edge_recv.at[landed + 1], device).start()

    pl.when(lat == seam - 1)(lambda: to_edge(1))
    pl.when(lat > 0)(lambda: to_edge(0))
    pl.when((lat < nlat - 1) & (lat != seam - 1))(lambda: to_edge(1))

    settle(half.at[pl.ds(0, NXY - 1)], second_recv.at[1])
    total[1] = jnp.sum(from_second[plane].astype(F32), axis=0).astype(BF)

    @pl.loop(1, NZ)
    def _(step):
        peer = (z + step) % NZ
        remote(total.at[1], summed.at[base + NXY + z], third_send.at[1], third_recv.at[1], depth_peer(peer)).start()

    summed[base + NXY + z] = total[1]
    settle(half.at[pl.ds(0, NZ - 1)], second_recv.at[0])
    total[0] = jnp.sum(from_second[depth].astype(F32), axis=0).astype(BF)

    @pl.loop(1, NXY)
    def _(step):
        peer = (xy + step) % NXY
        remote(total.at[0], summed.at[base + xy], third_send.at[0], third_recv.at[0], plane_peer(peer)).start()

    summed[base + xy] = total[0]

    def fourth_copy(which):
        start, count = ((0, NXY), (NXY, NZ))[which]
        rows = summed.at[pl.ds(base + start, count)]
        return remote(rows, rows, fourth_send.at[0], fourth_recv.at[0], partner)

    settle(half.at[pl.ds(0, NZ - 1)], third_recv.at[1])
    fourth_copy(1).start()
    settle(half.at[pl.ds(0, NXY - 1)], third_recv.at[0])
    fourth_copy(0).start()
    own_rows = pl.ds(base, NPEER)
    other_rows = pl.ds(other, NPEER)
    own_out = pltpu.make_async_copy(summed.at[own_rows], out.at[own_rows], out_sem.at[0])
    own_out.start()

    @pl.when(lat == 0)
    def _():
        edge[0] = jnp.zeros_like(edge[0])
        edge_bias[0] = jnp.zeros_like(edge_bias[0])

    @pl.when(lat == nlat - 1)
    def _():
        edge[1] = jnp.zeros_like(edge[1])
        edge_bias[1] = jnp.zeros_like(edge_bias[1])

    @pl.when(lat > 0)
    def _():
        settle(rows_out.at[0], edge_send.at[0])
        settle(rows_bias.at[0], edge_send.at[1])
        settle(edge.at[0], edge_recv.at[0])
        settle(edge_bias.at[0], edge_recv.at[1])

    @pl.when(lat < nlat - 1)
    def _():
        settle(rows_out.at[1], edge_send.at[2])
        settle(rows_bias.at[1], edge_send.at[3])
        settle(edge.at[1], edge_recv.at[2])
        settle(edge_bias.at[1], edge_recv.at[3])

    for j in range(2):
        total_grad = own[j] + side[j, 1].astype(F32) + (edge[0, j].astype(F32) + edge[1, j].astype(F32))
        grad_feat[j] = total_grad.astype(BF)
        grad_bias[j] = bias_sum[3 * j + 4] + side_bias[j, 1] + (edge_bias[0, j] + edge_bias[1, j])

    settle(ext.at[pl.ds(0, 2)], wide_send.at[0])
    settle(near_bias.at[pl.ds(0, 2)], near_send.at[0])

    @pl.when(lat > 0)
    def _():
        settle(ext.at[pl.ds(0, 3)], wide_send.at[1])
        settle(ext.at[0], wide_send.at[3])
        settle(near_bias.at[pl.ds(0, 3)], near_send.at[1])

    @pl.when(lat < nlat - 1)
    def _():
        settle(ext.at[pl.ds(0, 3)], wide_send.at[2])
        settle(ext.at[0], wide_send.at[4])
        settle(near_bias.at[pl.ds(0, 3)], near_send.at[2])

    core_copy(0).wait_send()
    core_copy(1).wait_send()
    settle(side, side_send.at[0])
    settle(side_bias, side_send.at[1])
    for sems, wide_index in ((first_send, 0), (second_send, 1), (third_send, 0)):
        settle(half.at[pl.ds(0, NXY - 1)], sems.at[wide_index])
        settle(half.at[pl.ds(0, NZ - 1)], sems.at[1 - wide_index])
    settle(half, fourth_send.at[0])
    settle(half, fourth_recv.at[0])
    other_out = pltpu.make_async_copy(summed.at[other_rows], out.at[other_rows], out_sem.at[1])
    other_out.start()
    own_out.wait()
    other_out.wait()


def layer_call(neighbours, counts, feat, key_bias, grad_out, w_query, w_key, w_value, w_out):
    _, _, slots, chans = feat.shape
    heads = key_bias.shape[0] // 2
    blocks = 12
    entries = counts.shape[2]
    keys_all = entries * slots
    vmem = pl.BlockSpec(memory_space=pltpu.VMEM)
    hbm = pl.BlockSpec(memory_space=pl.ANY)
    low = lambda *shape: pltpu.VMEM(shape, BF)
    wide = lambda *shape: pltpu.VMEM(shape, F32)
    dma = pltpu.SemaphoreType.DMA
    return pl.pallas_call(
        layer_kernel,
        out_shape=[
            jax.ShapeDtypeStruct((2 * NPEER, ROWS, chans), BF),
            jax.ShapeDtypeStruct((2, slots, chans), BF),
            jax.ShapeDtypeStruct((2, heads, slots), F32),
        ],
        in_specs=[hbm] * 3 + [vmem] + [hbm] * 5,
        out_specs=[hbm, vmem, vmem],
        scratch_shapes=[
            pltpu.SMEM(neighbours.shape, jnp.int32),
            pltpu.SMEM(counts.shape, jnp.int32),
            low(blocks, slots, chans),
            low(9, 2 * heads, slots),
            wide(blocks, heads, slots),
            low(2, slots, chans),
            low(chans, chans),
            low(chans, chans),
            low(2, slots, chans),
            low(2, slots, chans),
            low(2 * keys_all, 2 * chans),
            low(2 * NPEER, ROWS, chans),
            low(blocks, slots, chans),
            wide(2, slots, chans),
            wide(blocks, heads, slots),
            wide(2, keys_all, chans),
            wide(2, entries, heads, slots),
            low(chans, 2 * chans),
            low(2, keys_all, chans),
            wide(keys_all, PAIR * slots),
            wide(keys_all, PAIR * slots),
            low(keys_all, PAIR * slots),
            low(keys_all, PAIR * slots),
            low(keys_all, PAIR * slots),
            low(2 * keys_all, 2 * chans),
            low(chans, 2 * slots),
            low(chans, 2 * slots),
            low(NPEER, ROWS, chans),
            low(NPEER, ROWS, chans),
            low(NPEER, ROWS, chans),
            low(2, ROWS, chans),
            low(NPEER, ROWS, chans),
            low(2, ROWS, chans),
            low(2 * NPEER, ROWS, chans),
            low(2, 3, slots, chans),
            wide(2, 3, heads, slots),
            low(2, 2, slots, chans),
            wide(2, 2, heads, slots),
            low(2, 2, slots, chans),
            wide(2, 2, heads, slots),
        ]
        + [dma((count,)) for count in (7, 2, 5, 5, 3, 3)]
        + [dma((count,)) for count in (2, 2, 2, 2, 2, 2, 2, 2, 1, 1, 2, 2, 4, 4)],
        compiler_params=pltpu.CompilerParams(collective_id=0, has_side_effects=True, vmem_limit_bytes=62 << 20),
        name="layer_backward",
    )(neighbours, counts, feat, key_bias, grad_out, w_query, w_key, w_value, w_out)


def finish_kernel(scale, low, grad_feat, grad_bias, feat_out, bias_out, w0, w1, w2, w3, packed, plain, load_sem, store_sem):
    weights = (w0, w1, w2, w3)
    chans = w0.shape[0]
    loads = [pltpu.make_async_copy(low.at[pl.ds(chans * i, chans)], packed.at[i], load_sem.at[i]) for i in range(4)]
    for load in loads:
        load.start()
    stores = [
        pltpu.make_async_copy(grad_feat, feat_out.at[0], store_sem.at[4]),
        pltpu.make_async_copy(grad_bias, bias_out.at[0], store_sem.at[5]),
    ]
    for store in stores:
        store.start()
    for i in range(4):
        loads[i].wait()
        plain[i] = packed[i].astype(F32) * scale
        stores.append(pltpu.make_async_copy(plain.at[i], weights[i], store_sem.at[i]))
        stores[-1].start()
    for store in stores:
        store.wait()


def finish_call(low, grad_feat, grad_bias, scale):
    chans = low.shape[1]
    hbm = pl.BlockSpec(memory_space=pl.ANY)
    dma = pltpu.SemaphoreType.DMA
    weight = jax.ShapeDtypeStruct((chans, chans), F32)
    return pl.pallas_call(
        functools.partial(finish_kernel, scale),
        out_shape=[
            jax.ShapeDtypeStruct((1,) + grad_feat.shape, BF),
            jax.ShapeDtypeStruct((1,) + grad_bias.shape, F32),
        ]
        + [weight] * 4,
        in_specs=[hbm] * 3,
        out_specs=[hbm] * 6,
        scratch_shapes=[
            pltpu.VMEM((4, chans, chans), BF),
            pltpu.VMEM((4, chans, chans), F32),
            dma((4,)),
            dma((6,)),
        ],
        compiler_params=pltpu.CompilerParams(vmem_limit_bytes=62 << 20),
        name="scale_weights",
    )(low, grad_feat, grad_bias)


def per_device(
    features, w_query, w_key, w_value, w_out, key_bias, neighbours, key_counts, grad_out
):
    brows, bcols, slots, chans = features.shape
    heads = key_bias.shape[2]
    low, grad_features, grad_bias = layer_call(
        neighbours, key_counts, features, key_bias.reshape(bcols * heads, slots), grad_out,
        w_query, w_key, w_value, w_out,
    )
    cells = lax.axis_size("lat") * lax.axis_size("lon") * brows * bcols * slots
    return tuple(
        finish_call(low.reshape(4 * chans, chans), grad_features, grad_bias, float(cells) ** (-0.5))
    )


def solution(mesh):
    placed = (
        P("lat", "lon", None, None),
        P(),
        P(),
        P(),
        P(),
        P("lat", "lon", None, None),
        P("lat", "lon", None),
        P("lat", "lon", None),
        P("lat", "lon", None, None),
    )
    return jax.shard_map(
        per_device,
        mesh=mesh,
        in_specs=placed,
        out_specs=(P("lat", "lon", None, None), P("lat", "lon", None, None), P(), P(), P(), P()),
        check_vma=False,
    )
```

```python
import functools
import math

import jax
import jax.numpy as jnp
import numpy as np
from jax import lax
from jax.experimental import pallas as pl
from jax.experimental.pallas import tpu as pltpu
from jax.sharding import PartitionSpec as P

BF = jnp.bfloat16
F32 = jnp.float32
HEADS = 8
PAIR = 4
WINDOW = 256
NT = (((1,), (1,)), ((), ()))
TN = (((0,), (0,)), ((), ()))
FAR = -1e30


def bf16_parts(value, count):
    parts = []
    for _ in range(count):
        part = float(np.asarray(value, dtype=jnp.bfloat16).astype(np.float64))
        parts.append(part)
        value = value - part
    return parts


def mm(a, b, dims=None):
    if dims is None:
        return jnp.dot(a, b, preferred_element_type=F32)
    return lax.dot_general(a, b, dims, preferred_element_type=F32)


def project(ext, grad_rows, w_query, w_out, w_kv, query, grad_att, key_value):
    slots = ext.shape[1]
    entries = key_value.shape[0] // (2 * slots)
    for b in range(2):
        feat = ext[3 * b + 4]
        query[b] = mm(feat, w_query[...]).astype(BF)
        grad_att[b] = mm(grad_rows[b], w_out[...], NT).astype(BF)
        key_value[b * entries * slots:(b * entries + 1) * slots] = mm(feat, w_kv[...]).astype(BF)


def attend(
    neighbours, counts, ext, ext_bias, grad_out, query_all, grad_att_all, key_value, part, send_part,
    w_kv, gathered, scores, grad_probs, probs_low, scores_low, scores_rest, grad_kv,
    attended_t, grad_query_t, bias_parts,
):
    lat = lax.axis_index("lat")
    lon = lax.axis_index("lon")
    columns = 2 * lax.axis_size("lon")

    def local_slot(block):
        row = lax.div(block, columns) - lat + 1
        column = lax.rem(lax.rem(block, columns) - 2 * lon + 1 + columns, columns)
        return jnp.clip(column, 0, 3) * 3 + jnp.clip(row, 0, 2)

    slots, chans = ext.shape[1:]
    width = chans // HEADS
    entries = counts.shape[2]
    keys_all = entries * slots
    root = math.sqrt(width)
    parts = bf16_parts(root, 3)
    log2e = math.log2(math.e) / root
    lane = lax.broadcasted_iota(jnp.int32, (slots, WINDOW), 1)
    row = lax.broadcasted_iota(jnp.int32, (slots, WINDOW), 0)
    place_row = lax.broadcasted_iota(jnp.int32, (HEADS, WINDOW), 0)
    place_lane = lax.broadcasted_iota(jnp.int32, (HEADS, WINDOW), 1)
    pick_row = lax.broadcasted_iota(jnp.int32, (2 * HEADS, PAIR * slots), 0)
    pick_lane = lax.broadcasted_iota(jnp.int32, (2 * HEADS, PAIR * slots), 1)
    all_picks = []
    for b in range(2):
        picks = [local_slot(neighbours[0, b, e]) for e in range(entries)]
        all_picks.append(picks)
        query = query_all[b]
        grad_att = grad_att_all[b]
        gathered[b, 0:slots, :] = ext[3 * b + 4]
        for e in range(1, entries):
            gathered[b, e * slots:(e + 1) * slots, :] = ext[picks[e]]
        rest = pl.ds(b * keys_all + slots, keys_all - slots)
        key_value[rest, :] = mm(gathered[b, slots:], w_kv[...]).astype(BF)
        kv = key_value[pl.ds(b * keys_all, keys_all), :]
        bias_row = jnp.concatenate([ext_bias[picks[e]] for e in range(entries)], axis=1)
        bias_rows = jnp.zeros((2 * HEADS, keys_all), F32)
        for w in range(2):
            lo = w * (chans - WINDOW)
            first = PAIR * w
            spare = PAIR * width if w == 0 else 0
            region = (lane < PAIR * width) if w == 0 else (lane >= WINDOW - PAIR * width)
            place = jnp.zeros((HEADS, WINDOW), F32)
            for hh in range(PAIR):
                start = spare + 3 * hh
                place = jnp.where(
                    (place_row == first + hh) & (place_lane >= start) & (place_lane < start + 3), 1.0, place
                )
            bias_cols = mm(bias_row, place, TN)
            key_aug = []
            for e in range(entries):
                cols = bias_cols[e * slots:(e + 1) * slots]
                cols = jnp.where((lane == spare + 3 * PAIR) & (row >= counts[0, b, e]), FAR, cols)
                piece = kv[e * slots:(e + 1) * slots, lo:lo + WINDOW]
                key_aug.append(jnp.where(region, piece.astype(F32), cols).astype(BF))
            key_aug = jnp.concatenate(key_aug, axis=0)
            value_win = kv[:, chans + lo:chans + lo + WINDOW]
            query_win = query[:, lo:lo + WINDOW].astype(F32)
            grad_win = grad_att[:, lo:lo + WINDOW].astype(F32)
            query_aug, grad_aug = [], []
            for hh in range(PAIR):
                inside = (lane >= (first + hh) * width - lo) & (lane < (first + hh + 1) * width - lo)
                const = jnp.where(lane == spare + 3 * PAIR, 1.0, 0.0)
                for t in range(3):
                    const = jnp.where(lane == spare + 3 * hh + t, parts[t], const)
                query_aug.append(jnp.where(inside, query_win, const).astype(BF))
                grad_aug.append(jnp.where(inside, grad_win, 0.0).astype(BF))
            query_aug = jnp.concatenate(query_aug, axis=0)
            grad_aug = jnp.concatenate(grad_aug, axis=0)
            scores[...] = mm(key_aug, query_aug, NT)
            grad_probs[...] = mm(value_win, grad_aug, NT)
            for hh in range(PAIR):
                cut = pl.ds(hh * slots, slots)
                logits = scores[:, cut]
                powers = jnp.exp2((logits - jnp.max(logits, axis=0, keepdims=True)) * log2e)
                probs = powers * (1.0 / jnp.sum(powers, axis=0, keepdims=True))
                probs_low[:, cut] = probs.astype(BF)
                grads = grad_probs[:, cut]
                centre = jnp.sum(probs * grads, axis=0, keepdims=True)
                full = probs * (grads - centre)
                high = full.astype(BF)
                scores_low[:, cut] = high
                scores_rest[:, cut] = (full - high.astype(F32)).astype(BF)
            value_grad = mm(probs_low[...], grad_aug)
            key_grad = mm(scores_low[...], query_aug)
            chosen = jnp.where(pick_lane // slots + first == pick_row, 1.0, 0.0).astype(BF)
            bias_rows = bias_rows + mm(chosen, scores_low[...], NT) + mm(chosen, scores_rest[...], NT)
            scale = 1.0 / root
            base = b * keys_all
            rows = pl.ds(base, keys_all)
            half = WINDOW // 2
            edge = PAIR * width - half
            low_lane = lane[0:1, 0:half]
            if w == 0:
                grad_kv[rows, 0:half] = (key_grad[:, 0:half] * scale).astype(BF)
                grad_kv[rows, chans:chans + half] = value_grad[:, 0:half].astype(BF)
                saved_key, saved_value = key_grad[:, half:], value_grad[:, half:]
            else:
                middle = jnp.where(low_lane < edge, saved_key, key_grad[:, 0:half]) * scale
                grad_kv[rows, half:2 * half] = middle.astype(BF)
                grad_kv[rows, 2 * half:3 * half] = (key_grad[:, half:] * scale).astype(BF)
                middle = saved_value + value_grad[:, 0:half]
                grad_kv[rows, chans + half:chans + 2 * half] = middle.astype(BF)
                grad_kv[rows, chans + 2 * half:chans + 3 * half] = value_grad[:, half:].astype(BF)
            for pair in range(2):
                head = first + 2 * pair
                cut = pl.ds(2 * pair * slots, 2 * slots)
                value_rows = kv[:, chans + head * width:chans + (head + 2) * width]
                key_rows = kv[:, head * width:(head + 2) * width]
                both = mm(value_rows, probs_low[:, cut], TN)
                attended_t[head * width:(head + 1) * width, b * slots:(b + 1) * slots] = both[:width, :slots].astype(BF)
                attended_t[(head + 1) * width:(head + 2) * width, b * slots:(b + 1) * slots] = both[width:, slots:].astype(BF)
                both = mm(key_rows, scores_low[:, cut], TN) * scale
                grad_query_t[head * width:(head + 1) * width, b * slots:(b + 1) * slots] = both[:width, :slots].astype(BF)
                grad_query_t[(head + 1) * width:(head + 2) * width, b * slots:(b + 1) * slots] = both[width:, slots:].astype(BF)
        for e in range(entries):
            bias_parts[b, e] = bias_rows[:HEADS, e * slots:(e + 1) * slots]
    grad_query = jnp.transpose(grad_query_t[...].astype(F32)).astype(BF)
    feat_both = jnp.concatenate([ext[4], ext[7]], axis=0)
    grad_both = grad_out[...].reshape(2 * slots, chans)
    piece = chans // ROWS

    def put(index, value):
        part[index * piece:(index + 1) * piece] = value.astype(BF).reshape(piece, ROWS, chans)

    weight_kv = mm(gathered[...].reshape(2 * keys_all, chans), grad_kv[...], TN)
    put(1, weight_kv[:, :chans])
    put(2, weight_kv[:, chans:])
    send_part(0)
    put(0, mm(feat_both, grad_query, TN))
    put(3, mm(attended_t[...], grad_both))
    send_part(1)
    return all_picks, grad_query


def feature_parts(w_kv, grad_kv, feat_parts):
    keys_all = feat_parts.shape[1]
    for b in range(2):
        feat_parts[b] = mm(grad_kv[pl.ds(b * keys_all, keys_all), :], w_kv[...], NT)


def scatter(all_picks, grad_query, w_query, bias_parts, feat_parts, halo, own, bias_sum):
    slots, chans = halo.shape[1:]
    entries = len(all_picks[0])
    query_part = mm(grad_query, w_query[...], NT)
    for slot in range(halo.shape[0]):
        column = slot // 3
        total, bias_total = None, None
        for b in range(2):
            if column - b not in (0, 1, 2):
                continue
            for e in range(1, entries):
                hit = all_picks[b][e] == slot
                piece = jnp.where(hit, feat_parts[b, e * slots:(e + 1) * slots], 0.0)
                total = piece if total is None else total + piece
                piece = jnp.where(hit, bias_parts[b, e], 0.0)
                bias_total = piece if bias_total is None else bias_total + piece
        if slot in (4, 7):
            b = column - 1
            own[b] = total + (feat_parts[b, 0:slots] + query_part[b * slots:(b + 1) * slots])
            bias_total = bias_total + bias_parts[b, 0]
        else:
            halo[slot] = total.astype(BF)
        bias_sum[slot] = bias_total


MESH = pl.DeviceIdType.MESH
NXY = 16
NZ = 8
NPEER = NXY + NZ
ROWS = 32


def ring(offset, size):
    return min(offset, size - offset)


PLANE = sorted(
    [(dx, dy) for dx in range(4) for dy in range(4) if dx or dy],
    key=lambda o: -(ring(o[0], 4) + ring(o[1], 4)),
)
DEPTH = sorted(range(1, NZ), key=lambda o: -ring(o, NZ))


def remote(src, dst, send_sem, recv_sem, device):
    return pltpu.make_async_remote_copy(
        src_ref=src, dst_ref=dst, send_sem=send_sem, recv_sem=recv_sem,
        device_id=device, device_id_type=MESH,
    )


def layer_kernel(
    neighbours_hbm, counts_hbm, feat, key_bias, grad_out, w_query_hbm, w_key_hbm, w_value_hbm, w_out_hbm,
    out, grad_feat, grad_bias,
    neighbours, counts, ext, near_bias, ext_bias, grad_rows, w_query, w_out, query, grad_att, key_value,
    part, halo, own, bias_sum, feat_parts, bias_parts, w_kv, gathered, scores, grad_probs, probs_low,
    scores_low, scores_rest, grad_kv, attended_t, grad_query_t,
    from_core, half, from_first, mine, from_second, total, summed,
    side, side_bias, rows_out, rows_bias, edge, edge_bias,
    local_sem, out_sem, wide_send, wide_recv, near_send, near_recv,
    core_send, core_recv, first_send, first_recv, second_send, second_recv,
    third_send, third_recv, fourth_send, fourth_recv, side_send, side_recv, edge_send, edge_recv,
):
    lat = lax.axis_index("lat")
    lon = lax.axis_index("lon")
    core = lon % 2
    z = (lon // 2) % NZ
    x_lo = lon // (2 * NZ)
    x_hi = lat // 4
    y = lat % 4
    xy = (x_hi * 2 + x_lo) * 4 + y
    partner = (lat, lon + 1 - 2 * core)
    nlat = lax.axis_size("lat")
    nlon = lax.axis_size("lon")
    east = (lat, (lon + 1) % nlon)
    west = (lat, (lon + nlon - 1) % nlon)
    north = (lat - 1, lon)
    south = (lat + 1, lon)
    base = core * NPEER
    other = (1 - core) * NPEER

    off_lon = (lon + nlon - 1 + 2 * core) % nlon
    off = (lat, off_lon)
    seam = nlat // 2

    x = x_hi * 2 + x_lo

    def plane_peers():
        for dx, dy in PLANE:
            px = (x + dx) % 4
            py = (y + dy) % 4
            yield px * 4 + py, ((px // 2) * 4 + py, (px % 2) * (2 * NZ) + z * 2 + core)

    def depth_peers():
        for dz in DEPTH:
            pz = (z + dz) % NZ
            yield pz, (lat, x_lo * (2 * NZ) + pz * 2 + core)

    barrier = pltpu.get_barrier_semaphore()

    def greet(device):
        pl.semaphore_signal(barrier, inc=1, device_id=device, device_id_type=MESH)

    def settle(like, sem):
        pltpu.make_async_copy(like, like, sem).wait()

    chans = feat.shape[3]
    loads = [
        (feat.at[0, 0], ext.at[4], 0),
        (feat.at[0, 1], ext.at[7], 0),
        (w_query_hbm, w_query, 1),
        (grad_out.at[0], grad_rows, 2),
        (w_out_hbm, w_out, 3),
        (w_key_hbm, w_kv.at[:, pl.ds(0, chans)], 4),
        (w_value_hbm, w_kv.at[:, pl.ds(chans, chans)], 4),
        (neighbours_hbm, neighbours, 5),
        (counts_hbm, counts, 6),
    ]
    greet(partner)
    greet(off)

    @pl.when(lat > 0)
    def _():
        greet((lat - 1, off_lon))
        greet((lat - 1, partner[1]))

    @pl.when(lat < nlat - 1)
    def _():
        greet((lat + 1, off_lon))
        greet((lat + 1, partner[1]))

    for src, dst, index in loads:
        pltpu.make_async_copy(src, dst, local_sem.at[index]).start()
    for _, device in plane_peers():
        greet(device)
    for _, device in depth_peers():
        greet(device)

    near_bias[4] = key_bias[...]
    inner = jnp.minimum(lat, 1) + jnp.minimum(nlat - 1 - lat, 1)
    pl.semaphore_wait(barrier, NPEER + 2 * inner)

    feat_off = feat.at[0, core]
    feat_in = feat.at[0, 1 - core]
    s_off = 4 + 3 * core
    s_in = 7 - 3 * core
    t_off = 9 - 9 * core
    t_in = 9 * core
    b_off = 2 - 2 * core
    b_in = 2 * core

    def wide_copy(source, target, sent, landed, device):
        return remote(source, ext.at[target], wide_send.at[sent], wide_recv.at[landed], device)

    def near_copy(target, sent, landed, device):
        return remote(near_bias.at[4], near_bias.at[target], near_send.at[sent], near_recv.at[landed], device)

    def to_row(up):
        device = north if up else south
        corner = (lat - 1, off_lon) if up else (lat + 1, off_lon)
        inside = (corner[0], partner[1])
        step, row, sent, landed = (1, 2, 1, 2) if up else (-1, 0, 2, 1)
        wide_copy(feat_in, s_in + step, sent, landed, device).start()
        wide_copy(feat_off, t_off + row, sent, landed + 2, corner).start()
        wide_copy(feat_off, s_off + step, sent, landed + 2, device).start()
        near_copy(3 * row + 1, sent, landed, device).start()
        near_copy(3 * row + b_off, sent, landed, corner).start()
        near_copy(3 * row + b_in, sent, landed, inside).start()

    wide_copy(feat_in, t_in + 1, 0, 0, partner).start()
    wide_copy(feat_off, t_off + 1, 0, 0, off).start()
    near_copy(3 + b_in, 0, 0, partner).start()
    near_copy(3 + b_off, 0, 0, off).start()
    pl.when(lat == seam - 1)(lambda: to_row(False))
    pl.when(lat > 0)(lambda: to_row(True))
    pl.when((lat < nlat - 1) & (lat != seam - 1))(lambda: to_row(False))

    settle(ext.at[pl.ds(0, 2)], local_sem.at[0])
    settle(w_query, local_sem.at[1])
    settle(grad_rows, local_sem.at[2])
    settle(w_out, local_sem.at[3])
    settle(w_kv, local_sem.at[4])
    settle(neighbours, local_sem.at[5])
    settle(counts, local_sem.at[6])
    project(ext, grad_rows, w_query, w_out, w_kv, query, grad_att, key_value)

    def pass_on(row):
        landed = 1 + row // 2
        slot = s_in - 1 + row
        settle(ext.at[slot], wide_recv.at[landed])
        wide_copy(ext.at[slot], t_in + row, landed + 2, landed + 2, partner).start()

    def arrived(row):
        landed = 1 + row // 2
        settle(ext.at[pl.ds(0, 3)], wide_recv.at[landed + 2])
        settle(near_bias.at[pl.ds(0, 3)], near_recv.at[landed])

    pl.when(lat == seam - 1)(lambda: pass_on(0))
    pl.when(lat < nlat - 1)(lambda: pass_on(2))
    pl.when((lat > 0) & (lat != seam - 1))(lambda: pass_on(0))
    settle(ext.at[pl.ds(0, 2)], wide_recv.at[0])
    settle(near_bias.at[pl.ds(0, 2)], near_recv.at[0])
    pl.when(lat > 0)(lambda: arrived(0))
    pl.when(lat < nlat - 1)(lambda: arrived(2))
    heads = ext_bias.shape[1]
    for row in range(3):
        west_bias = near_bias[3 * row].astype(F32)
        own_bias = near_bias[3 * row + 1].astype(F32)
        east_bias = near_bias[3 * row + 2].astype(F32)
        ext_bias[row] = west_bias[heads:]
        ext_bias[3 + row] = own_bias[:heads]
        ext_bias[6 + row] = own_bias[heads:]
        ext_bias[9 + row] = east_bias[:heads]

    def core_copy(which):
        start, offset = ((2 - core, core), (3 - 3 * core, 1 - core))[which]
        count = NPEER // 2
        return remote(
            part.at[pl.ds(start * count, count)], from_core.at[pl.ds(offset * count, count)],
            core_send.at[which], core_recv.at[which], partner,
        )

    def send_part(which):
        core_copy(which).start()

    all_picks, grad_query = attend(
        neighbours, counts, ext, ext_bias, grad_rows, query, grad_att, key_value, part, send_part,
        w_kv, gathered, scores, grad_probs, probs_low, scores_low, scores_rest, grad_kv,
        attended_t, grad_query_t, bias_parts,
    )

    plane = pl.ds(0, NXY)
    depth = pl.ds(NXY, NZ)

    feature_parts(w_kv, grad_kv, feat_parts)
    core_copy(0).wait_recv()
    core_copy(1).wait_recv()
    half[...] = (part[pl.ds(base, NPEER)].astype(F32) + from_core[...].astype(F32)).astype(BF)

    for peer, device in depth_peers():
        remote(half.at[NXY + peer], from_first.at[NXY + z], first_send.at[1], first_recv.at[1], device).start()

    for peer, device in plane_peers():
        remote(half.at[peer], from_first.at[xy], first_send.at[0], first_recv.at[0], device).start()

    from_first[xy] = half[xy]
    from_first[NXY + z] = half[NXY + z]
    scatter(all_picks, grad_query, w_query, bias_parts, feat_parts, halo, own, bias_sum)
    for index in range(2):
        device = (west, east)[index]
        columns = pl.ds(9 * index, 3)
        remote(halo.at[columns], side.at[1 - index], side_send.at[0], side_recv.at[0], device).start()
        remote(bias_sum.at[columns], side_bias.at[1 - index], side_send.at[1], side_recv.at[1], device).start()

    settle(half.at[pl.ds(0, NZ - 1)], first_recv.at[1])
    mine[1] = jnp.sum(from_first[depth].astype(F32), axis=0).astype(BF)

    for peer, device in plane_peers():
        remote(mine.at[1], from_second.at[xy], second_send.at[1], second_recv.at[1], device).start()

    settle(half.at[pl.ds(0, NXY - 1)], first_recv.at[0])
    mine[0] = jnp.sum(from_first[plane].astype(F32), axis=0).astype(BF)

    for peer, device in depth_peers():
        remote(mine.at[0], from_second.at[NXY + z], second_send.at[0], second_recv.at[0], device).start()

    from_second[xy] = mine[1]
    from_second[NXY + z] = mine[0]

    def to_edge(index):
        device = (north, south)[index]
        landed = 2 - 2 * index
        remote(rows_out.at[index], edge.at[1 - index], edge_send.at[2 * index], edge_recv.at[landed], device).start()
        remote(rows_bias.at[index], edge_bias.at[1 - index], edge_send.at[2 * index + 1], edge_recv.at[landed + 1], device).start()

    def fold_columns():
        settle(side, side_recv.at[0])
        settle(side_bias, side_recv.at[1])
        for index in range(2):
            for j in range(2):
                slot = 3 * j + 3 + 2 * index
                rows_out[index, j] = (halo[slot].astype(F32) + side[j, 2 * index].astype(F32)).astype(BF)
                rows_bias[index, j] = bias_sum[slot] + side_bias[j, 2 * index]
        pl.when(lat == seam - 1)(lambda: to_edge(1))
        pl.when(lat > 0)(lambda: to_edge(0))
        pl.when((lat < nlat - 1) & (lat != seam - 1))(lambda: to_edge(1))

    wraps = (z == (NZ - 1) * core)
    pl.when(jnp.logical_not(wraps))(fold_columns)

    settle(half.at[pl.ds(0, NXY - 1)], second_recv.at[1])
    total[1] = jnp.sum(from_second[plane].astype(F32), axis=0).astype(BF)

    for peer, device in depth_peers():
        remote(total.at[1], summed.at[NXY + z], third_send.at[1], third_recv.at[1], device).start()

    summed[NXY + z] = total[1]
    pl.when(wraps)(fold_columns)
    settle(half.at[pl.ds(0, NZ - 1)], second_recv.at[0])
    total[0] = jnp.sum(from_second[depth].astype(F32), axis=0).astype(BF)

    for peer, device in plane_peers():
        remote(total.at[0], summed.at[xy], third_send.at[0], third_recv.at[0], device).start()

    summed[xy] = total[0]

    def fourth_copy(which):
        start, count = ((0, NXY), (NXY, NZ))[which]
        return remote(
            summed.at[pl.ds(start, count)], out.at[pl.ds(base + start, count)],
            fourth_send.at[0], fourth_recv.at[0], partner,
        )

    settle(half.at[pl.ds(0, NZ - 1)], third_recv.at[1])
    fourth_copy(1).start()
    settle(half.at[pl.ds(0, NXY - 1)], third_recv.at[0])
    fourth_copy(0).start()
    own_out = pltpu.make_async_copy(summed, out.at[pl.ds(base, NPEER)], out_sem.at[0])
    own_out.start()

    @pl.when(lat == 0)
    def _():
        edge[0] = jnp.zeros_like(edge[0])
        edge_bias[0] = jnp.zeros_like(edge_bias[0])

    @pl.when(lat == nlat - 1)
    def _():
        edge[1] = jnp.zeros_like(edge[1])
        edge_bias[1] = jnp.zeros_like(edge_bias[1])

    @pl.when(lat > 0)
    def _():
        settle(rows_out.at[0], edge_send.at[0])
        settle(rows_bias.at[0], edge_send.at[1])
        settle(edge.at[0], edge_recv.at[0])
        settle(edge_bias.at[0], edge_recv.at[1])

    @pl.when(lat < nlat - 1)
    def _():
        settle(rows_out.at[1], edge_send.at[2])
        settle(rows_bias.at[1], edge_send.at[3])
        settle(edge.at[1], edge_recv.at[2])
        settle(edge_bias.at[1], edge_recv.at[3])

    for j in range(2):
        total_grad = own[j] + side[j, 1].astype(F32) + (edge[0, j].astype(F32) + edge[1, j].astype(F32))
        grad_feat[j] = total_grad.astype(BF)
        grad_bias[j] = bias_sum[3 * j + 4] + side_bias[j, 1] + (edge_bias[0, j] + edge_bias[1, j])

    settle(ext.at[pl.ds(0, 2)], wide_send.at[0])
    settle(near_bias.at[pl.ds(0, 2)], near_send.at[0])

    @pl.when(lat > 0)
    def _():
        settle(ext.at[pl.ds(0, 3)], wide_send.at[1])
        settle(ext.at[0], wide_send.at[3])
        settle(near_bias.at[pl.ds(0, 3)], near_send.at[1])

    @pl.when(lat < nlat - 1)
    def _():
        settle(ext.at[pl.ds(0, 3)], wide_send.at[2])
        settle(ext.at[0], wide_send.at[4])
        settle(near_bias.at[pl.ds(0, 3)], near_send.at[2])

    core_copy(0).wait_send()
    core_copy(1).wait_send()
    settle(side, side_send.at[0])
    settle(side_bias, side_send.at[1])
    for sems, wide_index in ((first_send, 0), (second_send, 1), (third_send, 0)):
        settle(half.at[pl.ds(0, NXY - 1)], sems.at[wide_index])
        settle(half.at[pl.ds(0, NZ - 1)], sems.at[1 - wide_index])
    settle(half, fourth_send.at[0])
    settle(half, fourth_recv.at[0])
    own_out.wait()


def layer_call(neighbours, counts, feat, key_bias, grad_out, w_query, w_key, w_value, w_out):
    _, _, slots, chans = feat.shape
    heads = key_bias.shape[0] // 2
    blocks = 12
    entries = counts.shape[2]
    keys_all = entries * slots
    vmem = pl.BlockSpec(memory_space=pltpu.VMEM)
    hbm = pl.BlockSpec(memory_space=pl.ANY)
    low = lambda *shape: pltpu.VMEM(shape, BF)
    wide = lambda *shape: pltpu.VMEM(shape, F32)
    dma = pltpu.SemaphoreType.DMA
    return pl.pallas_call(
        layer_kernel,
        out_shape=[
            jax.ShapeDtypeStruct((2 * NPEER, ROWS, chans), BF),
            jax.ShapeDtypeStruct((2, slots, chans), BF),
            jax.ShapeDtypeStruct((2, heads, slots), F32),
        ],
        in_specs=[hbm] * 3 + [vmem] + [hbm] * 5,
        out_specs=[hbm, vmem, vmem],
        scratch_shapes=[
            pltpu.SMEM(neighbours.shape, jnp.int32),
            pltpu.SMEM(counts.shape, jnp.int32),
            low(blocks, slots, chans),
            low(9, 2 * heads, slots),
            wide(blocks, heads, slots),
            low(2, slots, chans),
            low(chans, chans),
            low(chans, chans),
            low(2, slots, chans),
            low(2, slots, chans),
            low(2 * keys_all, 2 * chans),
            low(2 * NPEER, ROWS, chans),
            low(blocks, slots, chans),
            wide(2, slots, chans),
            wide(blocks, heads, slots),
            wide(2, keys_all, chans),
            wide(2, entries, heads, slots),
            low(chans, 2 * chans),
            low(2, keys_all, chans),
            wide(keys_all, PAIR * slots),
            wide(keys_all, PAIR * slots),
            low(keys_all, PAIR * slots),
            low(keys_all, PAIR * slots),
            low(keys_all, PAIR * slots),
            low(2 * keys_all, 2 * chans),
            low(chans, 2 * slots),
            low(chans, 2 * slots),
            low(NPEER, ROWS, chans),
            low(NPEER, ROWS, chans),
            low(NPEER, ROWS, chans),
            low(2, ROWS, chans),
            low(NPEER, ROWS, chans),
            low(2, ROWS, chans),
            low(NPEER, ROWS, chans),
            low(2, 3, slots, chans),
            wide(2, 3, heads, slots),
            low(2, 2, slots, chans),
            wide(2, 2, heads, slots),
            low(2, 2, slots, chans),
            wide(2, 2, heads, slots),
        ]
        + [dma((count,)) for count in (7, 1, 5, 5, 3, 3)]
        + [dma((count,)) for count in (2, 2, 2, 2, 2, 2, 2, 2, 1, 1, 2, 2, 4, 4)],
        compiler_params=pltpu.CompilerParams(collective_id=0, has_side_effects=True, vmem_limit_bytes=62 << 20),
        name="layer_backward",
    )(neighbours, counts, feat, key_bias, grad_out, w_query, w_key, w_value, w_out)


def finish_kernel(
    scale, low, grad_feat, grad_bias, feat_out, bias_out, w0, w1, w2, w3,
    packed, plain, feat_rows, bias_rows, load_sem, store_sem,
):
    weights = (w0, w1, w2, w3)
    chans = w0.shape[0]
    loads = [(low.at[pl.ds(chans * i, chans)], packed.at[i]) for i in range(4)]
    loads += [(grad_feat, feat_rows), (grad_bias, bias_rows)]
    loads = [pltpu.make_async_copy(src, dst, load_sem.at[i]) for i, (src, dst) in enumerate(loads)]
    for load in loads:
        load.start()
    stores = [(plain.at[i], weights[i]) for i in range(4)]
    stores += [(feat_rows, feat_out.at[0]), (bias_rows, bias_out.at[0])]
    stores = [pltpu.make_async_copy(src, dst, store_sem.at[i]) for i, (src, dst) in enumerate(stores)]
    for i in range(6):
        loads[i].wait()
        if i < 4:
            plain[i] = packed[i].astype(F32) * scale
        stores[i].start()
    for store in stores:
        store.wait()


def finish_call(low, grad_feat, grad_bias, scale):
    chans = low.shape[1]
    hbm = pl.BlockSpec(memory_space=pl.ANY)
    dma = pltpu.SemaphoreType.DMA
    weight = jax.ShapeDtypeStruct((chans, chans), F32)
    return pl.pallas_call(
        functools.partial(finish_kernel, scale),
        out_shape=[
            jax.ShapeDtypeStruct((1,) + grad_feat.shape, BF),
            jax.ShapeDtypeStruct((1,) + grad_bias.shape, F32),
        ]
        + [weight] * 4,
        in_specs=[hbm] * 3,
        out_specs=[hbm] * 6,
        scratch_shapes=[
            pltpu.VMEM((4, chans, chans), BF),
            pltpu.VMEM((4, chans, chans), F32),
            pltpu.VMEM(grad_feat.shape, BF),
            pltpu.VMEM(grad_bias.shape, F32),
            dma((6,)),
            dma((6,)),
        ],
        compiler_params=pltpu.CompilerParams(vmem_limit_bytes=62 << 20),
        name="scale_weights",
    )(low, grad_feat, grad_bias)


def per_device(
    features, w_query, w_key, w_value, w_out, key_bias, neighbours, key_counts, grad_out
):
    brows, bcols, slots, chans = features.shape
    heads = key_bias.shape[2]
    low, grad_features, grad_bias = layer_call(
        neighbours, key_counts, features, key_bias.reshape(bcols * heads, slots), grad_out,
        w_query, w_key, w_value, w_out,
    )
    cells = lax.axis_size("lat") * lax.axis_size("lon") * brows * bcols * slots
    return tuple(
        finish_call(low.reshape(4 * chans, chans), grad_features, grad_bias, float(cells) ** (-0.5))
    )


def solution(mesh):
    placed = (
        P("lat", "lon", None, None),
        P(),
        P(),
        P(),
        P(),
        P("lat", "lon", None, None),
        P("lat", "lon", None),
        P("lat", "lon", None),
        P("lat", "lon", None, None),
    )
    return jax.shard_map(
        per_device,
        mesh=mesh,
        in_specs=placed,
        out_specs=(P("lat", "lon", None, None), P("lat", "lon", None, None), P(), P(), P(), P()),
        check_vma=False,
    )
```

```python
import functools
import math

import jax
import jax.numpy as jnp
import numpy as np
from jax import lax
from jax.experimental import pallas as pl
from jax.experimental.pallas import tpu as pltpu
from jax.sharding import PartitionSpec as P

BF = jnp.bfloat16
F32 = jnp.float32
HEADS = 8
PAIR = 4
WINDOW = 256
NT = (((1,), (1,)), ((), ()))
TN = (((0,), (0,)), ((), ()))
FAR = -1e30


def bf16_parts(value, count):
    parts = []
    for _ in range(count):
        part = float(np.asarray(value, dtype=jnp.bfloat16).astype(np.float64))
        parts.append(part)
        value = value - part
    return parts


def mm(a, b, dims=None):
    if dims is None:
        return jnp.dot(a, b, preferred_element_type=F32)
    return lax.dot_general(a, b, dims, preferred_element_type=F32)


def project(ext, grad_rows, w_query, w_out, w_kv, query, grad_att, key_value):
    slots = ext.shape[1]
    entries = key_value.shape[0] // (2 * slots)
    for b in range(2):
        feat = ext[3 * b + 4]
        query[b] = mm(feat, w_query[...]).astype(BF)
        grad_att[b] = mm(grad_rows[b], w_out[...], NT).astype(BF)
        key_value[b * entries * slots:(b * entries + 1) * slots] = mm(feat, w_kv[...]).astype(BF)


def attend(
    neighbours, counts, ext, ext_bias, grad_out, query_all, grad_att_all, key_value, part, send_part,
    w_kv, gathered, scores, grad_probs, probs_low, scores_low, grad_kv,
    attended_t, grad_query_t, bias_parts,
):
    lat = lax.axis_index("lat")
    lon = lax.axis_index("lon")
    columns = 2 * lax.axis_size("lon")

    def local_slot(block):
        row = lax.div(block, columns) - lat + 1
        column = lax.rem(lax.rem(block, columns) - 2 * lon + 1 + columns, columns)
        return jnp.clip(column, 0, 3) * 3 + jnp.clip(row, 0, 2)

    slots, chans = ext.shape[1:]
    width = chans // HEADS
    entries = counts.shape[2]
    keys_all = entries * slots
    root = math.sqrt(width)
    parts = bf16_parts(root, 3)
    log2e = math.log2(math.e) / root
    lane = lax.broadcasted_iota(jnp.int32, (slots, WINDOW), 1)
    row = lax.broadcasted_iota(jnp.int32, (slots, WINDOW), 0)
    place_row = lax.broadcasted_iota(jnp.int32, (HEADS, WINDOW), 0)
    place_lane = lax.broadcasted_iota(jnp.int32, (HEADS, WINDOW), 1)
    wide_lane = lax.broadcasted_iota(jnp.int32, (keys_all, slots), 1)
    bias_all = [jnp.zeros((keys_all, slots), F32)] * 2
    state = {}

    def gather(b):
        picks = [local_slot(neighbours[0, b, e]) for e in range(entries)]
        gathered[b, 0:slots, :] = ext[3 * b + 4]
        for e in range(1, entries):
            gathered[b, e * slots:(e + 1) * slots, :] = ext[picks[e]]
        rest = pl.ds(b * keys_all + slots, keys_all - slots)
        key_value[rest, :] = mm(gathered[b, slots:], w_kv[...]).astype(BF)
        kv = key_value[pl.ds(b * keys_all, keys_all), :]
        bias_row = jnp.concatenate([ext_bias[picks[e]] for e in range(entries)], axis=1)
        return picks, query_all[b], grad_att_all[b], kv, bias_row

    def prepare(b, w):
        picks, query, grad_att, kv, bias_row = state[b]
        lo = w * (chans - WINDOW)
        first = PAIR * w
        spare = PAIR * width if w == 0 else 0
        region = (lane < PAIR * width) if w == 0 else (lane >= WINDOW - PAIR * width)
        place = jnp.zeros((HEADS, WINDOW), F32)
        for hh in range(PAIR):
            start = spare + 3 * hh
            place = jnp.where(
                (place_row == first + hh) & (place_lane >= start) & (place_lane < start + 3), 1.0, place
            )
        bias_cols = mm(bias_row, place, TN)
        key_aug = []
        for e in range(entries):
            cols = bias_cols[e * slots:(e + 1) * slots]
            cols = jnp.where((lane == spare + 3 * PAIR) & (row >= counts[0, b, e]), FAR, cols)
            piece = kv[e * slots:(e + 1) * slots, lo:lo + WINDOW]
            key_aug.append(jnp.where(region, piece.astype(F32), cols).astype(BF))
        key_aug = jnp.concatenate(key_aug, axis=0)
        value_win = kv[:, chans + lo:chans + lo + WINDOW]
        query_win = query[:, lo:lo + WINDOW].astype(F32)
        grad_win = grad_att[:, lo:lo + WINDOW].astype(F32)
        query_aug, grad_aug = [], []
        for hh in range(PAIR):
            inside = (lane >= (first + hh) * width - lo) & (lane < (first + hh + 1) * width - lo)
            const = jnp.where(lane == spare + 3 * PAIR, 1.0, 0.0)
            for t in range(3):
                const = jnp.where(lane == spare + 3 * hh + t, parts[t], const)
            query_aug.append(jnp.where(inside, query_win, const).astype(BF))
            grad_aug.append(jnp.where(inside, grad_win, 0.0).astype(BF))
        query_aug = jnp.concatenate(query_aug, axis=0)
        grad_aug = jnp.concatenate(grad_aug, axis=0)
        scores[2 * b + w] = mm(key_aug, query_aug, NT)
        grad_probs[2 * b + w] = mm(value_win, grad_aug, NT)
        return query_aug, grad_aug, lo, first, spare, region

    def soften(b, w):
        first = PAIR * w
        bias_sums = bias_all[b]
        for hh in range(PAIR):
            cut = pl.ds(hh * slots, slots)
            logits = scores[2 * b + w, :, cut]
            powers = jnp.exp2((logits - jnp.max(logits, axis=0, keepdims=True)) * log2e)
            probs = powers * (1.0 / jnp.sum(powers, axis=0, keepdims=True))
            probs_low[2 * b + w, :, cut] = probs.astype(BF)
            grads = grad_probs[2 * b + w, :, cut]
            centre = jnp.sum(probs * grads, axis=0, keepdims=True)
            full = probs * (grads - centre)
            high = full.astype(BF)
            scores_low[2 * b + w, :, cut] = high
            bias_sums = jnp.where(wide_lane == first + hh, jnp.sum(full, axis=1, keepdims=True), bias_sums)
        bias_all[b] = bias_sums

    def finish(b, w):
        picks, query, grad_att, kv, bias_row = state[b]
        query_aug, grad_aug, lo, first, spare, region = state[b, w]
        value_grad = mm(probs_low[2 * b + w], grad_aug)
        key_grad = mm(scores_low[2 * b + w], query_aug)
        scale = 1.0 / root
        base = b * keys_all
        rows = pl.ds(base, keys_all)
        half = WINDOW // 2
        edge = PAIR * width - half
        low_lane = lane[0:1, 0:half]
        if w == 0:
            grad_kv[rows, 0:half] = (key_grad[:, 0:half] * scale).astype(BF)
            grad_kv[rows, chans:chans + half] = value_grad[:, 0:half].astype(BF)
            state[b, 'saved'] = key_grad[:, half:], value_grad[:, half:]
        else:
            saved_key, saved_value = state[b, 'saved']
            middle = jnp.where(low_lane < edge, saved_key, key_grad[:, 0:half]) * scale
            grad_kv[rows, half:2 * half] = middle.astype(BF)
            grad_kv[rows, 2 * half:3 * half] = (key_grad[:, half:] * scale).astype(BF)
            middle = saved_value + value_grad[:, 0:half]
            grad_kv[rows, chans + half:chans + 2 * half] = middle.astype(BF)
            grad_kv[rows, chans + 2 * half:chans + 3 * half] = value_grad[:, half:].astype(BF)
        for pair in range(2):
            head = first + 2 * pair
            cut = pl.ds(2 * pair * slots, 2 * slots)
            value_rows = kv[:, chans + head * width:chans + (head + 2) * width]
            key_rows = kv[:, head * width:(head + 2) * width]
            both = mm(value_rows, probs_low[2 * b + w, :, cut], TN)
            attended_t[head * width:(head + 1) * width, b * slots:(b + 1) * slots] = both[:width, :slots].astype(BF)
            attended_t[(head + 1) * width:(head + 2) * width, b * slots:(b + 1) * slots] = both[width:, slots:].astype(BF)
            both = mm(key_rows, scores_low[2 * b + w, :, cut], TN) * scale
            grad_query_t[head * width:(head + 1) * width, b * slots:(b + 1) * slots] = both[:width, :slots].astype(BF)
            grad_query_t[(head + 1) * width:(head + 2) * width, b * slots:(b + 1) * slots] = both[width:, slots:].astype(BF)

    steps = [(0, 0), (0, 1), (1, 0), (1, 1)]
    state[0] = gather(0)
    state[0, 0] = prepare(0, 0)
    state[1] = gather(1)
    for i, step in enumerate(steps):
        if i + 1 < len(steps):
            state[steps[i + 1]] = prepare(*steps[i + 1])
        soften(*step)
        finish(*step)
    all_picks = [state[b][0] for b in range(2)]
    for b in range(2):
        for e in range(entries):
            bias_parts[b, e] = jnp.transpose(bias_all[b][e * slots:(e + 1) * slots])[:HEADS]
    grad_query = jnp.transpose(grad_query_t[...].astype(F32)).astype(BF)
    feat_both = jnp.concatenate([ext[4], ext[7]], axis=0)
    grad_both = grad_out[...].reshape(2 * slots, chans)
    piece = chans // ROWS

    def put(index, value):
        part[index * piece:(index + 1) * piece] = value.astype(BF).reshape(piece, ROWS, chans)

    weight_kv = mm(gathered[...].reshape(2 * keys_all, chans), grad_kv[...], TN)
    put(1, weight_kv[:, :chans])
    put(2, weight_kv[:, chans:])
    send_part(0)
    put(0, mm(feat_both, grad_query, TN))
    put(3, mm(attended_t[...], grad_both))
    send_part(1)
    return all_picks, grad_query


def feature_parts(w_kv, grad_kv, feat_parts):
    keys_all = feat_parts.shape[1]
    for b in range(2):
        feat_parts[b] = mm(grad_kv[pl.ds(b * keys_all, keys_all), :], w_kv[...], NT)


def scatter(all_picks, grad_query, w_query, bias_parts, feat_parts, halo, own, bias_sum):
    slots, chans = halo.shape[1:]
    entries = len(all_picks[0])
    query_part = mm(grad_query, w_query[...], NT)
    for slot in range(halo.shape[0]):
        column = slot // 3
        total, bias_total = None, None
        for b in range(2):
            if column - b not in (0, 1, 2):
                continue
            for e in range(1, entries):
                hit = all_picks[b][e] == slot
                piece = jnp.where(hit, feat_parts[b, e * slots:(e + 1) * slots], 0.0)
                total = piece if total is None else total + piece
                piece = jnp.where(hit, bias_parts[b, e], 0.0)
                bias_total = piece if bias_total is None else bias_total + piece
        if slot in (4, 7):
            b = column - 1
            own[b] = total + (feat_parts[b, 0:slots] + query_part[b * slots:(b + 1) * slots])
            bias_total = bias_total + bias_parts[b, 0]
        else:
            halo[slot] = total.astype(BF)
        bias_sum[slot] = bias_total


MESH = pl.DeviceIdType.MESH
NXY = 16
NZ = 8
NPEER = NXY + NZ
ROWS = 32


def ring(offset, size):
    return min(offset, size - offset)


PLANE = sorted(
    [(dx, dy) for dx in range(4) for dy in range(4) if dx or dy],
    key=lambda o: -(ring(o[0], 4) + ring(o[1], 4)),
)
DEPTH = sorted(range(1, NZ), key=lambda o: -ring(o, NZ))


def remote(src, dst, send_sem, recv_sem, device):
    return pltpu.make_async_remote_copy(
        src_ref=src, dst_ref=dst, send_sem=send_sem, recv_sem=recv_sem,
        device_id=device, device_id_type=MESH,
    )


def layer_kernel(
    neighbours_hbm, counts_hbm, feat, key_bias, grad_out, w_query_hbm, w_key_hbm, w_value_hbm, w_out_hbm,
    out, grad_feat, grad_bias,
    neighbours, counts, ext, near_bias, ext_bias, grad_rows, w_query, w_out, query, grad_att, key_value,
    part, halo, own, bias_sum, feat_parts, bias_parts, w_kv, gathered, scores, grad_probs, probs_low,
    scores_low, grad_kv, attended_t, grad_query_t,
    from_core, half, from_first, mine, from_second, total, summed,
    side, side_bias, rows_out, rows_bias, edge, edge_bias,
    local_sem, out_sem, wide_send, wide_recv, near_send, near_recv,
    core_send, core_recv, first_send, first_recv, second_send, second_recv,
    third_send, third_recv, fourth_send, fourth_recv, side_send, side_recv, edge_send, edge_recv,
):
    lat = lax.axis_index("lat")
    lon = lax.axis_index("lon")
    core = lon % 2
    z = (lon // 2) % NZ
    x_lo = lon // (2 * NZ)
    x_hi = lat // 4
    y = lat % 4
    xy = (x_hi * 2 + x_lo) * 4 + y
    partner = (lat, lon + 1 - 2 * core)
    nlat = lax.axis_size("lat")
    nlon = lax.axis_size("lon")
    east = (lat, (lon + 1) % nlon)
    west = (lat, (lon + nlon - 1) % nlon)
    north = (lat - 1, lon)
    south = (lat + 1, lon)
    base = core * NPEER
    other = (1 - core) * NPEER

    off_lon = (lon + nlon - 1 + 2 * core) % nlon
    off = (lat, off_lon)
    seam = nlat // 2

    x = x_hi * 2 + x_lo

    def plane_peers():
        for dx, dy in PLANE:
            px = (x + dx) % 4
            py = (y + dy) % 4
            yield px * 4 + py, ((px // 2) * 4 + py, (px % 2) * (2 * NZ) + z * 2 + core)

    def depth_peers():
        for dz in DEPTH:
            pz = (z + dz) % NZ
            yield pz, (lat, x_lo * (2 * NZ) + pz * 2 + core)

    barrier = pltpu.get_barrier_semaphore()

    def greet(device):
        pl.semaphore_signal(barrier, inc=1, device_id=device, device_id_type=MESH)

    def settle(like, sem):
        pltpu.make_async_copy(like, like, sem).wait()

    chans = feat.shape[3]
    loads = [
        (feat.at[0, 0], ext.at[4], 0),
        (feat.at[0, 1], ext.at[7], 0),
        (w_query_hbm, w_query, 1),
        (grad_out.at[0], grad_rows, 2),
        (w_out_hbm, w_out, 3),
        (w_key_hbm, w_kv.at[:, pl.ds(0, chans)], 4),
        (w_value_hbm, w_kv.at[:, pl.ds(chans, chans)], 4),
        (neighbours_hbm, neighbours, 5),
        (counts_hbm, counts, 6),
    ]
    greet(partner)
    greet(off)

    @pl.when(lat > 0)
    def _():
        greet((lat - 1, off_lon))
        greet((lat - 1, partner[1]))

    @pl.when(lat < nlat - 1)
    def _():
        greet((lat + 1, off_lon))
        greet((lat + 1, partner[1]))

    for src, dst, index in loads:
        pltpu.make_async_copy(src, dst, local_sem.at[index]).start()
    for _, device in plane_peers():
        greet(device)
    for _, device in depth_peers():
        greet(device)

    near_bias[4] = key_bias[...]
    inner = jnp.minimum(lat, 1) + jnp.minimum(nlat - 1 - lat, 1)
    pl.semaphore_wait(barrier, NPEER + 2 * inner)

    feat_off = feat.at[0, core]
    feat_in = feat.at[0, 1 - core]
    s_off = 4 + 3 * core
    s_in = 7 - 3 * core
    t_off = 9 - 9 * core
    t_in = 9 * core
    b_off = 2 - 2 * core
    b_in = 2 * core

    def wide_copy(source, target, sent, landed, device):
        return remote(source, ext.at[target], wide_send.at[sent], wide_recv.at[landed], device)

    def near_copy(target, sent, landed, device):
        return remote(near_bias.at[4], near_bias.at[target], near_send.at[sent], near_recv.at[landed], device)

    def to_row(up):
        device = north if up else south
        corner = (lat - 1, off_lon) if up else (lat + 1, off_lon)
        inside = (corner[0], partner[1])
        step, row, sent, landed = (1, 2, 1, 2) if up else (-1, 0, 2, 1)
        wide_copy(feat_in, s_in + step, sent, landed, device).start()
        wide_copy(feat_off, t_off + row, sent, landed + 2, corner).start()
        wide_copy(feat_off, s_off + step, sent, landed + 2, device).start()
        near_copy(3 * row + 1, sent, landed, device).start()
        near_copy(3 * row + b_off, sent, landed, corner).start()
        near_copy(3 * row + b_in, sent, landed, inside).start()

    wide_copy(feat_in, t_in + 1, 0, 0, partner).start()
    wide_copy(feat_off, t_off + 1, 0, 0, off).start()
    near_copy(3 + b_in, 0, 0, partner).start()
    near_copy(3 + b_off, 0, 0, off).start()
    pl.when(lat == seam - 1)(lambda: to_row(False))
    pl.when(lat > 0)(lambda: to_row(True))
    pl.when((lat < nlat - 1) & (lat != seam - 1))(lambda: to_row(False))

    settle(ext.at[pl.ds(0, 2)], local_sem.at[0])
    settle(w_query, local_sem.at[1])
    settle(grad_rows, local_sem.at[2])
    settle(w_out, local_sem.at[3])
    settle(w_kv, local_sem.at[4])
    settle(neighbours, local_sem.at[5])
    settle(counts, local_sem.at[6])
    project(ext, grad_rows, w_query, w_out, w_kv, query, grad_att, key_value)

    def pass_on(row):
        landed = 1 + row // 2
        slot = s_in - 1 + row
        settle(ext.at[slot], wide_recv.at[landed])
        wide_copy(ext.at[slot], t_in + row, landed + 2, landed + 2, partner).start()

    def arrived(row):
        landed = 1 + row // 2
        settle(ext.at[pl.ds(0, 3)], wide_recv.at[landed + 2])
        settle(near_bias.at[pl.ds(0, 3)], near_recv.at[landed])

    pl.when(lat == seam - 1)(lambda: pass_on(0))
    pl.when(lat < nlat - 1)(lambda: pass_on(2))
    pl.when((lat > 0) & (lat != seam - 1))(lambda: pass_on(0))
    settle(ext.at[pl.ds(0, 2)], wide_recv.at[0])
    settle(near_bias.at[pl.ds(0, 2)], near_recv.at[0])
    pl.when(lat > 0)(lambda: arrived(0))
    pl.when(lat < nlat - 1)(lambda: arrived(2))
    heads = ext_bias.shape[1]
    for row in range(3):
        west_bias = near_bias[3 * row].astype(F32)
        own_bias = near_bias[3 * row + 1].astype(F32)
        east_bias = near_bias[3 * row + 2].astype(F32)
        ext_bias[row] = west_bias[heads:]
        ext_bias[3 + row] = own_bias[:heads]
        ext_bias[6 + row] = own_bias[heads:]
        ext_bias[9 + row] = east_bias[:heads]

    def core_copy(which):
        start, offset = ((2 - core, core), (3 - 3 * core, 1 - core))[which]
        count = NPEER // 2
        return remote(
            part.at[pl.ds(start * count, count)], from_core.at[pl.ds(offset * count, count)],
            core_send.at[which], core_recv.at[which], partner,
        )

    def send_part(which):
        core_copy(which).start()

    all_picks, grad_query = attend(
        neighbours, counts, ext, ext_bias, grad_rows, query, grad_att, key_value, part, send_part,
        w_kv, gathered, scores, grad_probs, probs_low, scores_low, grad_kv,
        attended_t, grad_query_t, bias_parts,
    )

    plane = pl.ds(0, NXY)
    depth = pl.ds(NXY, NZ)

    feature_parts(w_kv, grad_kv, feat_parts)
    core_copy(0).wait_recv()
    core_copy(1).wait_recv()
    half[...] = (part[pl.ds(base, NPEER)].astype(F32) + from_core[...].astype(F32)).astype(BF)

    for peer, device in depth_peers():
        remote(half.at[NXY + peer], from_first.at[NXY + z], first_send.at[1], first_recv.at[1], device).start()

    for peer, device in plane_peers():
        remote(half.at[peer], from_first.at[xy], first_send.at[0], first_recv.at[0], device).start()

    from_first[xy] = half[xy]
    from_first[NXY + z] = half[NXY + z]
    scatter(all_picks, grad_query, w_query, bias_parts, feat_parts, halo, own, bias_sum)
    for index in range(2):
        device = (west, east)[index]
        columns = pl.ds(9 * index, 3)
        remote(halo.at[columns], side.at[1 - index], side_send.at[0], side_recv.at[0], device).start()
        remote(bias_sum.at[columns], side_bias.at[1 - index], side_send.at[1], side_recv.at[1], device).start()

    settle(half.at[pl.ds(0, NZ - 1)], first_recv.at[1])
    mine[1] = jnp.sum(from_first[depth].astype(F32), axis=0).astype(BF)

    for peer, device in plane_peers():
        remote(mine.at[1], from_second.at[xy], second_send.at[1], second_recv.at[1], device).start()

    settle(half.at[pl.ds(0, NXY - 1)], first_recv.at[0])
    mine[0] = jnp.sum(from_first[plane].astype(F32), axis=0).astype(BF)

    for peer, device in depth_peers():
        remote(mine.at[0], from_second.at[NXY + z], second_send.at[0], second_recv.at[0], device).start()

    from_second[xy] = mine[1]
    from_second[NXY + z] = mine[0]

    def to_edge(index):
        device = (north, south)[index]
        landed = 2 - 2 * index
        remote(rows_out.at[index], edge.at[1 - index], edge_send.at[2 * index], edge_recv.at[landed], device).start()
        remote(rows_bias.at[index], edge_bias.at[1 - index], edge_send.at[2 * index + 1], edge_recv.at[landed + 1], device).start()

    def fold_columns():
        settle(side, side_recv.at[0])
        settle(side_bias, side_recv.at[1])
        for index in range(2):
            for j in range(2):
                slot = 3 * j + 3 + 2 * index
                rows_out[index, j] = (halo[slot].astype(F32) + side[j, 2 * index].astype(F32)).astype(BF)
                rows_bias[index, j] = bias_sum[slot] + side_bias[j, 2 * index]
        pl.when(lat == seam - 1)(lambda: to_edge(1))
        pl.when(lat > 0)(lambda: to_edge(0))
        pl.when((lat < nlat - 1) & (lat != seam - 1))(lambda: to_edge(1))

    wraps = (z == (NZ - 1) * core)
    pl.when(jnp.logical_not(wraps))(fold_columns)

    settle(half.at[pl.ds(0, NXY - 1)], second_recv.at[1])
    total[1] = jnp.sum(from_second[plane].astype(F32), axis=0).astype(BF)

    for peer, device in depth_peers():
        remote(total.at[1], summed.at[NXY + z], third_send.at[1], third_recv.at[1], device).start()

    summed[NXY + z] = total[1]
    pl.when(wraps)(fold_columns)
    settle(half.at[pl.ds(0, NZ - 1)], second_recv.at[0])
    total[0] = jnp.sum(from_second[depth].astype(F32), axis=0).astype(BF)

    for peer, device in plane_peers():
        remote(total.at[0], summed.at[xy], third_send.at[0], third_recv.at[0], device).start()

    summed[xy] = total[0]

    def fourth_copy(which):
        start, count = ((0, NXY), (NXY, NZ))[which]
        return remote(
            summed.at[pl.ds(start, count)], out.at[pl.ds(base + start, count)],
            fourth_send.at[0], fourth_recv.at[0], partner,
        )

    settle(half.at[pl.ds(0, NZ - 1)], third_recv.at[1])
    fourth_copy(1).start()
    settle(half.at[pl.ds(0, NXY - 1)], third_recv.at[0])
    fourth_copy(0).start()
    own_out = pltpu.make_async_copy(summed, out.at[pl.ds(base, NPEER)], out_sem.at[0])
    own_out.start()

    @pl.when(lat == 0)
    def _():
        edge[0] = jnp.zeros_like(edge[0])
        edge_bias[0] = jnp.zeros_like(edge_bias[0])

    @pl.when(lat == nlat - 1)
    def _():
        edge[1] = jnp.zeros_like(edge[1])
        edge_bias[1] = jnp.zeros_like(edge_bias[1])

    @pl.when(lat > 0)
    def _():
        settle(rows_out.at[0], edge_send.at[0])
        settle(rows_bias.at[0], edge_send.at[1])
        settle(edge.at[0], edge_recv.at[0])
        settle(edge_bias.at[0], edge_recv.at[1])

    @pl.when(lat < nlat - 1)
    def _():
        settle(rows_out.at[1], edge_send.at[2])
        settle(rows_bias.at[1], edge_send.at[3])
        settle(edge.at[1], edge_recv.at[2])
        settle(edge_bias.at[1], edge_recv.at[3])

    for j in range(2):
        total_grad = own[j] + side[j, 1].astype(F32) + (edge[0, j].astype(F32) + edge[1, j].astype(F32))
        grad_feat[j] = total_grad.astype(BF)
        grad_bias[j] = bias_sum[3 * j + 4] + side_bias[j, 1] + (edge_bias[0, j] + edge_bias[1, j])

    settle(ext.at[pl.ds(0, 2)], wide_send.at[0])
    settle(near_bias.at[pl.ds(0, 2)], near_send.at[0])

    @pl.when(lat > 0)
    def _():
        settle(ext.at[pl.ds(0, 3)], wide_send.at[1])
        settle(ext.at[0], wide_send.at[3])
        settle(near_bias.at[pl.ds(0, 3)], near_send.at[1])

    @pl.when(lat < nlat - 1)
    def _():
        settle(ext.at[pl.ds(0, 3)], wide_send.at[2])
        settle(ext.at[0], wide_send.at[4])
        settle(near_bias.at[pl.ds(0, 3)], near_send.at[2])

    core_copy(0).wait_send()
    core_copy(1).wait_send()
    settle(side, side_send.at[0])
    settle(side_bias, side_send.at[1])
    for sems, wide_index in ((first_send, 0), (second_send, 1), (third_send, 0)):
        settle(half.at[pl.ds(0, NXY - 1)], sems.at[wide_index])
        settle(half.at[pl.ds(0, NZ - 1)], sems.at[1 - wide_index])
    settle(half, fourth_send.at[0])
    settle(half, fourth_recv.at[0])
    own_out.wait()


def layer_call(neighbours, counts, feat, key_bias, grad_out, w_query, w_key, w_value, w_out):
    _, _, slots, chans = feat.shape
    heads = key_bias.shape[0] // 2
    blocks = 12
    entries = counts.shape[2]
    keys_all = entries * slots
    vmem = pl.BlockSpec(memory_space=pltpu.VMEM)
    hbm = pl.BlockSpec(memory_space=pl.ANY)
    low = lambda *shape: pltpu.VMEM(shape, BF)
    wide = lambda *shape: pltpu.VMEM(shape, F32)
    dma = pltpu.SemaphoreType.DMA
    return pl.pallas_call(
        layer_kernel,
        out_shape=[
            jax.ShapeDtypeStruct((2 * NPEER, ROWS, chans), BF),
            jax.ShapeDtypeStruct((2, slots, chans), BF),
            jax.ShapeDtypeStruct((2, heads, slots), F32),
        ],
        in_specs=[hbm] * 3 + [vmem] + [hbm] * 5,
        out_specs=[hbm, vmem, vmem],
        scratch_shapes=[
            pltpu.SMEM(neighbours.shape, jnp.int32),
            pltpu.SMEM(counts.shape, jnp.int32),
            low(blocks, slots, chans),
            low(9, 2 * heads, slots),
            wide(blocks, heads, slots),
            low(2, slots, chans),
            low(chans, chans),
            low(chans, chans),
            low(2, slots, chans),
            low(2, slots, chans),
            low(2 * keys_all, 2 * chans),
            low(2 * NPEER, ROWS, chans),
            low(blocks, slots, chans),
            wide(2, slots, chans),
            wide(blocks, heads, slots),
            wide(2, keys_all, chans),
            wide(2, entries, heads, slots),
            low(chans, 2 * chans),
            low(2, keys_all, chans),
            wide(4, keys_all, PAIR * slots),
            wide(4, keys_all, PAIR * slots),
            low(4, keys_all, PAIR * slots),
            low(4, keys_all, PAIR * slots),
            low(2 * keys_all, 2 * chans),
            low(chans, 2 * slots),
            low(chans, 2 * slots),
            low(NPEER, ROWS, chans),
            low(NPEER, ROWS, chans),
            low(NPEER, ROWS, chans),
            low(2, ROWS, chans),
            low(NPEER, ROWS, chans),
            low(2, ROWS, chans),
            low(NPEER, ROWS, chans),
            low(2, 3, slots, chans),
            wide(2, 3, heads, slots),
            low(2, 2, slots, chans),
            wide(2, 2, heads, slots),
            low(2, 2, slots, chans),
            wide(2, 2, heads, slots),
        ]
        + [dma((count,)) for count in (7, 1, 5, 5, 3, 3)]
        + [dma((count,)) for count in (2, 2, 2, 2, 2, 2, 2, 2, 1, 1, 2, 2, 4, 4)],
        compiler_params=pltpu.CompilerParams(collective_id=0, has_side_effects=True, vmem_limit_bytes=62 << 20),
        name="layer_backward",
    )(neighbours, counts, feat, key_bias, grad_out, w_query, w_key, w_value, w_out)


def finish_kernel(
    scale, low, grad_feat, grad_bias, feat_out, bias_out, w0, w1, w2, w3,
    packed, plain, feat_rows, bias_rows, load_sem, store_sem,
):
    weights = (w0, w1, w2, w3)
    chans = w0.shape[0]
    loads = [(low.at[pl.ds(chans * i, chans)], packed.at[i]) for i in range(4)]
    loads += [(grad_feat, feat_rows), (grad_bias, bias_rows)]
    loads = [pltpu.make_async_copy(src, dst, load_sem.at[i]) for i, (src, dst) in enumerate(loads)]
    for load in loads:
        load.start()
    stores = [(plain.at[i], weights[i]) for i in range(4)]
    stores += [(feat_rows, feat_out.at[0]), (bias_rows, bias_out.at[0])]
    stores = [pltpu.make_async_copy(src, dst, store_sem.at[i]) for i, (src, dst) in enumerate(stores)]
    for i in range(6):
        loads[i].wait()
        if i < 4:
            plain[i] = packed[i].astype(F32) * scale
        stores[i].start()
    for store in stores:
        store.wait()


def finish_call(low, grad_feat, grad_bias, scale):
    chans = low.shape[1]
    hbm = pl.BlockSpec(memory_space=pl.ANY)
    dma = pltpu.SemaphoreType.DMA
    weight = jax.ShapeDtypeStruct((chans, chans), F32)
    return pl.pallas_call(
        functools.partial(finish_kernel, scale),
        out_shape=[
            jax.ShapeDtypeStruct((1,) + grad_feat.shape, BF),
            jax.ShapeDtypeStruct((1,) + grad_bias.shape, F32),
        ]
        + [weight] * 4,
        in_specs=[hbm] * 3,
        out_specs=[hbm] * 6,
        scratch_shapes=[
            pltpu.VMEM((4, chans, chans), BF),
            pltpu.VMEM((4, chans, chans), F32),
            pltpu.VMEM(grad_feat.shape, BF),
            pltpu.VMEM(grad_bias.shape, F32),
            dma((6,)),
            dma((6,)),
        ],
        compiler_params=pltpu.CompilerParams(vmem_limit_bytes=62 << 20),
        name="scale_weights",
    )(low, grad_feat, grad_bias)


def per_device(
    features, w_query, w_key, w_value, w_out, key_bias, neighbours, key_counts, grad_out
):
    brows, bcols, slots, chans = features.shape
    heads = key_bias.shape[2]
    low, grad_features, grad_bias = layer_call(
        neighbours, key_counts, features, key_bias.reshape(bcols * heads, slots), grad_out,
        w_query, w_key, w_value, w_out,
    )
    cells = lax.axis_size("lat") * lax.axis_size("lon") * brows * bcols * slots
    return tuple(
        finish_call(low.reshape(4 * chans, chans), grad_features, grad_bias, float(cells) ** (-0.5))
    )


def solution(mesh):
    placed = (
        P("lat", "lon", None, None),
        P(),
        P(),
        P(),
        P(),
        P("lat", "lon", None, None),
        P("lat", "lon", None),
        P("lat", "lon", None),
        P("lat", "lon", None, None),
    )
    return jax.shard_map(
        per_device,
        mesh=mesh,
        in_specs=placed,
        out_specs=(P("lat", "lon", None, None), P("lat", "lon", None, None), P(), P(), P(), P()),
        check_vma=False,
    )
```

```python
import functools
import math

import jax
import jax.numpy as jnp
import numpy as np
from jax import lax
from jax.experimental import pallas as pl
from jax.experimental.pallas import tpu as pltpu
from jax.sharding import PartitionSpec as P

BF = jnp.bfloat16
F32 = jnp.float32
HEADS = 8
PAIR = 4
WINDOW = 256
NT = (((1,), (1,)), ((), ()))
TN = (((0,), (0,)), ((), ()))
FAR = -1e30


def bf16_parts(value, count):
    parts = []
    for _ in range(count):
        part = float(np.asarray(value, dtype=jnp.bfloat16).astype(np.float64))
        parts.append(part)
        value = value - part
    return parts


def mm(a, b, dims=None):
    if dims is None:
        return jnp.dot(a, b, preferred_element_type=F32)
    return lax.dot_general(a, b, dims, preferred_element_type=F32)


def project(ext, grad_rows, w_query, w_out, w_kv, query, grad_att, key_value):
    slots = ext.shape[1]
    entries = key_value.shape[0] // (2 * slots)
    for b in range(2):
        feat = ext[3 * b + 4]
        query[b] = mm(feat, w_query[...]).astype(BF)
        grad_att[b] = mm(grad_rows[b], w_out[...], NT).astype(BF)
        key_value[b * entries * slots:(b * entries + 1) * slots] = mm(feat, w_kv[...]).astype(BF)


def attend(
    neighbours, counts, ext, ext_bias, grad_out, query_all, grad_att_all, key_value, part, send_part,
    w_kv, gathered, scores, grad_probs, probs_low, scores_low, grad_kv,
    attended_t, grad_query_t, bias_parts,
):
    lat = lax.axis_index("lat")
    lon = lax.axis_index("lon")
    columns = 2 * lax.axis_size("lon")

    def local_slot(block):
        row = lax.div(block, columns) - lat + 1
        column = lax.rem(lax.rem(block, columns) - 2 * lon + 1 + columns, columns)
        return jnp.clip(column, 0, 3) * 3 + jnp.clip(row, 0, 2)

    slots, chans = ext.shape[1:]
    width = chans // HEADS
    entries = counts.shape[2]
    keys_all = entries * slots
    root = math.sqrt(width)
    parts = bf16_parts(root, 3)
    log2e = math.log2(math.e) / root
    lane = lax.broadcasted_iota(jnp.int32, (slots, WINDOW), 1)
    row = lax.broadcasted_iota(jnp.int32, (slots, WINDOW), 0)
    place_row = lax.broadcasted_iota(jnp.int32, (HEADS, WINDOW), 0)
    place_lane = lax.broadcasted_iota(jnp.int32, (HEADS, WINDOW), 1)
    wide_lane = lax.broadcasted_iota(jnp.int32, (keys_all, slots), 1)
    bias_all = [jnp.zeros((keys_all, slots), F32)] * 2
    state = {}

    def gather(b):
        picks = [local_slot(neighbours[0, b, e]) for e in range(entries)]
        gathered[b, 0:slots, :] = ext[3 * b + 4]
        for e in range(1, entries):
            gathered[b, e * slots:(e + 1) * slots, :] = ext[picks[e]]
        rest = pl.ds(b * keys_all + slots, keys_all - slots)
        key_value[rest, :] = mm(gathered[b, slots:], w_kv[...]).astype(BF)
        kv = key_value[pl.ds(b * keys_all, keys_all), :]
        bias_row = jnp.concatenate([ext_bias[picks[e]] for e in range(entries)], axis=1)
        return picks, query_all[b], grad_att_all[b], kv, bias_row

    def prepare(b, w):
        picks, query, grad_att, kv, bias_row = state[b]
        lo = w * (chans - WINDOW)
        first = PAIR * w
        spare = PAIR * width if w == 0 else 0
        region = (lane < PAIR * width) if w == 0 else (lane >= WINDOW - PAIR * width)
        place = jnp.zeros((HEADS, WINDOW), F32)
        for hh in range(PAIR):
            start = spare + 3 * hh
            place = jnp.where(
                (place_row == first + hh) & (place_lane >= start) & (place_lane < start + 3), 1.0, place
            )
        bias_cols = mm(bias_row, place, TN)
        key_aug = []
        for e in range(entries):
            cols = bias_cols[e * slots:(e + 1) * slots]
            cols = jnp.where((lane == spare + 3 * PAIR) & (row >= counts[0, b, e]), FAR, cols)
            piece = kv[e * slots:(e + 1) * slots, lo:lo + WINDOW]
            key_aug.append(jnp.where(region, piece.astype(F32), cols).astype(BF))
        key_aug = jnp.concatenate(key_aug, axis=0)
        value_win = kv[:, chans + lo:chans + lo + WINDOW]
        query_win = query[:, lo:lo + WINDOW].astype(F32)
        grad_win = grad_att[:, lo:lo + WINDOW].astype(F32)
        query_aug, grad_aug = [], []
        for hh in range(PAIR):
            inside = (lane >= (first + hh) * width - lo) & (lane < (first + hh + 1) * width - lo)
            const = jnp.where(lane == spare + 3 * PAIR, 1.0, 0.0)
            for t in range(3):
                const = jnp.where(lane == spare + 3 * hh + t, parts[t], const)
            query_aug.append(jnp.where(inside, query_win, const).astype(BF))
            grad_aug.append(jnp.where(inside, grad_win, 0.0).astype(BF))
        query_aug = jnp.concatenate(query_aug, axis=0)
        grad_aug = jnp.concatenate(grad_aug, axis=0)
        scores[2 * b + w] = mm(key_aug, query_aug, NT)
        grad_probs[2 * b + w] = mm(value_win, grad_aug, NT)
        return query_aug, grad_aug, lo, first, spare, region

    def soften(b, w):
        first = PAIR * w
        bias_sums = bias_all[b]
        for hh in range(PAIR):
            cut = pl.ds(hh * slots, slots)
            logits = scores[2 * b + w, :, cut]
            powers = jnp.exp2((logits - jnp.max(logits, axis=0, keepdims=True)) * log2e)
            probs = powers * (1.0 / jnp.sum(powers, axis=0, keepdims=True))
            probs_low[2 * b + w, :, cut] = probs.astype(BF)
            grads = grad_probs[2 * b + w, :, cut]
            centre = jnp.sum(probs * grads, axis=0, keepdims=True)
            full = probs * (grads - centre)
            high = full.astype(BF)
            scores_low[2 * b + w, :, cut] = high
            bias_sums = jnp.where(wide_lane == first + hh, jnp.sum(full, axis=1, keepdims=True), bias_sums)
        bias_all[b] = bias_sums

    def finish(b, w):
        picks, query, grad_att, kv, bias_row = state[b]
        query_aug, grad_aug, lo, first, spare, region = state[b, w]
        value_grad = mm(probs_low[2 * b + w], grad_aug)
        key_grad = mm(scores_low[2 * b + w], query_aug)
        scale = 1.0 / root
        base = b * keys_all
        rows = pl.ds(base, keys_all)
        half = WINDOW // 2
        edge = PAIR * width - half
        low_lane = lane[0:1, 0:half]
        if w == 0:
            grad_kv[rows, 0:half] = (key_grad[:, 0:half] * scale).astype(BF)
            grad_kv[rows, chans:chans + half] = value_grad[:, 0:half].astype(BF)
            state[b, 'saved'] = key_grad[:, half:], value_grad[:, half:]
        else:
            saved_key, saved_value = state[b, 'saved']
            middle = jnp.where(low_lane < edge, saved_key, key_grad[:, 0:half]) * scale
            grad_kv[rows, half:2 * half] = middle.astype(BF)
            grad_kv[rows, 2 * half:3 * half] = (key_grad[:, half:] * scale).astype(BF)
            middle = saved_value + value_grad[:, 0:half]
            grad_kv[rows, chans + half:chans + 2 * half] = middle.astype(BF)
            grad_kv[rows, chans + 2 * half:chans + 3 * half] = value_grad[:, half:].astype(BF)
        for pair in range(2):
            head = first + 2 * pair
            cut = pl.ds(2 * pair * slots, 2 * slots)
            value_rows = kv[:, chans + head * width:chans + (head + 2) * width]
            key_rows = kv[:, head * width:(head + 2) * width]
            both = mm(value_rows, probs_low[2 * b + w, :, cut], TN)
            attended_t[head * width:(head + 1) * width, b * slots:(b + 1) * slots] = both[:width, :slots].astype(BF)
            attended_t[(head + 1) * width:(head + 2) * width, b * slots:(b + 1) * slots] = both[width:, slots:].astype(BF)
            both = mm(key_rows, scores_low[2 * b + w, :, cut], TN) * scale
            grad_query_t[head * width:(head + 1) * width, b * slots:(b + 1) * slots] = both[:width, :slots].astype(BF)
            grad_query_t[(head + 1) * width:(head + 2) * width, b * slots:(b + 1) * slots] = both[width:, slots:].astype(BF)

    steps = [(0, 0), (0, 1), (1, 0), (1, 1)]
    state[0] = gather(0)
    state[0, 0] = prepare(0, 0)
    state[1] = gather(1)
    for i, step in enumerate(steps):
        if i + 1 < len(steps):
            state[steps[i + 1]] = prepare(*steps[i + 1])
        soften(*step)
        finish(*step)
    all_picks = [state[b][0] for b in range(2)]
    for b in range(2):
        for e in range(entries):
            bias_parts[b, e] = jnp.transpose(bias_all[b][e * slots:(e + 1) * slots])[:HEADS]
    grad_query = jnp.transpose(grad_query_t[...].astype(F32)).astype(BF)
    feat_both = jnp.concatenate([ext[4], ext[7]], axis=0)
    grad_both = grad_out[...].reshape(2 * slots, chans)
    piece = chans // ROWS

    def put(index, value):
        part[index * piece:(index + 1) * piece] = value.astype(BF).reshape(piece, ROWS, chans)

    weight_kv = mm(gathered[...].reshape(2 * keys_all, chans), grad_kv[...], TN)
    put(1, weight_kv[:, :chans])
    put(2, weight_kv[:, chans:])
    send_part(0)
    put(0, mm(feat_both, grad_query, TN))
    put(3, mm(attended_t[...], grad_both))
    send_part(1)
    return all_picks, grad_query


def feature_parts(w_kv, grad_kv, feat_parts):
    keys_all = feat_parts.shape[1]
    for b in range(2):
        feat_parts[b] = mm(grad_kv[pl.ds(b * keys_all, keys_all), :], w_kv[...], NT)


def scatter(all_picks, grad_query, w_query, bias_parts, feat_parts, halo, own, bias_sum):
    slots, chans = halo.shape[1:]
    entries = len(all_picks[0])
    query_part = mm(grad_query, w_query[...], NT)
    for slot in range(halo.shape[0]):
        column = slot // 3
        total, bias_total = None, None
        for b in range(2):
            if column - b not in (0, 1, 2):
                continue
            for e in range(1, entries):
                hit = all_picks[b][e] == slot
                piece = jnp.where(hit, feat_parts[b, e * slots:(e + 1) * slots], 0.0)
                total = piece if total is None else total + piece
                piece = jnp.where(hit, bias_parts[b, e], 0.0)
                bias_total = piece if bias_total is None else bias_total + piece
        if slot in (4, 7):
            b = column - 1
            own[b] = total + (feat_parts[b, 0:slots] + query_part[b * slots:(b + 1) * slots])
            bias_total = bias_total + bias_parts[b, 0]
        else:
            halo[slot] = total.astype(BF)
        bias_sum[slot] = bias_total


MESH = pl.DeviceIdType.MESH
NXY = 16
NZ = 8
NPEER = NXY + NZ
ROWS = 32


def ring(offset, size):
    return min(offset, size - offset)


PLANE = sorted(
    [(dx, dy) for dx in range(4) for dy in range(4) if dx or dy],
    key=lambda o: -(ring(o[0], 4) + ring(o[1], 4)),
)
DEPTH = sorted(range(1, NZ), key=lambda o: -ring(o, NZ))


def remote(src, dst, send_sem, recv_sem, device):
    return pltpu.make_async_remote_copy(
        src_ref=src, dst_ref=dst, send_sem=send_sem, recv_sem=recv_sem,
        device_id=device, device_id_type=MESH,
    )


def layer_kernel(
    neighbours_hbm, counts_hbm, feat, key_bias, grad_out, w_query_hbm, w_key_hbm, w_value_hbm, w_out_hbm,
    out, grad_feat, grad_bias,
    neighbours, counts, ext, near_bias, ext_bias, grad_rows, w_query, w_out, query, grad_att, key_value,
    part, halo, own, bias_sum, feat_parts, bias_parts, w_kv, gathered, scores, grad_probs, probs_low,
    scores_low, grad_kv, attended_t, grad_query_t,
    from_core, half, from_first, mine, from_second, total, summed,
    side, side_bias, rows_out, rows_bias, edge, edge_bias,
    local_sem, out_sem, wide_send, wide_recv, near_send, near_recv,
    core_send, core_recv, first_send, first_recv, second_send, second_recv,
    third_send, third_recv, fourth_send, fourth_recv, side_send, side_recv, edge_send, edge_recv,
):
    lat = lax.axis_index("lat")
    lon = lax.axis_index("lon")
    core = lon % 2
    z = (lon // 2) % NZ
    x_lo = lon // (2 * NZ)
    x_hi = lat // 4
    y = lat % 4
    xy = (x_hi * 2 + x_lo) * 4 + y
    partner = (lat, lon + 1 - 2 * core)
    nlat = lax.axis_size("lat")
    nlon = lax.axis_size("lon")
    east = (lat, (lon + 1) % nlon)
    west = (lat, (lon + nlon - 1) % nlon)
    north = (lat - 1, lon)
    south = (lat + 1, lon)
    base = core * NPEER
    other = (1 - core) * NPEER

    off_lon = (lon + nlon - 1 + 2 * core) % nlon
    off = (lat, off_lon)
    seam = nlat // 2

    x = x_hi * 2 + x_lo

    def plane_peers():
        for dx, dy in PLANE:
            px = (x + dx) % 4
            py = (y + dy) % 4
            yield px * 4 + py, ((px // 2) * 4 + py, (px % 2) * (2 * NZ) + z * 2 + core)

    def depth_peers():
        for dz in DEPTH:
            pz = (z + dz) % NZ
            yield pz, (lat, x_lo * (2 * NZ) + pz * 2 + core)

    barrier = pltpu.get_barrier_semaphore()

    def greet(device):
        pl.semaphore_signal(barrier, inc=1, device_id=device, device_id_type=MESH)

    def settle(like, sem):
        pltpu.make_async_copy(like, like, sem).wait()

    chans = feat.shape[3]
    loads = [
        (feat.at[0, 0], ext.at[4], 0),
        (feat.at[0, 1], ext.at[7], 0),
        (w_query_hbm, w_query, 1),
        (grad_out.at[0], grad_rows, 2),
        (w_out_hbm, w_out, 3),
        (w_key_hbm, w_kv.at[:, pl.ds(0, chans)], 4),
        (w_value_hbm, w_kv.at[:, pl.ds(chans, chans)], 4),
        (neighbours_hbm, neighbours, 5),
        (counts_hbm, counts, 6),
    ]
    greet(partner)
    greet(off)

    @pl.when(lat > 0)
    def _():
        greet((lat - 1, off_lon))
        greet((lat - 1, partner[1]))

    @pl.when(lat < nlat - 1)
    def _():
        greet((lat + 1, off_lon))
        greet((lat + 1, partner[1]))

    for src, dst, index in loads:
        pltpu.make_async_copy(src, dst, local_sem.at[index]).start()
    for _, device in plane_peers():
        greet(device)
    for _, device in depth_peers():
        greet(device)

    near_bias[4] = key_bias[...]
    inner = jnp.minimum(lat, 1) + jnp.minimum(nlat - 1 - lat, 1)
    pl.semaphore_wait(barrier, NPEER + 2 * inner)

    feat_off = feat.at[0, core]
    feat_in = feat.at[0, 1 - core]
    s_off = 4 + 3 * core
    s_in = 7 - 3 * core
    t_off = 9 - 9 * core
    t_in = 9 * core
    b_off = 2 - 2 * core
    b_in = 2 * core

    def wide_copy(source, target, sent, landed, device):
        return remote(source, ext.at[target], wide_send.at[sent], wide_recv.at[landed], device)

    def near_copy(target, sent, landed, device):
        return remote(near_bias.at[4], near_bias.at[target], near_send.at[sent], near_recv.at[landed], device)

    def to_row(up):
        device = north if up else south
        corner = (lat - 1, off_lon) if up else (lat + 1, off_lon)
        inside = (corner[0], partner[1])
        step, row, sent, landed = (1, 2, 1, 2) if up else (-1, 0, 2, 1)
        wide_copy(feat_in, s_in + step, sent, landed, device).start()
        wide_copy(feat_off, t_off + row, sent, landed + 2, corner).start()
        wide_copy(feat_off, s_off + step, sent, landed + 2, device).start()
        near_copy(3 * row + 1, sent, landed, device).start()
        near_copy(3 * row + b_off, sent, landed, corner).start()
        near_copy(3 * row + b_in, sent, landed, inside).start()

    wide_copy(feat_in, t_in + 1, 0, 0, partner).start()
    wide_copy(feat_off, t_off + 1, 0, 0, off).start()
    near_copy(3 + b_in, 0, 0, partner).start()
    near_copy(3 + b_off, 0, 0, off).start()
    pl.when(lat == seam - 1)(lambda: to_row(False))
    pl.when(lat > 0)(lambda: to_row(True))
    pl.when((lat < nlat - 1) & (lat != seam - 1))(lambda: to_row(False))

    settle(ext.at[pl.ds(0, 2)], local_sem.at[0])
    settle(w_query, local_sem.at[1])
    settle(grad_rows, local_sem.at[2])
    settle(w_out, local_sem.at[3])
    settle(w_kv, local_sem.at[4])
    settle(neighbours, local_sem.at[5])
    settle(counts, local_sem.at[6])
    project(ext, grad_rows, w_query, w_out, w_kv, query, grad_att, key_value)

    def pass_on(row):
        landed = 1 + row // 2
        slot = s_in - 1 + row
        settle(ext.at[slot], wide_recv.at[landed])
        wide_copy(ext.at[slot], t_in + row, landed + 2, landed + 2, partner).start()

    def arrived(row):
        landed = 1 + row // 2
        settle(ext.at[pl.ds(0, 3)], wide_recv.at[landed + 2])
        settle(near_bias.at[pl.ds(0, 3)], near_recv.at[landed])

    pl.when(lat == seam - 1)(lambda: pass_on(0))
    pl.when(lat < nlat - 1)(lambda: pass_on(2))
    pl.when((lat > 0) & (lat != seam - 1))(lambda: pass_on(0))
    settle(ext.at[pl.ds(0, 2)], wide_recv.at[0])
    settle(near_bias.at[pl.ds(0, 2)], near_recv.at[0])
    pl.when(lat > 0)(lambda: arrived(0))
    pl.when(lat < nlat - 1)(lambda: arrived(2))
    heads = ext_bias.shape[1]
    for row in range(3):
        west_bias = near_bias[3 * row].astype(F32)
        own_bias = near_bias[3 * row + 1].astype(F32)
        east_bias = near_bias[3 * row + 2].astype(F32)
        ext_bias[row] = west_bias[heads:]
        ext_bias[3 + row] = own_bias[:heads]
        ext_bias[6 + row] = own_bias[heads:]
        ext_bias[9 + row] = east_bias[:heads]

    def core_copy(which):
        start, offset = ((2 - core, core), (3 - 3 * core, 1 - core))[which]
        count = NPEER // 2
        return remote(
            part.at[pl.ds(start * count, count)], from_core.at[pl.ds(offset * count, count)],
            core_send.at[which], core_recv.at[which], partner,
        )

    def send_part(which):
        core_copy(which).start()

    all_picks, grad_query = attend(
        neighbours, counts, ext, ext_bias, grad_rows, query, grad_att, key_value, part, send_part,
        w_kv, gathered, scores, grad_probs, probs_low, scores_low, grad_kv,
        attended_t, grad_query_t, bias_parts,
    )

    plane = pl.ds(0, NXY)
    depth = pl.ds(NXY, NZ)

    feature_parts(w_kv, grad_kv, feat_parts)
    core_copy(0).wait_recv()
    core_copy(1).wait_recv()
    half[...] = (part[pl.ds(base, NPEER)].astype(F32) + from_core[...].astype(F32)).astype(BF)

    for peer, device in depth_peers():
        remote(half.at[NXY + peer], from_first.at[NXY + z], first_send.at[1], first_recv.at[1], device).start()

    for peer, device in plane_peers():
        remote(half.at[peer], from_first.at[xy], first_send.at[0], first_recv.at[0], device).start()

    from_first[xy] = half[xy]
    from_first[NXY + z] = half[NXY + z]
    scatter(all_picks, grad_query, w_query, bias_parts, feat_parts, halo, own, bias_sum)
    for index in range(2):
        device = (west, east)[index]
        columns = pl.ds(9 * index, 3)
        remote(halo.at[columns], side.at[1 - index], side_send.at[0], side_recv.at[0], device).start()
        remote(bias_sum.at[columns], side_bias.at[1 - index], side_send.at[1], side_recv.at[1], device).start()

    settle(half.at[pl.ds(0, NZ - 1)], first_recv.at[1])
    mine[1] = jnp.sum(from_first[depth].astype(F32), axis=0).astype(BF)

    for peer, device in plane_peers():
        remote(mine.at[1], from_second.at[xy], second_send.at[1], second_recv.at[1], device).start()

    settle(half.at[pl.ds(0, NXY - 1)], first_recv.at[0])
    mine[0] = jnp.sum(from_first[plane].astype(F32), axis=0).astype(BF)

    for peer, device in depth_peers():
        remote(mine.at[0], from_second.at[NXY + z], second_send.at[0], second_recv.at[0], device).start()

    from_second[xy] = mine[1]
    from_second[NXY + z] = mine[0]

    def to_edge(index):
        device = (north, south)[index]
        landed = 2 - 2 * index
        remote(rows_out.at[index], edge.at[1 - index], edge_send.at[2 * index], edge_recv.at[landed], device).start()
        remote(rows_bias.at[index], edge_bias.at[1 - index], edge_send.at[2 * index + 1], edge_recv.at[landed + 1], device).start()

    def fold_columns():
        settle(side, side_recv.at[0])
        settle(side_bias, side_recv.at[1])
        for index in range(2):
            for j in range(2):
                slot = 3 * j + 3 + 2 * index
                rows_out[index, j] = (halo[slot].astype(F32) + side[j, 2 * index].astype(F32)).astype(BF)
                rows_bias[index, j] = bias_sum[slot] + side_bias[j, 2 * index]
        pl.when(lat == seam - 1)(lambda: to_edge(1))
        pl.when(lat > 0)(lambda: to_edge(0))
        pl.when((lat < nlat - 1) & (lat != seam - 1))(lambda: to_edge(1))

    wraps = (z == (NZ - 1) * core)
    pl.when(jnp.logical_not(wraps))(fold_columns)

    settle(half.at[pl.ds(0, NXY - 1)], second_recv.at[1])
    total[1] = jnp.sum(from_second[plane].astype(F32), axis=0).astype(BF)

    for peer, device in depth_peers():
        remote(total.at[1], summed.at[NXY + z], third_send.at[1], third_recv.at[1], device).start()

    summed[NXY + z] = total[1]
    settle(half.at[pl.ds(0, NZ - 1)], second_recv.at[0])
    total[0] = jnp.sum(from_second[depth].astype(F32), axis=0).astype(BF)

    for peer, device in plane_peers():
        remote(total.at[0], summed.at[xy], third_send.at[0], third_recv.at[0], device).start()

    summed[xy] = total[0]
    pl.when(wraps)(fold_columns)

    def fourth_copy(which):
        start, count = ((0, NXY), (NXY, NZ))[which]
        return remote(
            summed.at[pl.ds(start, count)], out.at[pl.ds(base + start, count)],
            fourth_send.at[0], fourth_recv.at[0], partner,
        )

    settle(half.at[pl.ds(0, NZ - 1)], third_recv.at[1])
    fourth_copy(1).start()
    settle(half.at[pl.ds(0, NXY - 1)], third_recv.at[0])
    fourth_copy(0).start()
    own_out = pltpu.make_async_copy(summed, out.at[pl.ds(base, NPEER)], out_sem.at[0])
    own_out.start()

    @pl.when(lat == 0)
    def _():
        edge[0] = jnp.zeros_like(edge[0])
        edge_bias[0] = jnp.zeros_like(edge_bias[0])

    @pl.when(lat == nlat - 1)
    def _():
        edge[1] = jnp.zeros_like(edge[1])
        edge_bias[1] = jnp.zeros_like(edge_bias[1])

    @pl.when(lat > 0)
    def _():
        settle(rows_out.at[0], edge_send.at[0])
        settle(rows_bias.at[0], edge_send.at[1])
        settle(edge.at[0], edge_recv.at[0])
        settle(edge_bias.at[0], edge_recv.at[1])

    @pl.when(lat < nlat - 1)
    def _():
        settle(rows_out.at[1], edge_send.at[2])
        settle(rows_bias.at[1], edge_send.at[3])
        settle(edge.at[1], edge_recv.at[2])
        settle(edge_bias.at[1], edge_recv.at[3])

    for j in range(2):
        total_grad = own[j] + side[j, 1].astype(F32) + (edge[0, j].astype(F32) + edge[1, j].astype(F32))
        grad_feat[j] = total_grad.astype(BF)
        grad_bias[j] = bias_sum[3 * j + 4] + side_bias[j, 1] + (edge_bias[0, j] + edge_bias[1, j])

    settle(ext.at[pl.ds(0, 2)], wide_send.at[0])
    settle(near_bias.at[pl.ds(0, 2)], near_send.at[0])

    @pl.when(lat > 0)
    def _():
        settle(ext.at[pl.ds(0, 3)], wide_send.at[1])
        settle(ext.at[0], wide_send.at[3])
        settle(near_bias.at[pl.ds(0, 3)], near_send.at[1])

    @pl.when(lat < nlat - 1)
    def _():
        settle(ext.at[pl.ds(0, 3)], wide_send.at[2])
        settle(ext.at[0], wide_send.at[4])
        settle(near_bias.at[pl.ds(0, 3)], near_send.at[2])

    core_copy(0).wait_send()
    core_copy(1).wait_send()
    settle(side, side_send.at[0])
    settle(side_bias, side_send.at[1])
    for sems, wide_index in ((first_send, 0), (second_send, 1), (third_send, 0)):
        settle(half.at[pl.ds(0, NXY - 1)], sems.at[wide_index])
        settle(half.at[pl.ds(0, NZ - 1)], sems.at[1 - wide_index])
    settle(half, fourth_send.at[0])
    settle(half, fourth_recv.at[0])
    own_out.wait()


def layer_call(neighbours, counts, feat, key_bias, grad_out, w_query, w_key, w_value, w_out):
    _, _, slots, chans = feat.shape
    heads = key_bias.shape[0] // 2
    blocks = 12
    entries = counts.shape[2]
    keys_all = entries * slots
    vmem = pl.BlockSpec(memory_space=pltpu.VMEM)
    hbm = pl.BlockSpec(memory_space=pl.ANY)
    low = lambda *shape: pltpu.VMEM(shape, BF)
    wide = lambda *shape: pltpu.VMEM(shape, F32)
    dma = pltpu.SemaphoreType.DMA
    return pl.pallas_call(
        layer_kernel,
        out_shape=[
            jax.ShapeDtypeStruct((2 * NPEER, ROWS, chans), BF),
            jax.ShapeDtypeStruct((2, slots, chans), BF),
            jax.ShapeDtypeStruct((2, heads, slots), F32),
        ],
        in_specs=[hbm] * 3 + [vmem] + [hbm] * 5,
        out_specs=[hbm, vmem, vmem],
        scratch_shapes=[
            pltpu.SMEM(neighbours.shape, jnp.int32),
            pltpu.SMEM(counts.shape, jnp.int32),
            low(blocks, slots, chans),
            low(9, 2 * heads, slots),
            wide(blocks, heads, slots),
            low(2, slots, chans),
            low(chans, chans),
            low(chans, chans),
            low(2, slots, chans),
            low(2, slots, chans),
            low(2 * keys_all, 2 * chans),
            low(2 * NPEER, ROWS, chans),
            low(blocks, slots, chans),
            wide(2, slots, chans),
            wide(blocks, heads, slots),
            wide(2, keys_all, chans),
            wide(2, entries, heads, slots),
            low(chans, 2 * chans),
            low(2, keys_all, chans),
            wide(4, keys_all, PAIR * slots),
            wide(4, keys_all, PAIR * slots),
            low(4, keys_all, PAIR * slots),
            low(4, keys_all, PAIR * slots),
            low(2 * keys_all, 2 * chans),
            low(chans, 2 * slots),
            low(chans, 2 * slots),
            low(NPEER, ROWS, chans),
            low(NPEER, ROWS, chans),
            low(NPEER, ROWS, chans),
            low(2, ROWS, chans),
            low(NPEER, ROWS, chans),
            low(2, ROWS, chans),
            low(NPEER, ROWS, chans),
            low(2, 3, slots, chans),
            wide(2, 3, heads, slots),
            low(2, 2, slots, chans),
            wide(2, 2, heads, slots),
            low(2, 2, slots, chans),
            wide(2, 2, heads, slots),
        ]
        + [dma((count,)) for count in (7, 1, 5, 5, 3, 3)]
        + [dma((count,)) for count in (2, 2, 2, 2, 2, 2, 2, 2, 1, 1, 2, 2, 4, 4)],
        compiler_params=pltpu.CompilerParams(collective_id=0, has_side_effects=True, vmem_limit_bytes=62 << 20),
        name="layer_backward",
    )(neighbours, counts, feat, key_bias, grad_out, w_query, w_key, w_value, w_out)


def finish_kernel(
    scale, low, grad_feat, grad_bias, feat_out, bias_out, w0, w1, w2, w3,
    packed, plain, feat_rows, bias_rows, load_sem, store_sem,
):
    weights = (w0, w1, w2, w3)
    chans = w0.shape[0]
    loads = [(low.at[pl.ds(chans * i, chans)], packed.at[i]) for i in range(4)]
    loads += [(grad_feat, feat_rows), (grad_bias, bias_rows)]
    loads = [pltpu.make_async_copy(src, dst, load_sem.at[i]) for i, (src, dst) in enumerate(loads)]
    for load in loads:
        load.start()
    stores = [(plain.at[i], weights[i]) for i in range(4)]
    stores += [(feat_rows, feat_out.at[0]), (bias_rows, bias_out.at[0])]
    stores = [pltpu.make_async_copy(src, dst, store_sem.at[i]) for i, (src, dst) in enumerate(stores)]
    for i in range(6):
        loads[i].wait()
        if i < 4:
            plain[i] = packed[i].astype(F32) * scale
        stores[i].start()
    for store in stores:
        store.wait()


def finish_call(low, grad_feat, grad_bias, scale):
    chans = low.shape[1]
    hbm = pl.BlockSpec(memory_space=pl.ANY)
    dma = pltpu.SemaphoreType.DMA
    weight = jax.ShapeDtypeStruct((chans, chans), F32)
    return pl.pallas_call(
        functools.partial(finish_kernel, scale),
        out_shape=[
            jax.ShapeDtypeStruct((1,) + grad_feat.shape, BF),
            jax.ShapeDtypeStruct((1,) + grad_bias.shape, F32),
        ]
        + [weight] * 4,
        in_specs=[hbm] * 3,
        out_specs=[hbm] * 6,
        scratch_shapes=[
            pltpu.VMEM((4, chans, chans), BF),
            pltpu.VMEM((4, chans, chans), F32),
            pltpu.VMEM(grad_feat.shape, BF),
            pltpu.VMEM(grad_bias.shape, F32),
            dma((6,)),
            dma((6,)),
        ],
        compiler_params=pltpu.CompilerParams(vmem_limit_bytes=62 << 20),
        name="scale_weights",
    )(low, grad_feat, grad_bias)


def per_device(
    features, w_query, w_key, w_value, w_out, key_bias, neighbours, key_counts, grad_out
):
    brows, bcols, slots, chans = features.shape
    heads = key_bias.shape[2]
    low, grad_features, grad_bias = layer_call(
        neighbours, key_counts, features, key_bias.reshape(bcols * heads, slots), grad_out,
        w_query, w_key, w_value, w_out,
    )
    cells = lax.axis_size("lat") * lax.axis_size("lon") * brows * bcols * slots
    return tuple(
        finish_call(low.reshape(4 * chans, chans), grad_features, grad_bias, float(cells) ** (-0.5))
    )


def solution(mesh):
    placed = (
        P("lat", "lon", None, None),
        P(),
        P(),
        P(),
        P(),
        P("lat", "lon", None, None),
        P("lat", "lon", None),
        P("lat", "lon", None),
        P("lat", "lon", None, None),
    )
    return jax.shard_map(
        per_device,
        mesh=mesh,
        in_specs=placed,
        out_specs=(P("lat", "lon", None, None), P("lat", "lon", None, None), P(), P(), P(), P()),
        check_vma=False,
    )
```

```python
import functools
import math

import jax
import jax.numpy as jnp
import numpy as np
from jax import lax
from jax.experimental import pallas as pl
from jax.experimental.pallas import tpu as pltpu
from jax.sharding import PartitionSpec as P

BF = jnp.bfloat16
F32 = jnp.float32
HEADS = 8
PAIR = 4
WINDOW = 256
NT = (((1,), (1,)), ((), ()))
TN = (((0,), (0,)), ((), ()))
FAR = -1e30


def bf16_parts(value, count):
    parts = []
    for _ in range(count):
        part = float(np.asarray(value, dtype=jnp.bfloat16).astype(np.float64))
        parts.append(part)
        value = value - part
    return parts


def mm(a, b, dims=None):
    if dims is None:
        return jnp.dot(a, b, preferred_element_type=F32)
    return lax.dot_general(a, b, dims, preferred_element_type=F32)


def project(ext, grad_rows, w_query, w_out, w_kv, query, grad_att, key_value):
    slots = ext.shape[1]
    entries = key_value.shape[0] // (2 * slots)
    for b in range(2):
        feat = ext[3 * b + 4]
        query[b] = mm(feat, w_query[...]).astype(BF)
        grad_att[b] = mm(grad_rows[b], w_out[...], NT).astype(BF)
        key_value[b * entries * slots:(b * entries + 1) * slots] = mm(feat, w_kv[...]).astype(BF)


def attend(
    neighbours, counts, ext, ext_bias, grad_out, query_all, grad_att_all, key_value, part, send_part,
    w_kv, gathered, scores, grad_probs, probs_low, scores_low, grad_kv,
    attended_t, grad_query_t, bias_parts,
):
    lat = lax.axis_index("lat")
    lon = lax.axis_index("lon")
    columns = 2 * lax.axis_size("lon")

    def local_slot(block):
        row = lax.div(block, columns) - lat + 1
        column = lax.rem(lax.rem(block, columns) - 2 * lon + 1 + columns, columns)
        return jnp.clip(column, 0, 3) * 3 + jnp.clip(row, 0, 2)

    slots, chans = ext.shape[1:]
    width = chans // HEADS
    entries = counts.shape[2]
    keys_all = entries * slots
    root = math.sqrt(width)
    parts = bf16_parts(root, 3)
    log2e = math.log2(math.e) / root
    lane = lax.broadcasted_iota(jnp.int32, (slots, WINDOW), 1)
    row = lax.broadcasted_iota(jnp.int32, (slots, WINDOW), 0)
    place_row = lax.broadcasted_iota(jnp.int32, (HEADS, WINDOW), 0)
    place_lane = lax.broadcasted_iota(jnp.int32, (HEADS, WINDOW), 1)
    wide_lane = lax.broadcasted_iota(jnp.int32, (keys_all, slots), 1)
    bias_all = [jnp.zeros((keys_all, slots), F32)] * 2
    state = {}

    def gather(b):
        picks = [local_slot(neighbours[0, b, e]) for e in range(entries)]
        gathered[b, 0:slots, :] = ext[3 * b + 4]
        for e in range(1, entries):
            gathered[b, e * slots:(e + 1) * slots, :] = ext[picks[e]]
        rest = pl.ds(b * keys_all + slots, keys_all - slots)
        key_value[rest, :] = mm(gathered[b, slots:], w_kv[...]).astype(BF)
        kv = key_value[pl.ds(b * keys_all, keys_all), :]
        bias_row = jnp.concatenate([ext_bias[picks[e]] for e in range(entries)], axis=1)
        return picks, query_all[b], grad_att_all[b], kv, bias_row

    def prepare(b, w):
        picks, query, grad_att, kv, bias_row = state[b]
        lo = w * (chans - WINDOW)
        first = PAIR * w
        spare = PAIR * width if w == 0 else 0
        region = (lane < PAIR * width) if w == 0 else (lane >= WINDOW - PAIR * width)
        place = jnp.zeros((HEADS, WINDOW), F32)
        for hh in range(PAIR):
            start = spare + 3 * hh
            place = jnp.where(
                (place_row == first + hh) & (place_lane >= start) & (place_lane < start + 3), 1.0, place
            )
        bias_cols = mm(bias_row, place, TN)
        key_aug = []
        for e in range(entries):
            cols = bias_cols[e * slots:(e + 1) * slots]
            cols = jnp.where((lane == spare + 3 * PAIR) & (row >= counts[0, b, e]), FAR, cols)
            piece = kv[e * slots:(e + 1) * slots, lo:lo + WINDOW]
            key_aug.append(jnp.where(region, piece.astype(F32), cols).astype(BF))
        key_aug = jnp.concatenate(key_aug, axis=0)
        value_win = kv[:, chans + lo:chans + lo + WINDOW]
        query_win = query[:, lo:lo + WINDOW].astype(F32)
        grad_win = grad_att[:, lo:lo + WINDOW].astype(F32)
        query_aug, grad_aug = [], []
        for hh in range(PAIR):
            inside = (lane >= (first + hh) * width - lo) & (lane < (first + hh + 1) * width - lo)
            const = jnp.where(lane == spare + 3 * PAIR, 1.0, 0.0)
            for t in range(3):
                const = jnp.where(lane == spare + 3 * hh + t, parts[t], const)
            query_aug.append(jnp.where(inside, query_win, const).astype(BF))
            grad_aug.append(jnp.where(inside, grad_win, 0.0).astype(BF))
        query_aug = jnp.concatenate(query_aug, axis=0)
        grad_aug = jnp.concatenate(grad_aug, axis=0)
        scores[2 * b + w] = mm(key_aug, query_aug, NT)
        grad_probs[2 * b + w] = mm(value_win, grad_aug, NT)
        return query_aug, grad_aug, lo, first, spare, region

    def soften(b, w):
        first = PAIR * w
        bias_sums = bias_all[b]
        for hh in range(PAIR):
            cut = pl.ds(hh * slots, slots)
            logits = scores[2 * b + w, :, cut]
            powers = jnp.exp2((logits - jnp.max(logits, axis=0, keepdims=True)) * log2e)
            probs = powers * (1.0 / jnp.sum(powers, axis=0, keepdims=True))
            probs_low[2 * b + w, :, cut] = probs.astype(BF)
            grads = grad_probs[2 * b + w, :, cut]
            centre = jnp.sum(probs * grads, axis=0, keepdims=True)
            full = probs * (grads - centre)
            high = full.astype(BF)
            scores_low[2 * b + w, :, cut] = high
            bias_sums = jnp.where(wide_lane == first + hh, jnp.sum(full, axis=1, keepdims=True), bias_sums)
        bias_all[b] = bias_sums

    def finish(b, w):
        picks, query, grad_att, kv, bias_row = state[b]
        query_aug, grad_aug, lo, first, spare, region = state[b, w]
        value_grad = mm(probs_low[2 * b + w], grad_aug)
        key_grad = mm(scores_low[2 * b + w], query_aug)
        scale = 1.0 / root
        base = b * keys_all
        rows = pl.ds(base, keys_all)
        half = WINDOW // 2
        edge = PAIR * width - half
        low_lane = lane[0:1, 0:half]
        if w == 0:
            grad_kv[rows, 0:half] = (key_grad[:, 0:half] * scale).astype(BF)
            grad_kv[rows, chans:chans + half] = value_grad[:, 0:half].astype(BF)
            state[b, 'saved'] = key_grad[:, half:], value_grad[:, half:]
        else:
            saved_key, saved_value = state[b, 'saved']
            middle = jnp.where(low_lane < edge, saved_key, key_grad[:, 0:half]) * scale
            grad_kv[rows, half:2 * half] = middle.astype(BF)
            grad_kv[rows, 2 * half:3 * half] = (key_grad[:, half:] * scale).astype(BF)
            middle = saved_value + value_grad[:, 0:half]
            grad_kv[rows, chans + half:chans + 2 * half] = middle.astype(BF)
            grad_kv[rows, chans + 2 * half:chans + 3 * half] = value_grad[:, half:].astype(BF)
        for pair in range(2):
            head = first + 2 * pair
            cut = pl.ds(2 * pair * slots, 2 * slots)
            value_rows = kv[:, chans + head * width:chans + (head + 2) * width]
            key_rows = kv[:, head * width:(head + 2) * width]
            both = mm(value_rows, probs_low[2 * b + w, :, cut], TN)
            attended_t[head * width:(head + 1) * width, b * slots:(b + 1) * slots] = both[:width, :slots].astype(BF)
            attended_t[(head + 1) * width:(head + 2) * width, b * slots:(b + 1) * slots] = both[width:, slots:].astype(BF)
            both = mm(key_rows, scores_low[2 * b + w, :, cut], TN) * scale
            grad_query_t[head * width:(head + 1) * width, b * slots:(b + 1) * slots] = both[:width, :slots].astype(BF)
            grad_query_t[(head + 1) * width:(head + 2) * width, b * slots:(b + 1) * slots] = both[width:, slots:].astype(BF)

    steps = [(0, 0), (0, 1), (1, 0), (1, 1)]
    state[0] = gather(0)
    state[0, 0] = prepare(0, 0)
    state[1] = gather(1)
    for i, step in enumerate(steps):
        if i + 1 < len(steps):
            state[steps[i + 1]] = prepare(*steps[i + 1])
        soften(*step)
        finish(*step)
    all_picks = [state[b][0] for b in range(2)]
    for b in range(2):
        for e in range(entries):
            bias_parts[b, e] = jnp.transpose(bias_all[b][e * slots:(e + 1) * slots])[:HEADS]
    grad_query = jnp.transpose(grad_query_t[...].astype(F32)).astype(BF)
    feat_both = jnp.concatenate([ext[4], ext[7]], axis=0)
    grad_both = grad_out[...].reshape(2 * slots, chans)
    piece = chans // ROWS

    def put(index, value):
        part[index * piece:(index + 1) * piece] = value.astype(BF).reshape(piece, ROWS, chans)

    weight_kv = mm(gathered[...].reshape(2 * keys_all, chans), grad_kv[...], TN)
    put(1, weight_kv[:, :chans])
    put(2, weight_kv[:, chans:])
    send_part(0)
    put(0, mm(feat_both, grad_query, TN))
    put(3, mm(attended_t[...], grad_both))
    send_part(1)
    return all_picks, grad_query


def feature_parts(w_kv, grad_kv, feat_parts):
    keys_all = feat_parts.shape[1]
    for b in range(2):
        feat_parts[b] = mm(grad_kv[pl.ds(b * keys_all, keys_all), :], w_kv[...], NT)


def scatter(all_picks, grad_query, w_query, bias_parts, feat_parts, halo, own, bias_sum):
    slots, chans = halo.shape[1:]
    entries = len(all_picks[0])
    query_part = mm(grad_query, w_query[...], NT)
    for slot in range(halo.shape[0]):
        column = slot // 3
        total, bias_total = None, None
        for b in range(2):
            if column - b not in (0, 1, 2):
                continue
            for e in range(1, entries):
                hit = all_picks[b][e] == slot
                piece = jnp.where(hit, feat_parts[b, e * slots:(e + 1) * slots], 0.0)
                total = piece if total is None else total + piece
                piece = jnp.where(hit, bias_parts[b, e], 0.0)
                bias_total = piece if bias_total is None else bias_total + piece
        if slot in (4, 7):
            b = column - 1
            own[b] = total + (feat_parts[b, 0:slots] + query_part[b * slots:(b + 1) * slots])
            bias_total = bias_total + bias_parts[b, 0]
        else:
            halo[slot] = total.astype(BF)
        bias_sum[slot] = bias_total


MESH = pl.DeviceIdType.MESH
NXY = 16
NZ = 8
NPEER = NXY + NZ
ROWS = 32


def ring(offset, size):
    return min(offset, size - offset)


PLANE = sorted(
    [(dx, dy) for dx in range(4) for dy in range(4) if dx or dy],
    key=lambda o: -(ring(o[0], 4) + ring(o[1], 4)),
)
DEPTH = sorted(range(1, NZ), key=lambda o: -ring(o, NZ))


def remote(src, dst, send_sem, recv_sem, device):
    return pltpu.make_async_remote_copy(
        src_ref=src, dst_ref=dst, send_sem=send_sem, recv_sem=recv_sem,
        device_id=device, device_id_type=MESH,
    )


def layer_kernel(
    neighbours_hbm, counts_hbm, feat, key_bias, grad_out, w_query_hbm, w_key_hbm, w_value_hbm, w_out_hbm,
    out, grad_feat, grad_bias,
    neighbours, counts, ext, near_bias, ext_bias, grad_rows, w_query, w_out, query, grad_att, key_value,
    part, halo, own, bias_sum, feat_parts, bias_parts, w_kv, gathered, scores, grad_probs, probs_low,
    scores_low, grad_kv, attended_t, grad_query_t,
    from_core, half, from_first, mine, from_second, total, summed,
    side, side_bias, rows_out, rows_bias, edge, edge_bias,
    local_sem, out_sem, wide_send, wide_recv, near_send, near_recv,
    core_send, core_recv, first_send, first_recv, second_send, second_recv,
    third_send, third_recv, fourth_send, fourth_recv, side_send, side_recv, edge_send, edge_recv,
):
    lat = lax.axis_index("lat")
    lon = lax.axis_index("lon")
    core = lon % 2
    z = (lon // 2) % NZ
    x_lo = lon // (2 * NZ)
    x_hi = lat // 4
    y = lat % 4
    xy = (x_hi * 2 + x_lo) * 4 + y
    partner = (lat, lon + 1 - 2 * core)
    nlat = lax.axis_size("lat")
    nlon = lax.axis_size("lon")
    east = (lat, (lon + 1) % nlon)
    west = (lat, (lon + nlon - 1) % nlon)
    north = (lat - 1, lon)
    south = (lat + 1, lon)
    base = core * NPEER
    other = (1 - core) * NPEER

    off_lon = (lon + nlon - 1 + 2 * core) % nlon
    off = (lat, off_lon)
    seam = nlat // 2

    x = x_hi * 2 + x_lo

    def plane_peers():
        for dx, dy in PLANE:
            px = (x + dx) % 4
            py = (y + dy) % 4
            yield px * 4 + py, ((px // 2) * 4 + py, (px % 2) * (2 * NZ) + z * 2 + core)

    def depth_peers():
        for dz in DEPTH:
            pz = (z + dz) % NZ
            yield pz, (lat, x_lo * (2 * NZ) + pz * 2 + core)

    barrier = pltpu.get_barrier_semaphore()

    def greet(device):
        pl.semaphore_signal(barrier, inc=1, device_id=device, device_id_type=MESH)

    def settle(like, sem):
        pltpu.make_async_copy(like, like, sem).wait()

    chans = feat.shape[3]
    loads = [
        (feat.at[0, 0], ext.at[4], 0),
        (feat.at[0, 1], ext.at[7], 0),
        (w_query_hbm, w_query, 1),
        (grad_out.at[0], grad_rows, 2),
        (w_out_hbm, w_out, 3),
        (w_key_hbm, w_kv.at[:, pl.ds(0, chans)], 4),
        (w_value_hbm, w_kv.at[:, pl.ds(chans, chans)], 4),
        (neighbours_hbm, neighbours, 5),
        (counts_hbm, counts, 6),
    ]
    greet(partner)
    greet(off)

    @pl.when(lat > 0)
    def _():
        greet((lat - 1, off_lon))
        greet((lat - 1, partner[1]))

    @pl.when(lat < nlat - 1)
    def _():
        greet((lat + 1, off_lon))
        greet((lat + 1, partner[1]))

    for src, dst, index in loads:
        pltpu.make_async_copy(src, dst, local_sem.at[index]).start()
    for _, device in plane_peers():
        greet(device)
    for _, device in depth_peers():
        greet(device)

    near_bias[4] = key_bias[...]
    inner = jnp.minimum(lat, 1) + jnp.minimum(nlat - 1 - lat, 1)
    pl.semaphore_wait(barrier, NPEER + 2 * inner)

    feat_off = feat.at[0, core]
    feat_in = feat.at[0, 1 - core]
    s_off = 4 + 3 * core
    s_in = 7 - 3 * core
    t_off = 9 - 9 * core
    t_in = 9 * core
    b_off = 2 - 2 * core
    b_in = 2 * core

    def wide_copy(source, target, sent, landed, device):
        return remote(source, ext.at[target], wide_send.at[sent], wide_recv.at[landed], device)

    def near_copy(target, sent, landed, device):
        return remote(near_bias.at[4], near_bias.at[target], near_send.at[sent], near_recv.at[landed], device)

    def to_row(up):
        device = north if up else south
        corner = (lat - 1, off_lon) if up else (lat + 1, off_lon)
        inside = (corner[0], partner[1])
        step, row, sent, landed = (1, 2, 1, 2) if up else (-1, 0, 2, 1)
        wide_copy(feat_in, s_in + step, sent, landed, device).start()
        wide_copy(feat_off, t_off + row, sent, landed + 2, corner).start()
        wide_copy(feat_off, s_off + step, sent, landed + 2, device).start()
        near_copy(3 * row + 1, sent, landed, device).start()
        near_copy(3 * row + b_off, sent, landed, corner).start()
        near_copy(3 * row + b_in, sent, landed, inside).start()

    pl.when(lat == seam - 1)(lambda: to_row(False))
    pl.when(lat == seam)(lambda: to_row(True))
    wide_copy(feat_in, t_in + 1, 0, 0, partner).start()
    wide_copy(feat_off, t_off + 1, 0, 0, off).start()
    near_copy(3 + b_in, 0, 0, partner).start()
    near_copy(3 + b_off, 0, 0, off).start()
    pl.when((lat > 0) & (lat != seam))(lambda: to_row(True))
    pl.when((lat < nlat - 1) & (lat != seam - 1))(lambda: to_row(False))

    settle(ext.at[pl.ds(0, 2)], local_sem.at[0])
    settle(w_query, local_sem.at[1])
    settle(grad_rows, local_sem.at[2])
    settle(w_out, local_sem.at[3])
    settle(w_kv, local_sem.at[4])
    settle(neighbours, local_sem.at[5])
    settle(counts, local_sem.at[6])
    project(ext, grad_rows, w_query, w_out, w_kv, query, grad_att, key_value)

    def pass_on(row):
        landed = 1 + row // 2
        slot = s_in - 1 + row
        settle(ext.at[slot], wide_recv.at[landed])
        wide_copy(ext.at[slot], t_in + row, landed + 2, landed + 2, partner).start()

    def arrived(row):
        landed = 1 + row // 2
        settle(ext.at[pl.ds(0, 3)], wide_recv.at[landed + 2])
        settle(near_bias.at[pl.ds(0, 3)], near_recv.at[landed])

    pl.when(lat == seam - 1)(lambda: pass_on(0))
    pl.when(lat < nlat - 1)(lambda: pass_on(2))
    pl.when((lat > 0) & (lat != seam - 1))(lambda: pass_on(0))
    settle(ext.at[pl.ds(0, 2)], wide_recv.at[0])
    settle(near_bias.at[pl.ds(0, 2)], near_recv.at[0])
    pl.when(lat > 0)(lambda: arrived(0))
    pl.when(lat < nlat - 1)(lambda: arrived(2))
    heads = ext_bias.shape[1]
    for row in range(3):
        west_bias = near_bias[3 * row].astype(F32)
        own_bias = near_bias[3 * row + 1].astype(F32)
        east_bias = near_bias[3 * row + 2].astype(F32)
        ext_bias[row] = west_bias[heads:]
        ext_bias[3 + row] = own_bias[:heads]
        ext_bias[6 + row] = own_bias[heads:]
        ext_bias[9 + row] = east_bias[:heads]

    def core_copy(which):
        start, offset = ((2 - core, core), (3 - 3 * core, 1 - core))[which]
        count = NPEER // 2
        return remote(
            part.at[pl.ds(start * count, count)], from_core.at[pl.ds(offset * count, count)],
            core_send.at[which], core_recv.at[which], partner,
        )

    def send_part(which):
        core_copy(which).start()

    all_picks, grad_query = attend(
        neighbours, counts, ext, ext_bias, grad_rows, query, grad_att, key_value, part, send_part,
        w_kv, gathered, scores, grad_probs, probs_low, scores_low, grad_kv,
        attended_t, grad_query_t, bias_parts,
    )

    plane = pl.ds(0, NXY)
    depth = pl.ds(NXY, NZ)

    feature_parts(w_kv, grad_kv, feat_parts)
    core_copy(0).wait_recv()
    core_copy(1).wait_recv()
    half[...] = (part[pl.ds(base, NPEER)].astype(F32) + from_core[...].astype(F32)).astype(BF)

    for peer, device in depth_peers():
        remote(half.at[NXY + peer], from_first.at[NXY + z], first_send.at[1], first_recv.at[1], device).start()

    for peer, device in plane_peers():
        remote(half.at[peer], from_first.at[xy], first_send.at[0], first_recv.at[0], device).start()

    from_first[xy] = half[xy]
    from_first[NXY + z] = half[NXY + z]
    scatter(all_picks, grad_query, w_query, bias_parts, feat_parts, halo, own, bias_sum)
    for index in range(2):
        device = (west, east)[index]
        columns = pl.ds(9 * index, 3)
        remote(halo.at[columns], side.at[1 - index], side_send.at[0], side_recv.at[0], device).start()
        remote(bias_sum.at[columns], side_bias.at[1 - index], side_send.at[1], side_recv.at[1], device).start()

    settle(half.at[pl.ds(0, NZ - 1)], first_recv.at[1])
    mine[1] = jnp.sum(from_first[depth].astype(F32), axis=0).astype(BF)

    for peer, device in plane_peers():
        remote(mine.at[1], from_second.at[xy], second_send.at[1], second_recv.at[1], device).start()

    settle(half.at[pl.ds(0, NXY - 1)], first_recv.at[0])
    mine[0] = jnp.sum(from_first[plane].astype(F32), axis=0).astype(BF)

    for peer, device in depth_peers():
        remote(mine.at[0], from_second.at[NXY + z], second_send.at[0], second_recv.at[0], device).start()

    from_second[xy] = mine[1]
    from_second[NXY + z] = mine[0]

    def to_edge(index):
        device = (north, south)[index]
        landed = 2 - 2 * index
        remote(rows_out.at[index], edge.at[1 - index], edge_send.at[2 * index], edge_recv.at[landed], device).start()
        remote(rows_bias.at[index], edge_bias.at[1 - index], edge_send.at[2 * index + 1], edge_recv.at[landed + 1], device).start()

    def fold_columns():
        settle(side, side_recv.at[0])
        settle(side_bias, side_recv.at[1])
        for index in range(2):
            for j in range(2):
                slot = 3 * j + 3 + 2 * index
                rows_out[index, j] = (halo[slot].astype(F32) + side[j, 2 * index].astype(F32)).astype(BF)
                rows_bias[index, j] = bias_sum[slot] + side_bias[j, 2 * index]
        pl.when(lat == seam - 1)(lambda: to_edge(1))
        pl.when(lat > 0)(lambda: to_edge(0))
        pl.when((lat < nlat - 1) & (lat != seam - 1))(lambda: to_edge(1))

    wraps = (z == (NZ - 1) * core)
    pl.when(jnp.logical_not(wraps))(fold_columns)

    settle(half.at[pl.ds(0, NXY - 1)], second_recv.at[1])
    total[1] = jnp.sum(from_second[plane].astype(F32), axis=0).astype(BF)

    for peer, device in depth_peers():
        remote(total.at[1], summed.at[NXY + z], third_send.at[1], third_recv.at[1], device).start()

    summed[NXY + z] = total[1]
    settle(half.at[pl.ds(0, NZ - 1)], second_recv.at[0])
    total[0] = jnp.sum(from_second[depth].astype(F32), axis=0).astype(BF)

    for peer, device in plane_peers():
        remote(total.at[0], summed.at[xy], third_send.at[0], third_recv.at[0], device).start()

    summed[xy] = total[0]
    pl.when(wraps)(fold_columns)

    def fourth_copy(which):
        start, count = ((0, NXY), (NXY, NZ))[which]
        return remote(
            summed.at[pl.ds(start, count)], out.at[pl.ds(base + start, count)],
            fourth_send.at[0], fourth_recv.at[0], partner,
        )

    settle(half.at[pl.ds(0, NZ - 1)], third_recv.at[1])
    fourth_copy(1).start()
    settle(half.at[pl.ds(0, NXY - 1)], third_recv.at[0])
    fourth_copy(0).start()
    own_out = pltpu.make_async_copy(summed, out.at[pl.ds(base, NPEER)], out_sem.at[0])
    own_out.start()

    @pl.when(lat == 0)
    def _():
        edge[0] = jnp.zeros_like(edge[0])
        edge_bias[0] = jnp.zeros_like(edge_bias[0])

    @pl.when(lat == nlat - 1)
    def _():
        edge[1] = jnp.zeros_like(edge[1])
        edge_bias[1] = jnp.zeros_like(edge_bias[1])

    @pl.when(lat > 0)
    def _():
        settle(rows_out.at[0], edge_send.at[0])
        settle(rows_bias.at[0], edge_send.at[1])
        settle(edge.at[0], edge_recv.at[0])
        settle(edge_bias.at[0], edge_recv.at[1])

    @pl.when(lat < nlat - 1)
    def _():
        settle(rows_out.at[1], edge_send.at[2])
        settle(rows_bias.at[1], edge_send.at[3])
        settle(edge.at[1], edge_recv.at[2])
        settle(edge_bias.at[1], edge_recv.at[3])

    for j in range(2):
        total_grad = own[j] + side[j, 1].astype(F32) + (edge[0, j].astype(F32) + edge[1, j].astype(F32))
        grad_feat[j] = total_grad.astype(BF)
        grad_bias[j] = bias_sum[3 * j + 4] + side_bias[j, 1] + (edge_bias[0, j] + edge_bias[1, j])

    settle(ext.at[pl.ds(0, 2)], wide_send.at[0])
    settle(near_bias.at[pl.ds(0, 2)], near_send.at[0])

    @pl.when(lat > 0)
    def _():
        settle(ext.at[pl.ds(0, 3)], wide_send.at[1])
        settle(ext.at[0], wide_send.at[3])
        settle(near_bias.at[pl.ds(0, 3)], near_send.at[1])

    @pl.when(lat < nlat - 1)
    def _():
        settle(ext.at[pl.ds(0, 3)], wide_send.at[2])
        settle(ext.at[0], wide_send.at[4])
        settle(near_bias.at[pl.ds(0, 3)], near_send.at[2])

    core_copy(0).wait_send()
    core_copy(1).wait_send()
    settle(side, side_send.at[0])
    settle(side_bias, side_send.at[1])
    for sems, wide_index in ((first_send, 0), (second_send, 1), (third_send, 0)):
        settle(half.at[pl.ds(0, NXY - 1)], sems.at[wide_index])
        settle(half.at[pl.ds(0, NZ - 1)], sems.at[1 - wide_index])
    settle(half, fourth_send.at[0])
    settle(half, fourth_recv.at[0])
    own_out.wait()


def layer_call(neighbours, counts, feat, key_bias, grad_out, w_query, w_key, w_value, w_out):
    _, _, slots, chans = feat.shape
    heads = key_bias.shape[0] // 2
    blocks = 12
    entries = counts.shape[2]
    keys_all = entries * slots
    vmem = pl.BlockSpec(memory_space=pltpu.VMEM)
    hbm = pl.BlockSpec(memory_space=pl.ANY)
    low = lambda *shape: pltpu.VMEM(shape, BF)
    wide = lambda *shape: pltpu.VMEM(shape, F32)
    dma = pltpu.SemaphoreType.DMA
    return pl.pallas_call(
        layer_kernel,
        out_shape=[
            jax.ShapeDtypeStruct((2 * NPEER, ROWS, chans), BF),
            jax.ShapeDtypeStruct((2, slots, chans), BF),
            jax.ShapeDtypeStruct((2, heads, slots), F32),
        ],
        in_specs=[hbm] * 3 + [vmem] + [hbm] * 5,
        out_specs=[hbm, vmem, vmem],
        scratch_shapes=[
            pltpu.SMEM(neighbours.shape, jnp.int32),
            pltpu.SMEM(counts.shape, jnp.int32),
            low(blocks, slots, chans),
            low(9, 2 * heads, slots),
            wide(blocks, heads, slots),
            low(2, slots, chans),
            low(chans, chans),
            low(chans, chans),
            low(2, slots, chans),
            low(2, slots, chans),
            low(2 * keys_all, 2 * chans),
            low(2 * NPEER, ROWS, chans),
            low(blocks, slots, chans),
            wide(2, slots, chans),
            wide(blocks, heads, slots),
            wide(2, keys_all, chans),
            wide(2, entries, heads, slots),
            low(chans, 2 * chans),
            low(2, keys_all, chans),
            wide(4, keys_all, PAIR * slots),
            wide(4, keys_all, PAIR * slots),
            low(4, keys_all, PAIR * slots),
            low(4, keys_all, PAIR * slots),
            low(2 * keys_all, 2 * chans),
            low(chans, 2 * slots),
            low(chans, 2 * slots),
            low(NPEER, ROWS, chans),
            low(NPEER, ROWS, chans),
            low(NPEER, ROWS, chans),
            low(2, ROWS, chans),
            low(NPEER, ROWS, chans),
            low(2, ROWS, chans),
            low(NPEER, ROWS, chans),
            low(2, 3, slots, chans),
            wide(2, 3, heads, slots),
            low(2, 2, slots, chans),
            wide(2, 2, heads, slots),
            low(2, 2, slots, chans),
            wide(2, 2, heads, slots),
        ]
        + [dma((count,)) for count in (7, 1, 5, 5, 3, 3)]
        + [dma((count,)) for count in (2, 2, 2, 2, 2, 2, 2, 2, 1, 1, 2, 2, 4, 4)],
        compiler_params=pltpu.CompilerParams(collective_id=0, has_side_effects=True, vmem_limit_bytes=62 << 20),
        name="layer_backward",
    )(neighbours, counts, feat, key_bias, grad_out, w_query, w_key, w_value, w_out)


def finish_kernel(
    scale, low, grad_feat, grad_bias, feat_out, bias_out, w0, w1, w2, w3,
    packed, plain, feat_rows, bias_rows, load_sem, store_sem,
):
    weights = (w0, w1, w2, w3)
    chans = w0.shape[0]
    loads = [(low.at[pl.ds(chans * i, chans)], packed.at[i]) for i in range(4)]
    loads += [(grad_feat, feat_rows), (grad_bias, bias_rows)]
    loads = [pltpu.make_async_copy(src, dst, load_sem.at[i]) for i, (src, dst) in enumerate(loads)]
    for load in loads:
        load.start()
    stores = [(plain.at[i], weights[i]) for i in range(4)]
    stores += [(feat_rows, feat_out.at[0]), (bias_rows, bias_out.at[0])]
    stores = [pltpu.make_async_copy(src, dst, store_sem.at[i]) for i, (src, dst) in enumerate(stores)]
    for i in range(6):
        loads[i].wait()
        if i < 4:
            plain[i] = packed[i].astype(F32) * scale
        stores[i].start()
    for store in stores:
        store.wait()


def finish_call(low, grad_feat, grad_bias, scale):
    chans = low.shape[1]
    hbm = pl.BlockSpec(memory_space=pl.ANY)
    dma = pltpu.SemaphoreType.DMA
    weight = jax.ShapeDtypeStruct((chans, chans), F32)
    return pl.pallas_call(
        functools.partial(finish_kernel, scale),
        out_shape=[
            jax.ShapeDtypeStruct((1,) + grad_feat.shape, BF),
            jax.ShapeDtypeStruct((1,) + grad_bias.shape, F32),
        ]
        + [weight] * 4,
        in_specs=[hbm] * 3,
        out_specs=[hbm] * 6,
        scratch_shapes=[
            pltpu.VMEM((4, chans, chans), BF),
            pltpu.VMEM((4, chans, chans), F32),
            pltpu.VMEM(grad_feat.shape, BF),
            pltpu.VMEM(grad_bias.shape, F32),
            dma((6,)),
            dma((6,)),
        ],
        compiler_params=pltpu.CompilerParams(vmem_limit_bytes=62 << 20),
        name="scale_weights",
    )(low, grad_feat, grad_bias)


def per_device(
    features, w_query, w_key, w_value, w_out, key_bias, neighbours, key_counts, grad_out
):
    brows, bcols, slots, chans = features.shape
    heads = key_bias.shape[2]
    low, grad_features, grad_bias = layer_call(
        neighbours, key_counts, features, key_bias.reshape(bcols * heads, slots), grad_out,
        w_query, w_key, w_value, w_out,
    )
    cells = lax.axis_size("lat") * lax.axis_size("lon") * brows * bcols * slots
    return tuple(
        finish_call(low.reshape(4 * chans, chans), grad_features, grad_bias, float(cells) ** (-0.5))
    )


def solution(mesh):
    placed = (
        P("lat", "lon", None, None),
        P(),
        P(),
        P(),
        P(),
        P("lat", "lon", None, None),
        P("lat", "lon", None),
        P("lat", "lon", None),
        P("lat", "lon", None, None),
    )
    return jax.shard_map(
        per_device,
        mesh=mesh,
        in_specs=placed,
        out_specs=(P("lat", "lon", None, None), P("lat", "lon", None, None), P(), P(), P(), P()),
        check_vma=False,
    )
```

```python
import functools
import math

import jax
import jax.numpy as jnp
import numpy as np
from jax import lax
from jax.experimental import pallas as pl
from jax.experimental.pallas import tpu as pltpu
from jax.sharding import PartitionSpec as P

BF = jnp.bfloat16
F32 = jnp.float32
HEADS = 8
PAIR = 4
WINDOW = 256
NT = (((1,), (1,)), ((), ()))
TN = (((0,), (0,)), ((), ()))
FAR = -1e30


def bf16_parts(value, count):
    parts = []
    for _ in range(count):
        part = float(np.asarray(value, dtype=jnp.bfloat16).astype(np.float64))
        parts.append(part)
        value = value - part
    return parts


def mm(a, b, dims=None):
    if dims is None:
        return jnp.dot(a, b, preferred_element_type=F32)
    return lax.dot_general(a, b, dims, preferred_element_type=F32)


def project(ext, grad_rows, w_query, w_out, w_kv, query, grad_att, key_value):
    slots = ext.shape[1]
    entries = key_value.shape[0] // (2 * slots)
    for b in range(2):
        feat = ext[3 * b + 4]
        query[b] = mm(feat, w_query[...]).astype(BF)
        grad_att[b] = mm(grad_rows[b], w_out[...], NT).astype(BF)
        key_value[b * entries * slots:(b * entries + 1) * slots] = mm(feat, w_kv[...]).astype(BF)


def attend(
    neighbours, counts, ext, ext_bias, grad_out, query_all, grad_att_all, key_value, part, send_part,
    w_kv, gathered, scores, grad_probs, probs_low, scores_low, grad_kv,
    attended_t, grad_query_t, bias_parts,
):
    lat = lax.axis_index("lat")
    lon = lax.axis_index("lon")
    columns = 2 * lax.axis_size("lon")

    def local_slot(block):
        row = lax.div(block, columns) - lat + 1
        column = lax.rem(lax.rem(block, columns) - 2 * lon + 1 + columns, columns)
        return jnp.clip(column, 0, 3) * 3 + jnp.clip(row, 0, 2)

    slots, chans = ext.shape[1:]
    width = chans // HEADS
    entries = counts.shape[2]
    keys_all = entries * slots
    root = math.sqrt(width)
    parts = bf16_parts(root, 3)
    log2e = math.log2(math.e) / root
    lane = lax.broadcasted_iota(jnp.int32, (slots, WINDOW), 1)
    row = lax.broadcasted_iota(jnp.int32, (slots, WINDOW), 0)
    place_row = lax.broadcasted_iota(jnp.int32, (HEADS, WINDOW), 0)
    place_lane = lax.broadcasted_iota(jnp.int32, (HEADS, WINDOW), 1)
    wide_lane = lax.broadcasted_iota(jnp.int32, (keys_all, slots), 1)
    bias_all = [jnp.zeros((keys_all, slots), F32)] * 2
    state = {}

    def gather(b):
        picks = [local_slot(neighbours[0, b, e]) for e in range(entries)]
        gathered[b, 0:slots, :] = ext[3 * b + 4]
        for e in range(1, entries):
            gathered[b, e * slots:(e + 1) * slots, :] = ext[picks[e]]
        rest = pl.ds(b * keys_all + slots, keys_all - slots)
        key_value[rest, :] = mm(gathered[b, slots:], w_kv[...]).astype(BF)
        kv = key_value[pl.ds(b * keys_all, keys_all), :]
        bias_row = jnp.concatenate([ext_bias[picks[e]] for e in range(entries)], axis=1)
        return picks, query_all[b], grad_att_all[b], kv, bias_row

    def prepare(b, w):
        picks, query, grad_att, kv, bias_row = state[b]
        lo = w * (chans - WINDOW)
        first = PAIR * w
        spare = PAIR * width if w == 0 else 0
        region = (lane < PAIR * width) if w == 0 else (lane >= WINDOW - PAIR * width)
        place = jnp.zeros((HEADS, WINDOW), F32)
        for hh in range(PAIR):
            start = spare + 3 * hh
            place = jnp.where(
                (place_row == first + hh) & (place_lane >= start) & (place_lane < start + 3), 1.0, place
            )
        bias_cols = mm(bias_row, place, TN)
        key_aug = []
        for e in range(entries):
            cols = bias_cols[e * slots:(e + 1) * slots]
            cols = jnp.where((lane == spare + 3 * PAIR) & (row >= counts[0, b, e]), FAR, cols)
            piece = kv[e * slots:(e + 1) * slots, lo:lo + WINDOW]
            key_aug.append(jnp.where(region, piece.astype(F32), cols).astype(BF))
        key_aug = jnp.concatenate(key_aug, axis=0)
        value_win = kv[:, chans + lo:chans + lo + WINDOW]
        query_win = query[:, lo:lo + WINDOW].astype(F32)
        grad_win = grad_att[:, lo:lo + WINDOW].astype(F32)
        query_aug, grad_aug = [], []
        for hh in range(PAIR):
            inside = (lane >= (first + hh) * width - lo) & (lane < (first + hh + 1) * width - lo)
            const = jnp.where(lane == spare + 3 * PAIR, 1.0, 0.0)
            for t in range(3):
                const = jnp.where(lane == spare + 3 * hh + t, parts[t], const)
            query_aug.append(jnp.where(inside, query_win, const).astype(BF))
            grad_aug.append(jnp.where(inside, grad_win, 0.0).astype(BF))
        query_aug = jnp.concatenate(query_aug, axis=0)
        grad_aug = jnp.concatenate(grad_aug, axis=0)
        scores[2 * b + w] = mm(key_aug, query_aug, NT)
        grad_probs[2 * b + w] = mm(value_win, grad_aug, NT)
        return query_aug, grad_aug, lo, first, spare, region

    def soften(b, w):
        first = PAIR * w
        bias_sums = bias_all[b]
        for hh in range(PAIR):
            cut = pl.ds(hh * slots, slots)
            logits = scores[2 * b + w, :, cut]
            powers = jnp.exp2((logits - jnp.max(logits, axis=0, keepdims=True)) * log2e)
            probs = powers * (1.0 / jnp.sum(powers, axis=0, keepdims=True))
            probs_low[2 * b + w, :, cut] = probs.astype(BF)
            grads = grad_probs[2 * b + w, :, cut]
            centre = jnp.sum(probs * grads, axis=0, keepdims=True)
            full = probs * (grads - centre)
            high = full.astype(BF)
            scores_low[2 * b + w, :, cut] = high
            bias_sums = jnp.where(wide_lane == first + hh, jnp.sum(full, axis=1, keepdims=True), bias_sums)
        bias_all[b] = bias_sums

    def finish(b, w):
        picks, query, grad_att, kv, bias_row = state[b]
        query_aug, grad_aug, lo, first, spare, region = state[b, w]
        value_grad = mm(probs_low[2 * b + w], grad_aug)
        key_grad = mm(scores_low[2 * b + w], query_aug)
        scale = 1.0 / root
        base = b * keys_all
        rows = pl.ds(base, keys_all)
        half = WINDOW // 2
        edge = PAIR * width - half
        low_lane = lane[0:1, 0:half]
        if w == 0:
            grad_kv[rows, 0:half] = (key_grad[:, 0:half] * scale).astype(BF)
            grad_kv[rows, chans:chans + half] = value_grad[:, 0:half].astype(BF)
            state[b, 'saved'] = key_grad[:, half:], value_grad[:, half:]
        else:
            saved_key, saved_value = state[b, 'saved']
            middle = jnp.where(low_lane < edge, saved_key, key_grad[:, 0:half]) * scale
            grad_kv[rows, half:2 * half] = middle.astype(BF)
            grad_kv[rows, 2 * half:3 * half] = (key_grad[:, half:] * scale).astype(BF)
            middle = saved_value + value_grad[:, 0:half]
            grad_kv[rows, chans + half:chans + 2 * half] = middle.astype(BF)
            grad_kv[rows, chans + 2 * half:chans + 3 * half] = value_grad[:, half:].astype(BF)
        for pair in range(2):
            head = first + 2 * pair
            cut = pl.ds(2 * pair * slots, 2 * slots)
            value_rows = kv[:, chans + head * width:chans + (head + 2) * width]
            key_rows = kv[:, head * width:(head + 2) * width]
            both = mm(value_rows, probs_low[2 * b + w, :, cut], TN)
            attended_t[head * width:(head + 1) * width, b * slots:(b + 1) * slots] = both[:width, :slots].astype(BF)
            attended_t[(head + 1) * width:(head + 2) * width, b * slots:(b + 1) * slots] = both[width:, slots:].astype(BF)
            both = mm(key_rows, scores_low[2 * b + w, :, cut], TN) * scale
            grad_query_t[head * width:(head + 1) * width, b * slots:(b + 1) * slots] = both[:width, :slots].astype(BF)
            grad_query_t[(head + 1) * width:(head + 2) * width, b * slots:(b + 1) * slots] = both[width:, slots:].astype(BF)

    steps = [(0, 0), (0, 1), (1, 0), (1, 1)]
    state[0] = gather(0)
    state[0, 0] = prepare(0, 0)
    state[1] = gather(1)
    for i, step in enumerate(steps):
        if i + 1 < len(steps):
            state[steps[i + 1]] = prepare(*steps[i + 1])
        soften(*step)
        finish(*step)
    all_picks = [state[b][0] for b in range(2)]
    for b in range(2):
        for e in range(entries):
            bias_parts[b, e] = jnp.transpose(bias_all[b][e * slots:(e + 1) * slots])[:HEADS]
    grad_query = jnp.transpose(grad_query_t[...].astype(F32)).astype(BF)
    feat_both = jnp.concatenate([ext[4], ext[7]], axis=0)
    grad_both = grad_out[...].reshape(2 * slots, chans)
    piece = chans // ROWS

    def put(index, value):
        part[index * piece:(index + 1) * piece] = value.astype(BF).reshape(piece, ROWS, chans)

    weight_kv = mm(gathered[...].reshape(2 * keys_all, chans), grad_kv[...], TN)
    put(1, weight_kv[:, :chans])
    put(2, weight_kv[:, chans:])
    send_part(0)
    put(0, mm(feat_both, grad_query, TN))
    put(3, mm(attended_t[...], grad_both))
    send_part(1)
    return all_picks, grad_query


def feature_parts(w_kv, grad_kv, feat_parts):
    keys_all = feat_parts.shape[1]
    for b in range(2):
        feat_parts[b] = mm(grad_kv[pl.ds(b * keys_all, keys_all), :], w_kv[...], NT)


def scatter(all_picks, grad_query, w_query, bias_parts, feat_parts, halo, own, bias_sum):
    slots, chans = halo.shape[1:]
    entries = len(all_picks[0])
    query_part = mm(grad_query, w_query[...], NT)
    for slot in range(halo.shape[0]):
        column = slot // 3
        total, bias_total = None, None
        for b in range(2):
            if column - b not in (0, 1, 2):
                continue
            for e in range(1, entries):
                hit = all_picks[b][e] == slot
                piece = jnp.where(hit, feat_parts[b, e * slots:(e + 1) * slots], 0.0)
                total = piece if total is None else total + piece
                piece = jnp.where(hit, bias_parts[b, e], 0.0)
                bias_total = piece if bias_total is None else bias_total + piece
        if slot in (4, 7):
            b = column - 1
            own[b] = total + (feat_parts[b, 0:slots] + query_part[b * slots:(b + 1) * slots])
            bias_total = bias_total + bias_parts[b, 0]
        else:
            halo[slot] = total.astype(BF)
        bias_sum[slot] = bias_total


MESH = pl.DeviceIdType.MESH
NXY = 16
NZ = 8
NPEER = NXY + NZ
ROWS = 32


def ring(offset, size):
    return min(offset, size - offset)


PLANE = sorted(
    [(dx, dy) for dx in range(4) for dy in range(4) if dx or dy],
    key=lambda o: -(ring(o[0], 4) + ring(o[1], 4)),
)
DEPTH = sorted(range(1, NZ), key=lambda o: -ring(o, NZ))


def remote(src, dst, send_sem, recv_sem, device):
    return pltpu.make_async_remote_copy(
        src_ref=src, dst_ref=dst, send_sem=send_sem, recv_sem=recv_sem,
        device_id=device, device_id_type=MESH,
    )


def layer_kernel(
    neighbours_hbm, counts_hbm, feat, key_bias, grad_out, w_query_hbm, w_key_hbm, w_value_hbm, w_out_hbm,
    out, grad_feat, grad_bias,
    neighbours, counts, ext, near_bias, ext_bias, grad_rows, w_query, w_out, query, grad_att, key_value,
    part, halo, own, bias_sum, feat_parts, bias_parts, w_kv, gathered, scores, grad_probs, probs_low,
    scores_low, grad_kv, attended_t, grad_query_t,
    from_core, half, from_first, mine, from_second, total, summed,
    side, side_bias, rows_out, rows_bias, edge, edge_bias,
    local_sem, out_sem, wide_send, wide_recv, near_send, near_recv,
    core_send, core_recv, first_send, first_recv, second_send, second_recv,
    third_send, third_recv, fourth_send, fourth_recv, side_send, side_recv, edge_send, edge_recv,
):
    lat = lax.axis_index("lat")
    lon = lax.axis_index("lon")
    core = lon % 2
    z = (lon // 2) % NZ
    x_lo = lon // (2 * NZ)
    x_hi = lat // 4
    y = lat % 4
    xy = (x_hi * 2 + x_lo) * 4 + y
    partner = (lat, lon + 1 - 2 * core)
    nlat = lax.axis_size("lat")
    nlon = lax.axis_size("lon")
    east = (lat, (lon + 1) % nlon)
    west = (lat, (lon + nlon - 1) % nlon)
    north = (lat - 1, lon)
    south = (lat + 1, lon)
    base = core * NPEER
    other = (1 - core) * NPEER

    off_lon = (lon + nlon - 1 + 2 * core) % nlon
    off = (lat, off_lon)
    seam = nlat // 2

    x = x_hi * 2 + x_lo

    def plane_peers():
        for dx, dy in PLANE:
            px = (x + dx) % 4
            py = (y + dy) % 4
            yield px * 4 + py, ((px // 2) * 4 + py, (px % 2) * (2 * NZ) + z * 2 + core)

    def depth_peers():
        for dz in DEPTH:
            pz = (z + dz) % NZ
            yield pz, (lat, x_lo * (2 * NZ) + pz * 2 + core)

    barrier = pltpu.get_barrier_semaphore()

    def greet(device):
        pl.semaphore_signal(barrier, inc=1, device_id=device, device_id_type=MESH)

    def settle(like, sem):
        pltpu.make_async_copy(like, like, sem).wait()

    chans = feat.shape[3]
    loads = [
        (feat.at[0, 0], ext.at[4], 0),
        (feat.at[0, 1], ext.at[7], 0),
        (w_query_hbm, w_query, 1),
        (grad_out.at[0], grad_rows, 2),
        (w_out_hbm, w_out, 3),
        (w_key_hbm, w_kv.at[:, pl.ds(0, chans)], 4),
        (w_value_hbm, w_kv.at[:, pl.ds(chans, chans)], 4),
        (neighbours_hbm, neighbours, 5),
        (counts_hbm, counts, 6),
    ]
    for _, device in plane_peers():
        greet(device)
    for _, device in depth_peers():
        greet(device)
    greet(partner)
    greet(off)

    @pl.when(lat > 0)
    def _():
        greet((lat - 1, off_lon))
        greet((lat - 1, partner[1]))

    @pl.when(lat < nlat - 1)
    def _():
        greet((lat + 1, off_lon))
        greet((lat + 1, partner[1]))


    for src, dst, index in loads:
        pltpu.make_async_copy(src, dst, local_sem.at[index]).start()
    near_bias[4] = key_bias[...]
    inner = jnp.minimum(lat, 1) + jnp.minimum(nlat - 1 - lat, 1)
    pl.semaphore_wait(barrier, NPEER + 2 * inner)

    feat_off = feat.at[0, core]
    feat_in = feat.at[0, 1 - core]
    s_off = 4 + 3 * core
    s_in = 7 - 3 * core
    t_off = 9 - 9 * core
    t_in = 9 * core
    b_off = 2 - 2 * core
    b_in = 2 * core

    def wide_copy(source, target, sent, landed, device):
        return remote(source, ext.at[target], wide_send.at[sent], wide_recv.at[landed], device)

    def near_copy(target, sent, landed, device):
        return remote(near_bias.at[4], near_bias.at[target], near_send.at[sent], near_recv.at[landed], device)

    def to_row(up):
        device = north if up else south
        corner = (lat - 1, off_lon) if up else (lat + 1, off_lon)
        inside = (corner[0], partner[1])
        step, row, sent, landed = (1, 2, 1, 2) if up else (-1, 0, 2, 1)
        wide_copy(feat_in, s_in + step, sent, landed, device).start()
        wide_copy(feat_off, t_off + row, sent, landed + 2, corner).start()
        wide_copy(feat_off, s_off + step, sent, landed + 2, device).start()
        near_copy(3 * row + 1, sent, landed, device).start()
        near_copy(3 * row + b_off, sent, landed, corner).start()
        near_copy(3 * row + b_in, sent, landed, inside).start()

    pl.when(lat == seam - 1)(lambda: to_row(False))
    pl.when(lat == seam)(lambda: to_row(True))
    wide_copy(feat_in, t_in + 1, 0, 0, partner).start()
    wide_copy(feat_off, t_off + 1, 0, 0, off).start()
    near_copy(3 + b_in, 0, 0, partner).start()
    near_copy(3 + b_off, 0, 0, off).start()
    pl.when((lat > 0) & (lat != seam))(lambda: to_row(True))
    pl.when((lat < nlat - 1) & (lat != seam - 1))(lambda: to_row(False))

    settle(ext.at[pl.ds(0, 2)], local_sem.at[0])
    settle(w_query, local_sem.at[1])
    settle(grad_rows, local_sem.at[2])
    settle(w_out, local_sem.at[3])
    settle(w_kv, local_sem.at[4])
    settle(neighbours, local_sem.at[5])
    settle(counts, local_sem.at[6])
    project(ext, grad_rows, w_query, w_out, w_kv, query, grad_att, key_value)

    def pass_on(row):
        landed = 1 + row // 2
        slot = s_in - 1 + row
        settle(ext.at[slot], wide_recv.at[landed])
        wide_copy(ext.at[slot], t_in + row, landed + 2, landed + 2, partner).start()

    def arrived(row):
        landed = 1 + row // 2
        settle(ext.at[pl.ds(0, 3)], wide_recv.at[landed + 2])
        settle(near_bias.at[pl.ds(0, 3)], near_recv.at[landed])

    pl.when(lat == seam - 1)(lambda: pass_on(0))
    pl.when(lat < nlat - 1)(lambda: pass_on(2))
    pl.when((lat > 0) & (lat != seam - 1))(lambda: pass_on(0))
    settle(ext.at[pl.ds(0, 2)], wide_recv.at[0])
    settle(near_bias.at[pl.ds(0, 2)], near_recv.at[0])
    pl.when(lat > 0)(lambda: arrived(0))
    pl.when(lat < nlat - 1)(lambda: arrived(2))
    heads = ext_bias.shape[1]
    for row in range(3):
        west_bias = near_bias[3 * row].astype(F32)
        own_bias = near_bias[3 * row + 1].astype(F32)
        east_bias = near_bias[3 * row + 2].astype(F32)
        ext_bias[row] = west_bias[heads:]
        ext_bias[3 + row] = own_bias[:heads]
        ext_bias[6 + row] = own_bias[heads:]
        ext_bias[9 + row] = east_bias[:heads]

    def core_copy(which):
        start, offset = ((2 - core, core), (3 - 3 * core, 1 - core))[which]
        count = NPEER // 2
        return remote(
            part.at[pl.ds(start * count, count)], from_core.at[pl.ds(offset * count, count)],
            core_send.at[which], core_recv.at[which], partner,
        )

    def send_part(which):
        core_copy(which).start()

    all_picks, grad_query = attend(
        neighbours, counts, ext, ext_bias, grad_rows, query, grad_att, key_value, part, send_part,
        w_kv, gathered, scores, grad_probs, probs_low, scores_low, grad_kv,
        attended_t, grad_query_t, bias_parts,
    )

    plane = pl.ds(0, NXY)
    depth = pl.ds(NXY, NZ)

    feature_parts(w_kv, grad_kv, feat_parts)
    core_copy(0).wait_recv()
    core_copy(1).wait_recv()
    half[...] = (part[pl.ds(base, NPEER)].astype(F32) + from_core[...].astype(F32)).astype(BF)

    for peer, device in depth_peers():
        remote(half.at[NXY + peer], from_first.at[NXY + z], first_send.at[1], first_recv.at[1], device).start()

    for peer, device in plane_peers():
        remote(half.at[peer], from_first.at[xy], first_send.at[0], first_recv.at[0], device).start()

    from_first[xy] = half[xy]
    from_first[NXY + z] = half[NXY + z]
    scatter(all_picks, grad_query, w_query, bias_parts, feat_parts, halo, own, bias_sum)
    for index in range(2):
        device = (west, east)[index]
        columns = pl.ds(9 * index, 3)
        remote(halo.at[columns], side.at[1 - index], side_send.at[0], side_recv.at[0], device).start()
        remote(bias_sum.at[columns], side_bias.at[1 - index], side_send.at[1], side_recv.at[1], device).start()

    settle(half.at[pl.ds(0, NZ - 1)], first_recv.at[1])
    mine[1] = jnp.sum(from_first[depth].astype(F32), axis=0).astype(BF)

    for peer, device in plane_peers():
        remote(mine.at[1], from_second.at[xy], second_send.at[1], second_recv.at[1], device).start()

    settle(half.at[pl.ds(0, NXY - 1)], first_recv.at[0])
    mine[0] = jnp.sum(from_first[plane].astype(F32), axis=0).astype(BF)

    for peer, device in depth_peers():
        remote(mine.at[0], from_second.at[NXY + z], second_send.at[0], second_recv.at[0], device).start()

    from_second[xy] = mine[1]
    from_second[NXY + z] = mine[0]

    def to_edge(index):
        device = (north, south)[index]
        landed = 2 - 2 * index
        remote(rows_out.at[index], edge.at[1 - index], edge_send.at[2 * index], edge_recv.at[landed], device).start()
        remote(rows_bias.at[index], edge_bias.at[1 - index], edge_send.at[2 * index + 1], edge_recv.at[landed + 1], device).start()

    def fold_columns():
        settle(side, side_recv.at[0])
        settle(side_bias, side_recv.at[1])
        for index in range(2):
            for j in range(2):
                slot = 3 * j + 3 + 2 * index
                rows_out[index, j] = (halo[slot].astype(F32) + side[j, 2 * index].astype(F32)).astype(BF)
                rows_bias[index, j] = bias_sum[slot] + side_bias[j, 2 * index]
        pl.when(lat == seam - 1)(lambda: to_edge(1))
        pl.when(lat > 0)(lambda: to_edge(0))
        pl.when((lat < nlat - 1) & (lat != seam - 1))(lambda: to_edge(1))

    wraps = (z == (NZ - 1) * core)
    pl.when(jnp.logical_not(wraps))(fold_columns)

    settle(half.at[pl.ds(0, NXY - 1)], second_recv.at[1])
    total[1] = jnp.sum(from_second[plane].astype(F32), axis=0).astype(BF)

    for peer, device in depth_peers():
        remote(total.at[1], summed.at[NXY + z], third_send.at[1], third_recv.at[1], device).start()

    summed[NXY + z] = total[1]
    settle(half.at[pl.ds(0, NZ - 1)], second_recv.at[0])
    total[0] = jnp.sum(from_second[depth].astype(F32), axis=0).astype(BF)

    for peer, device in plane_peers():
        remote(total.at[0], summed.at[xy], third_send.at[0], third_recv.at[0], device).start()

    summed[xy] = total[0]
    pl.when(wraps)(fold_columns)

    def fourth_copy(which):
        start, count = ((0, NXY), (NXY, NZ))[which]
        return remote(
            summed.at[pl.ds(start, count)], out.at[pl.ds(base + start, count)],
            fourth_send.at[0], fourth_recv.at[0], partner,
        )

    settle(half.at[pl.ds(0, NZ - 1)], third_recv.at[1])
    fourth_copy(1).start()
    settle(half.at[pl.ds(0, NXY - 1)], third_recv.at[0])
    fourth_copy(0).start()
    own_out = pltpu.make_async_copy(summed, out.at[pl.ds(base, NPEER)], out_sem.at[0])
    own_out.start()

    @pl.when(lat == 0)
    def _():
        edge[0] = jnp.zeros_like(edge[0])
        edge_bias[0] = jnp.zeros_like(edge_bias[0])

    @pl.when(lat == nlat - 1)
    def _():
        edge[1] = jnp.zeros_like(edge[1])
        edge_bias[1] = jnp.zeros_like(edge_bias[1])

    @pl.when(lat > 0)
    def _():
        settle(rows_out.at[0], edge_send.at[0])
        settle(rows_bias.at[0], edge_send.at[1])
        settle(edge.at[0], edge_recv.at[0])
        settle(edge_bias.at[0], edge_recv.at[1])

    @pl.when(lat < nlat - 1)
    def _():
        settle(rows_out.at[1], edge_send.at[2])
        settle(rows_bias.at[1], edge_send.at[3])
        settle(edge.at[1], edge_recv.at[2])
        settle(edge_bias.at[1], edge_recv.at[3])

    for j in range(2):
        total_grad = own[j] + side[j, 1].astype(F32) + (edge[0, j].astype(F32) + edge[1, j].astype(F32))
        grad_feat[j] = total_grad.astype(BF)
        grad_bias[j] = bias_sum[3 * j + 4] + side_bias[j, 1] + (edge_bias[0, j] + edge_bias[1, j])

    settle(ext.at[pl.ds(0, 2)], wide_send.at[0])
    settle(near_bias.at[pl.ds(0, 2)], near_send.at[0])

    @pl.when(lat > 0)
    def _():
        settle(ext.at[pl.ds(0, 3)], wide_send.at[1])
        settle(ext.at[0], wide_send.at[3])
        settle(near_bias.at[pl.ds(0, 3)], near_send.at[1])

    @pl.when(lat < nlat - 1)
    def _():
        settle(ext.at[pl.ds(0, 3)], wide_send.at[2])
        settle(ext.at[0], wide_send.at[4])
        settle(near_bias.at[pl.ds(0, 3)], near_send.at[2])

    core_copy(0).wait_send()
    core_copy(1).wait_send()
    settle(side, side_send.at[0])
    settle(side_bias, side_send.at[1])
    for sems, wide_index in ((first_send, 0), (second_send, 1), (third_send, 0)):
        settle(half.at[pl.ds(0, NXY - 1)], sems.at[wide_index])
        settle(half.at[pl.ds(0, NZ - 1)], sems.at[1 - wide_index])
    settle(half, fourth_send.at[0])
    settle(half, fourth_recv.at[0])
    own_out.wait()


def layer_call(neighbours, counts, feat, key_bias, grad_out, w_query, w_key, w_value, w_out):
    _, _, slots, chans = feat.shape
    heads = key_bias.shape[0] // 2
    blocks = 12
    entries = counts.shape[2]
    keys_all = entries * slots
    vmem = pl.BlockSpec(memory_space=pltpu.VMEM)
    hbm = pl.BlockSpec(memory_space=pl.ANY)
    low = lambda *shape: pltpu.VMEM(shape, BF)
    wide = lambda *shape: pltpu.VMEM(shape, F32)
    dma = pltpu.SemaphoreType.DMA
    return pl.pallas_call(
        layer_kernel,
        out_shape=[
            jax.ShapeDtypeStruct((2 * NPEER, ROWS, chans), BF),
            jax.ShapeDtypeStruct((2, slots, chans), BF),
            jax.ShapeDtypeStruct((2, heads, slots), F32),
        ],
        in_specs=[hbm] * 3 + [vmem] + [hbm] * 5,
        out_specs=[hbm, vmem, vmem],
        scratch_shapes=[
            pltpu.SMEM(neighbours.shape, jnp.int32),
            pltpu.SMEM(counts.shape, jnp.int32),
            low(blocks, slots, chans),
            low(9, 2 * heads, slots),
            wide(blocks, heads, slots),
            low(2, slots, chans),
            low(chans, chans),
            low(chans, chans),
            low(2, slots, chans),
            low(2, slots, chans),
            low(2 * keys_all, 2 * chans),
            low(2 * NPEER, ROWS, chans),
            low(blocks, slots, chans),
            wide(2, slots, chans),
            wide(blocks, heads, slots),
            wide(2, keys_all, chans),
            wide(2, entries, heads, slots),
            low(chans, 2 * chans),
            low(2, keys_all, chans),
            wide(4, keys_all, PAIR * slots),
            wide(4, keys_all, PAIR * slots),
            low(4, keys_all, PAIR * slots),
            low(4, keys_all, PAIR * slots),
            low(2 * keys_all, 2 * chans),
            low(chans, 2 * slots),
            low(chans, 2 * slots),
            low(NPEER, ROWS, chans),
            low(NPEER, ROWS, chans),
            low(NPEER, ROWS, chans),
            low(2, ROWS, chans),
            low(NPEER, ROWS, chans),
            low(2, ROWS, chans),
            low(NPEER, ROWS, chans),
            low(2, 3, slots, chans),
            wide(2, 3, heads, slots),
            low(2, 2, slots, chans),
            wide(2, 2, heads, slots),
            low(2, 2, slots, chans),
            wide(2, 2, heads, slots),
        ]
        + [dma((count,)) for count in (7, 1, 5, 5, 3, 3)]
        + [dma((count,)) for count in (2, 2, 2, 2, 2, 2, 2, 2, 1, 1, 2, 2, 4, 4)],
        compiler_params=pltpu.CompilerParams(collective_id=0, has_side_effects=True, vmem_limit_bytes=62 << 20),
        name="layer_backward",
    )(neighbours, counts, feat, key_bias, grad_out, w_query, w_key, w_value, w_out)


def finish_kernel(
    scale, low, grad_feat, grad_bias, feat_out, bias_out, w0, w1, w2, w3,
    packed, plain, feat_rows, bias_rows, load_sem, store_sem,
):
    weights = (w0, w1, w2, w3)
    chans = w0.shape[0]
    loads = [(low.at[pl.ds(chans * i, chans)], packed.at[i]) for i in range(4)]
    loads += [(grad_feat, feat_rows), (grad_bias, bias_rows)]
    loads = [pltpu.make_async_copy(src, dst, load_sem.at[i]) for i, (src, dst) in enumerate(loads)]
    for load in loads:
        load.start()
    stores = [(plain.at[i], weights[i]) for i in range(4)]
    stores += [(feat_rows, feat_out.at[0]), (bias_rows, bias_out.at[0])]
    stores = [pltpu.make_async_copy(src, dst, store_sem.at[i]) for i, (src, dst) in enumerate(stores)]
    for i in range(6):
        loads[i].wait()
        if i < 4:
            plain[i] = packed[i].astype(F32) * scale
        stores[i].start()
    for store in stores:
        store.wait()


def finish_call(low, grad_feat, grad_bias, scale):
    chans = low.shape[1]
    hbm = pl.BlockSpec(memory_space=pl.ANY)
    dma = pltpu.SemaphoreType.DMA
    weight = jax.ShapeDtypeStruct((chans, chans), F32)
    return pl.pallas_call(
        functools.partial(finish_kernel, scale),
        out_shape=[
            jax.ShapeDtypeStruct((1,) + grad_feat.shape, BF),
            jax.ShapeDtypeStruct((1,) + grad_bias.shape, F32),
        ]
        + [weight] * 4,
        in_specs=[hbm] * 3,
        out_specs=[hbm] * 6,
        scratch_shapes=[
            pltpu.VMEM((4, chans, chans), BF),
            pltpu.VMEM((4, chans, chans), F32),
            pltpu.VMEM(grad_feat.shape, BF),
            pltpu.VMEM(grad_bias.shape, F32),
            dma((6,)),
            dma((6,)),
        ],
        compiler_params=pltpu.CompilerParams(vmem_limit_bytes=62 << 20),
        name="scale_weights",
    )(low, grad_feat, grad_bias)


def per_device(
    features, w_query, w_key, w_value, w_out, key_bias, neighbours, key_counts, grad_out
):
    brows, bcols, slots, chans = features.shape
    heads = key_bias.shape[2]
    low, grad_features, grad_bias = layer_call(
        neighbours, key_counts, features, key_bias.reshape(bcols * heads, slots), grad_out,
        w_query, w_key, w_value, w_out,
    )
    cells = lax.axis_size("lat") * lax.axis_size("lon") * brows * bcols * slots
    return tuple(
        finish_call(low.reshape(4 * chans, chans), grad_features, grad_bias, float(cells) ** (-0.5))
    )


def solution(mesh):
    placed = (
        P("lat", "lon", None, None),
        P(),
        P(),
        P(),
        P(),
        P("lat", "lon", None, None),
        P("lat", "lon", None),
        P("lat", "lon", None),
        P("lat", "lon", None, None),
    )
    return jax.shard_map(
        per_device,
        mesh=mesh,
        in_specs=placed,
        out_specs=(P("lat", "lon", None, None), P("lat", "lon", None, None), P(), P(), P(), P()),
        check_vma=False,
    )
```
